32 devices in a mesh: section: 4 (over y, x), dp: 8 (over z, core).
Axes of the slice: x: 2, y: 2, z: 4, core: 2. Of those that a mesh axis runs over, the one named last changes fastest.
Arguments:
- inputs: bfloat16 [61440, 512], P('dp'), may hold values from -6 to 6
- cotangent: bfloat16 [61440, 512], P('dp'), may hold values from -6 to 6
- latent_codes: bfloat16 [64, 256], replicated, may hold values from -6 to 6
- positions: bfloat16 [3, 61440], P(None, 'dp'), may hold values from -1 to 1
- shape_ids: int32 [61440], P('dp'), may hold values from 0 to 63
- direction_first: bfloat16 [4, 771, 512], P('section'), may hold values from -0.21875 to 0.21875
- gain_first: bfloat16 [4, 512], P('section'), may hold values from 0.099609375 to 1.8984375
- bias_first: bfloat16 [4, 512], P('section'), may hold values from -3 to 3
- direction_second: bfloat16 [4, 512, 512], P('section'), may hold values from -0.25 to 0.25
- gain_second: bfloat16 [4, 512], P('section'), may hold values from 0.099609375 to 1.8984375
- bias_second: bfloat16 [4, 512], P('section'), may hold values from -3 to 3
Outputs:
- activations: bfloat16 [4, 61440, 512], P('section', 'dp')
- input_grads: bfloat16 [4, 61440, 512], P('section', 'dp')
- code_grad: float32 [64, 256], P(('section', 'dp'))
- direction_first_grad: float32 [4, 771, 512], P('section')
- gain_first_grad: float32 [4, 512], P('section')
- bias_first_grad: float32 [4, 512], P('section')
- direction_second_grad: float32 [4, 512, 512], P('section')
- gain_second_grad: float32 [4, 512], P('section')
- bias_second_grad: float32 [4, 512], P('section')
The draws below stay inside these ranges and needn't reach their ends.
All inputs are finite; a program needn't handle non-finite values.
Results may differ from the reference program's by a relative error of at most 0.0095.
Values may be sent and summed in bfloat16 or wider, within the bound.
No kernel may reach another device: no remote copies, remote signals or barrier semaphores. Data moves between devices by JAX's collectives and lax.ppermute only.
A program may use at most 128 MiB of HBM per device.

```python
import jax
import jax.numpy as jnp
from jax import lax

D = 512
LATENT = 256
COORDS = 3
INWIDTH = 771
POINTS = 61440
SHAPES = 64
N_SECTION = 4


def plant(drawn, key, smallest, top_value):
    longest = drawn.shape.index(max(drawn.shape))
    spots = []
    for shift in (0, 1):
        where = [jax.random.randint(jax.random.fold_in(key, axis), (), 0, length) for axis, length in enumerate(drawn.shape)]
        where[longest] = (where[longest] + shift) % drawn.shape[longest]
        spots.append(tuple(where))
    return drawn.at[spots[0]].set(smallest).at[spots[1]].set(top_value)


def block_scale(rng, extent, cuts, low, largest):
    def one(axis_at, shards_of):
        steps = jax.random.uniform(jax.random.fold_in(jax.random.fold_in(rng, 6), axis_at), (shards_of,), jnp.float32, low / len(cuts), largest / len(cuts))
        return jnp.repeat(jnp.exp(steps), extent[axis_at] // shards_of).reshape((-1,) + (1,) * (len(extent) - axis_at - 1))

    loudness = one(*cuts[0])
    for cut in cuts[1:]:
        loudness = loudness * one(*cut)
    return loudness


def normal_values(rng, extent, scale, limit, pieces=(), kind=jnp.bfloat16):
    values = jax.random.normal(rng, extent, jnp.float32) * scale
    if len(pieces) > 0:
        values = block_scale(rng, extent, pieces, -0.22, 0.18) * values
    return jnp.clip(values, min=-limit, max=limit).astype(kind)


def setup_inputs(seed: int = 0) -> dict:
    splits = jax.random.split(jax.random.key(seed), 12)
    return {
        "inputs": normal_values(splits[0], (POINTS, D), 1.0, 6.0, ((0, 8),)),
        "cotangent": normal_values(splits[1], (POINTS, D), 1.0, 6.0, ((0, 8),)),
        "latent_codes": normal_values(splits[2], (SHAPES, LATENT), 1.0, 6.0),
        "positions": jnp.clip(jax.random.uniform(splits[3], (COORDS, POINTS), jnp.float32, -1.0, 1.0) * block_scale(splits[3], (COORDS, POINTS), ((1, 8),), -0.4, 0.0), -1.0, 1.0).astype(jnp.bfloat16),
        "shape_ids": plant(jax.random.randint(splits[4], (POINTS,), 0, SHAPES), jax.random.fold_in(splits[4], 1), 0, SHAPES - 1).astype(jnp.int32),
        "direction_first": normal_values(splits[5], (N_SECTION, INWIDTH, D), INWIDTH ** -0.5, 0.21875, ((0, 4),)),
        "gain_first": jnp.clip(1.0 + 0.18 * jax.random.normal(splits[6], (N_SECTION, D), jnp.float32), 0.099609375, 1.8984375).astype(jnp.bfloat16),
        "bias_first": normal_values(splits[7], (N_SECTION, D), 0.5, 3.0, ((0, 4),)),
        "direction_second": normal_values(splits[8], (N_SECTION, D, D), D ** -0.5, 0.25, ((0, 4),)),
        "gain_second": jnp.clip(1.0 + 0.18 * jax.random.normal(splits[9], (N_SECTION, D), jnp.float32), 0.099609375, 1.8984375).astype(jnp.bfloat16),
        "bias_second": normal_values(splits[10], (N_SECTION, D), 0.5, 3.0, ((0, 4),)),
    }


@jax.custom_vjp
def low(v):
    return lax.optimization_barrier(v.astype(jnp.bfloat16)).astype(jnp.float32)

@jax.custom_vjp
def low_back(v):
    return v

def low_keep(v):
    return (low(v), None)

def low_pass(kept, grad):
    return (grad,)

def back_keep(v):
    return (v, None)

def back_low(kept, grad):
    return (low(grad),)
low.defvjp(low_keep, low_pass)
low_back.defvjp(back_keep, back_low)

def product(left_side, right_side):
    return jnp.dot(left_side, right_side, precision=lax.Precision.HIGHEST, preferred_element_type=jnp.float32)

def norm_weight(direction, gain_row):
    column_scale = gain_row / jnp.sqrt(lax.optimization_barrier(jnp.sum(direction * direction, axis=0)) + 1e-06)
    return direction * column_scale[None, :]

def forward(inputs, latent_codes, direction_first, gain_first, bias_first, direction_second, gain_second, bias_second, nudges, shape_ids, places):
    hidden = inputs
    outputs = []
    for section_index in range(N_SECTION):
        entering = low_back(hidden + nudges[section_index])
        skip_rows = low_back(latent_codes[shape_ids])
        joined = jnp.concatenate([entering, skip_rows, places], axis=1)
        weight_first = low(norm_weight(direction_first[section_index], gain_first[section_index]))
        weight_second = low(norm_weight(direction_second[section_index], gain_second[section_index]))
        inner_sum = low_back(product(joined, weight_first) + bias_first[section_index][None, :])
        active = low(jax.nn.silu(inner_sum))
        outer_sum = low_back(product(active, weight_second) + bias_second[section_index][None, :])
        hidden = low_back(low(jax.nn.silu(outer_sum)))
        outputs.append(hidden)
    return jnp.stack(outputs)

def reference(inputs, cotangent, latent_codes, positions, shape_ids, direction_first, gain_first, bias_first, direction_second, gain_second, bias_second):
    places = positions.astype(jnp.float32).T
    floats = tuple((array.astype(jnp.float32) for array in (inputs, latent_codes, direction_first, gain_first, bias_first, direction_second, gain_second, bias_second)))
    nudges = jnp.zeros((N_SECTION,) + inputs.shape, jnp.float32)

    def forward_only(*arrays):
        return forward(*arrays, shape_ids, places)
    stacked, pullback = jax.vjp(forward_only, *floats, nudges)
    cotangents = jnp.zeros_like(stacked).at[N_SECTION - 1].set(cotangent.astype(jnp.float32))
    gradients = pullback(cotangents)
    return (stacked.astype(jnp.bfloat16), gradients[8].astype(jnp.bfloat16), gradients[1], gradients[2], gradients[3], gradients[4], gradients[5], gradients[6], gradients[7])
```

```python
import functools

import jax
import jax.numpy as jnp
from jax import lax
from jax.experimental import pallas as pl
from jax.experimental.pallas import tpu as pltpu
from jax.sharding import PartitionSpec as P

BF = jnp.bfloat16
F32 = jnp.float32
NT = (((1,), (1,)), ((), ()))
TN = (((0,), (0,)), ((), ()))
SECTIONS = 4
ROWS = 960
SUB = 480
VMEM = 60 * 2**20


def up(value, step):
    return -(-value // step) * step


def mm(left, right, dims=(((1,), (0,)), ((), ()))):
    return lax.dot_general(left, right, dims, preferred_element_type=F32)


def silu_parts(half):
    half = half.astype(BF)
    lift = BF(1.0) + jnp.tanh(half)
    out = half * lift
    return out, lift + out * (BF(2.0) - lift)


def chain_kernel(
    width, extra, sc, h_in, g_in, ext, w_own, w_mine, w_other, b2,
    act, ig, h_keep, a_keep, og_keep, in_keep,
    hs, gs, mids, slope1, slope2, weights, sems,
):
    section, half = sc[0], sc[1]
    rows = h_in.shape[0]
    packed = weights.shape[1]
    part = packed // 2
    subs = [pl.ds(i, SUB) for i in range(0, rows, SUB)]
    first = pl.program_id(0) == 0

    def copies(k):
        slot = jnp.bitwise_xor(k, section)
        own = pltpu.make_async_copy(w_own, weights.at[k], sems.at[0, k])
        got = jnp.maximum(slot - 1, 0)
        mine = pltpu.make_async_copy(
            w_mine.at[got], weights.at[k, pl.ds(half * part, part)], sems.at[0, k]
        )
        other = pltpu.make_async_copy(
            w_other.at[got], weights.at[k, pl.ds((1 - half) * part, part)], sems.at[1, k]
        )
        return slot, own, mine, other

    def each(k, act_on):
        slot, own, mine, other = copies(k)

        @pl.when(slot == 0)
        def _():
            act_on(own)

        @pl.when(slot != 0)
        def _():
            act_on(mine)
            act_on(other)

    @pl.when(first)
    def _():
        for k in range(SECTIONS):
            each(k, lambda c: c.start())

    hs[0] = h_in[...]
    gs[SECTIONS] = g_in[...] * BF(0.5)

    def forward(k, unused):
        @pl.when(first)
        def _():
            each(k, lambda c: c.wait())

        for r in subs:
            z = mm(hs[k, r, :], weights[k, :width, :]) + mm(ext[r, :], weights[k, 2 * width :, :])
            out, slope = silu_parts(z)
            mids[k, r, :] = out
            slope1[k, r, :] = slope
            z = mm(out, weights[k, width : 2 * width, :]) + b2[k]
            out, slope = silu_parts(z)
            hs[k + 1, r, :] = out
            slope2[k, r, :] = slope
        return 0

    lax.fori_loop(0, SECTIONS, forward, 0)
    act[...] = hs[section + 1]
    h_keep[...] = hs[section]
    a_keep[...] = mids[section]

    def backward(j, unused):
        k = SECTIONS - 1 - j
        for r in subs:
            og = gs[k + 1, r, :] * slope2[k, r, :]
            slope2[k, r, :] = og
            back = mm(og, weights[k, width : 2 * width, :], NT)
            ing = (back * slope1[k, r, :].astype(F32)).astype(BF)
            slope1[k, r, :] = ing
            gs[k, r, :] = mm(ing, weights[k, :width, :], NT).astype(BF)
        return 0

    lax.fori_loop(0, SECTIONS - section, backward, 0)
    ig[...] = gs[section] * BF(2.0)
    og_keep[...] = slope2[section]
    in_keep[...] = slope1[section]


def run_chain(scalars, h, g, ext, w_own, w_mine, w_other, b2):
    total, width = h.shape
    extra = ext.shape[1]
    packed = w_own.shape[0]
    rows = lambda cols: pl.BlockSpec((ROWS, cols), lambda i, sc: (i, 0))
    hbm = pl.BlockSpec(memory_space=pl.ANY)
    out = jax.ShapeDtypeStruct((total, width), BF)
    block = lambda n: pltpu.VMEM((n, ROWS, width), BF)
    return pl.pallas_call(
        functools.partial(chain_kernel, width, extra),
        grid_spec=pltpu.PrefetchScalarGridSpec(
            num_scalar_prefetch=1,
            grid=(total // ROWS,),
            in_specs=[rows(width), rows(width), rows(extra), hbm, hbm, hbm,
                      pl.BlockSpec(b2.shape, lambda i, sc: (0, 0, 0))],
            out_specs=[rows(width)] * 6,
            scratch_shapes=[
                block(SECTIONS + 1), block(SECTIONS + 1), block(SECTIONS), block(SECTIONS), block(SECTIONS),
                pltpu.VMEM((SECTIONS, packed, width), BF),
                pltpu.SemaphoreType.DMA((2, SECTIONS)),
            ],
        ),
        out_shape=[out] * 6,
        compiler_params=pltpu.CompilerParams(vmem_limit_bytes=VMEM),
        cost_estimate=pl.CostEstimate(
            flops=2 * total * width * width * 20, bytes_accessed=total * width * 18,
            transcendentals=total * width * 8,
        ),
    )(scalars, h, g, ext, w_own, w_mine, w_other, b2)


def weight_kernel(width, cells, steps, h, a, og, ing, ext, out, acc1, acc2, acce, accb):
    step = pl.program_id(0)

    @pl.when(step == 0)
    def _():
        for acc in (acc1, acc2, acce, accb):
            acc[...] = jnp.zeros_like(acc)

    acc2[...] += mm(a[...], og[...], TN)
    acc1[...] += mm(h[...], ing[...], TN)
    acce[...] += mm(ext[...], ing[...], TN)
    accb[...] += jnp.sum(og[...].astype(F32).reshape(-1, 8, width), axis=0)

    @pl.when(step == steps - 1)
    def _():
        out[:width, :] = acc2[...].astype(BF)
        out[width : 2 * width, :] = acc1[...].astype(BF)
        last = jnp.sum(accb[...], axis=0, keepdims=True)
        row = lax.broadcasted_iota(jnp.int32, acce.shape, 0)
        out[2 * width :, :] = jnp.where(row == cells - 1, last, acce[...]).astype(BF)


def run_weight(h, a, og, ing, ext, cells):
    total, width = h.shape
    rows = lambda cols: pl.BlockSpec((ROWS, cols), lambda i: (i, 0))
    steps = total // ROWS
    packed = 2 * width + cells
    return pl.pallas_call(
        functools.partial(weight_kernel, width, cells, steps),
        grid=(steps,),
        in_specs=[rows(width)] * 4 + [rows(cells)],
        out_specs=pl.BlockSpec((packed, width), lambda i: (0, 0)),
        scratch_shapes=[pltpu.VMEM((width, width), F32), pltpu.VMEM((width, width), F32),
                        pltpu.VMEM((cells, width), F32), pltpu.VMEM((8, width), F32)],
        out_shape=jax.ShapeDtypeStruct((packed, width), BF),
        compiler_params=pltpu.CompilerParams(vmem_limit_bytes=VMEM),
        cost_estimate=pl.CostEstimate(
            flops=2 * total * packed * width, bytes_accessed=total * width * 9, transcendentals=0,
        ),
    )(h, a, og, ing, ext)


def swap_section(block, distance):
    route = [(i, i ^ distance) for i in range(lax.axis_size("section"))]
    return lax.ppermute(block, "section", route)


def swap_dp(block, distance):
    route = [(i, i ^ distance) for i in range(lax.axis_size("dp"))]
    return lax.ppermute(block, "dp", route)


def cut(array, first, count):
    return lax.dynamic_slice_in_dim(array, first, count, 0)


def sum_over_dp(packed):
    devices = lax.axis_size("dp")
    me = lax.axis_index("dp")
    core, place = me % 2, me // 2
    spots = devices // 2
    half = packed.shape[0] // 2
    piece = half // spots
    mine = cut(packed, core * half, half).astype(F32)
    theirs = swap_dp(cut(packed, (1 - core) * half, half), 1).astype(F32)
    chip = (mine + theirs).astype(BF)
    total = cut(chip, place * piece, piece).astype(F32)
    for distance in range(1, spots):
        away = jnp.bitwise_xor(place, distance)
        total = total + swap_dp(cut(chip, away * piece, piece), 2 * distance).astype(F32)
    total = total.astype(BF)
    slots = [total] + [swap_dp(total, 2 * distance) for distance in range(1, spots)]
    stack = jnp.stack(slots)
    other = swap_dp(stack, 1)
    order = jnp.bitwise_xor(jnp.arange(spots), place)
    both = jnp.stack([stack[order], other[order]]).reshape(2, half, -1)
    return jnp.where(core == 0, both, both[::-1]).reshape(packed.shape)


def norm_scale(direction, gain_row):
    norm = jnp.sqrt(jnp.sum(direction * direction, axis=0) + 1e-06)
    return norm


def weight_pullback(direction, gain_row, summed):
    norm = jnp.sqrt(jnp.sum(direction * direction, axis=0) + 1e-06)
    along = jnp.sum(direction * summed, axis=0)
    gain_grad = along / norm
    scale = gain_row / norm
    return scale[None, :] * summed - (scale * along / (norm * norm))[None, :] * direction, gain_grad


def shards(
    inputs, cotangent, latent_codes, positions, shape_ids,
    direction_first, gain_first, bias_first, direction_second, gain_second, bias_second,
):
    section = lax.axis_index("section")
    dp_rank = lax.axis_index("dp")
    dp_count = lax.axis_size("dp")
    core = dp_rank % 2
    total, width = inputs.shape
    shapes, latent = latent_codes.shape
    coords = positions.shape[0]
    cells = up(shapes + coords + 1, 128)
    dir_first = direction_first[0].astype(F32)
    dir_second = direction_second[0].astype(F32)
    gains_first = gain_first[0].astype(F32)
    gains_second = gain_second[0].astype(F32)

    def weight(direction, gain_row):
        scale = gain_row / jnp.sqrt(jnp.sum(direction * direction, axis=0) + 1e-06)
        return (direction * scale[None, :]).astype(BF)

    w1 = weight(dir_first, gains_first)
    w2 = weight(dir_second, gains_second)
    w_skip = w1[width : width + latent]
    by_shape = 0.5 * (mm(latent_codes, w_skip) + bias_first[0].astype(F32)[None, :])
    by_shape_high = by_shape.astype(BF)
    by_shape_low = (by_shape - by_shape_high.astype(F32)).astype(BF)
    half = BF(0.5)
    pad = lambda count: jnp.zeros((count, width), BF)
    packed = jnp.concatenate([
        w1[:width] * half, w2 * half,
        by_shape_high, w1[width + latent :] * half, pad(cells - shapes - coords - 1), bias_second * half,
        by_shape_low, pad(cells - shapes),
    ])
    part = packed.shape[0] // 2
    sending = cut(packed, core * part, part)
    mine = jnp.stack([swap_section(sending, d) for d in range(1, SECTIONS)])
    other = swap_dp(mine, 1)
    spot = 2 * width + cells - 1
    in_part = spot - part
    others_b2 = jnp.where(core == 1, mine[:, in_part], other[:, in_part])
    b2_slots = jnp.concatenate([bias_second * half, others_b2]).astype(F32)
    b2 = b2_slots[jnp.bitwise_xor(jnp.arange(SECTIONS), section)][:, None, :]

    onehot = (shape_ids[:, None] == jnp.arange(shapes, dtype=jnp.int32)[None, :]).astype(BF)
    blank = lambda count: jnp.zeros((total, count), BF)
    ext = jnp.concatenate(
        [onehot, positions.T, blank(cells - shapes - coords), onehot, blank(cells - shapes)], axis=1
    )

    scalars = jnp.stack([section, core]).astype(jnp.int32)
    act, ig, h_keep, a_keep, og_keep, in_keep = run_chain(
        scalars, inputs, cotangent, ext, packed, mine, other, b2
    )
    partial = run_weight(h_keep, a_keep, og_keep, in_keep, ext, cells)
    summed = sum_over_dp(partial).astype(F32)
    sum_second = summed[:width]
    grid = summed[2 * width : 2 * width + shapes]
    places = summed[2 * width + shapes : 2 * width + shapes + coords]
    bias_sum_second = summed[2 * width + cells - 1]
    bias_sum_first = jnp.sum(grid, axis=0)
    grid_low = grid.astype(BF)
    skip_sum = mm(latent_codes, grid_low, TN)
    sum_first = jnp.concatenate([summed[width : 2 * width], skip_sum, places])
    dir_grad_first, gain_grad_first = weight_pullback(dir_first, gains_first, sum_first)
    dir_grad_second, gain_grad_second = weight_pullback(dir_second, gains_second, sum_second)
    code_part = mm(grid_low, w_skip, NT)
    owned = shapes // (SECTIONS * dp_count)
    code = cut(code_part, (section * dp_count + dp_rank) * owned, owned)
    for distance in range(1, SECTIONS):
        away = jnp.bitwise_xor(section, distance)
        code = code + swap_section(cut(code_part, (away * dp_count + dp_rank) * owned, owned), distance)
    return (
        act[None], ig[None], code,
        dir_grad_first[None], gain_grad_first[None], bias_sum_first[None],
        dir_grad_second[None], gain_grad_second[None], bias_sum_second[None],
    )


def solution(mesh):
    in_specs = (
        P("dp", None), P("dp", None), P(), P(None, "dp"), P("dp"),
        P("section", None, None), P("section", None), P("section", None),
        P("section", None, None), P("section", None), P("section", None),
    )
    out_specs = (
        P("section", "dp", None), P("section", "dp", None), P(("section", "dp"), None),
        P("section", None, None), P("section", None), P("section", None),
        P("section", None, None), P("section", None), P("section", None),
    )
    return jax.shard_map(shards, mesh=mesh, in_specs=in_specs, out_specs=out_specs, check_vma=False)
```

```python
import functools

import jax
import jax.numpy as jnp
import numpy as np
from jax import lax
from jax.experimental import pallas as pl
from jax.experimental.pallas import tpu as pltpu
from jax.sharding import PartitionSpec as P

BF = jnp.bfloat16
F32 = jnp.float32
NT = (((1,), (1,)), ((), ()))
TN = (((0,), (0,)), ((), ()))
SECTIONS = 4
ROWS = 768
CALLS = (2, 2, 1)
VMEM = 44 * 2**20
GIVE_X = (7, 6, 3, 8)
GIVE_Y = (8, 3, 6, 7)
FURTHER = (0, 1, 1, 2)


def up(value, step):
    return -(-value // step) * step


def mm(left, right, dims=(((1,), (0,)), ((), ()))):
    return lax.dot_general(left, right, dims, preferred_element_type=F32)


def silu_parts(half):
    lift = 1.0 + jnp.tanh(half)
    out = (half * lift).astype(BF)
    lift = lift.astype(BF)
    return out, lift + out * (BF(2.0) - lift)


def stream(count, *stages):
    values = [None] * count
    for tick in range(count + len(stages) - 1):
        for j, stage in enumerate(stages):
            i = tick - j
            if 0 <= i < count:
                values[i] = stage(i, values[i])


class Plan:
    def __init__(self, width, coords, shapes, devices):
        self.width, self.coords, self.shapes, self.devices = width, coords, shapes, devices
        self.spots = devices // 2
        self.share = width // devices
        self.owned = shapes // devices
        self.per = self.owned // SECTIONS
        self.room = up(self.owned + 1, 16)
        self.cells = self.room * devices
        self.piece = 2 * self.share + self.room
        self.half = self.piece * self.spots
        self.packed = 2 * self.half
        table = np.full((self.cells, 1), -1, np.int32)
        for p in range(devices):
            place = 2 * (p % self.spots) + p // self.spots
            for j in range(self.owned):
                table[p * self.room + j, 0] = ((j // self.per) * devices + place) * self.per + j % self.per
        self.cell_shape = table

    def special(self, j):
        return j * self.room + self.owned


class Block:
    def __init__(self, plan, weights, ext, subs):
        self.width, self.plan, self.weights, self.ext, self.subs = plan.width, plan, weights, ext, subs

    def first(self, k):
        return self.weights[k, : self.width, :]

    def second(self, k):
        return self.weights[k, self.width : 2 * self.width, :]

    def inner(self, k, source):
        beside = self.weights[k, 2 * self.width :, :]
        return lambda i, unused: mm(source(i), self.first(k)) + mm(self.ext[self.subs[i], :], beside)

    def outer(self, k):
        begin = 2 * self.width + self.plan.coords * self.plan.room
        spot = self.plan.owned
        offset = self.weights[k, begin : begin + self.plan.room, :].astype(F32)[spot : spot + 1]
        return lambda i, active: mm(active, self.second(k)) + offset

    def back_second(self, k, grads):
        return lambda i, unused: mm(grads(i), self.second(k), NT)

    def back_first(self, k):
        return lambda i, grads: mm(grads, self.first(k), NT)


def place_cells(point, places, cell_shape, plan, ext, ext_turned):
    rows = ext.shape[0]
    hit = jnp.where(cell_shape[...] == jnp.broadcast_to(point[...], (plan.cells, rows)), 1.0, 0.0)
    cell = lax.broadcasted_iota(jnp.int32, (plan.cells, rows), 0)
    for j in range(plan.coords):
        hit = jnp.where(cell == plan.special(j), places[j : j + 1, :].astype(F32), hit)
    ext_turned[...] = hit.astype(BF)
    ext[...] = hit.T.astype(BF)


def clear(step, accs):
    @pl.when(step == 0)
    def _():
        for acc in accs:
            acc[...] = jnp.zeros_like(acc)


def add_weight_grads(accs, active, outer_grad, entering, inner_grad, ext_turned):
    first, second, cell, bias = accs
    second[...] += mm(active, outer_grad, TN)
    first[...] += mm(entering, inner_grad, TN)
    cell[...] += mm(ext_turned[...], inner_grad)
    bias[...] += jnp.sum(outer_grad.astype(F32).reshape(-1, 8, outer_grad.shape[1]), axis=0)


def store_weight_grads(step, steps, accs, out, plan):
    first, second, cell, bias = accs

    @pl.when(step == steps - 1)
    def _():
        last = jnp.sum(bias[...], axis=0, keepdims=True)
        row = lax.broadcasted_iota(jnp.int32, cell.shape, 0)
        cell[...] = jnp.where(row == plan.special(plan.coords), last, cell[...])
        for p in range(plan.devices):
            base, rows, room = p * plan.piece, plan.share, plan.room
            out[base : base + rows, :] = second[p * rows : (p + 1) * rows, :].astype(BF)
            out[base + rows : base + 2 * rows, :] = first[p * rows : (p + 1) * rows, :].astype(BF)
            out[base + 2 * rows : base + plan.piece, :] = cell[p * room : (p + 1) * room, :].astype(BF)


def self_kernel(
    plan, steps, aliased, sc, h_in, g_in, ids, places, cell_shape, weights, *refs
):
    act, ig, give_x, give_y, out, ext, ext_turned, states, mids, slope1, slope2, *accs = refs[aliased:]
    section = sc[1]
    step = pl.program_id(0)
    rows = h_in.shape[0]
    half = rows // 2
    subs = [pl.ds(0, half), pl.ds(half, half)]
    do = Block(plan, weights, ext, subs)
    clear(step, accs)
    place_cells(ids, places, cell_shape, plan, ext, ext_turned)
    states[0] = h_in[...]

    def keep_active(k):
        def stage(i, z):
            active, slope = silu_parts(z)
            mids[k, subs[i], :] = active
            slope1[k, subs[i], :] = slope
            return active
        return stage

    def keep_state(k):
        def stage(i, z):
            after, slope = silu_parts(z)
            states[k + 1, subs[i], :] = after
            if k == SECTIONS - 1:
                slope = slope * (g_in[subs[i], :] * BF(0.5))
            slope2[k, subs[i], :] = slope
        return stage

    def inner_grad(k):
        def stage(i, grads):
            grads = (grads * slope1[k, subs[i], :].astype(F32)).astype(BF)
            slope1[k, subs[i], :] = grads
            return grads
        return stage

    def enter_grad(k, own, end):
        def stage(i, grads):
            grads = grads.astype(BF)
            states[5 + k, subs[i], :] = grads
            if own:
                ig[subs[i], :] = grads * BF(2.0)
            if not end:
                slope2[k - 1, subs[i], :] = grads * slope2[k - 1, subs[i], :]
        return stage

    def back(k, own, end):
        return [do.back_second(k, lambda i: slope2[k, subs[i], :]), inner_grad(k), do.back_first(k),
                enter_grad(k, own, end)]

    top = SECTIONS - 1
    stages = []
    for k in range(SECTIONS):
        source = (lambda i: h_in[subs[i], :]) if k == 0 else (lambda i, k=k: states[k, subs[i], :])
        stages += [do.inner(k, source), keep_active(k), do.outer(k), keep_state(k)]
    stream(2, *stages, *back(top, False, False))

    for own in range(SECTIONS):
        @pl.when(section == own)
        def _(own=own):
            further = FURTHER[own]
            stages = []
            for k in range(top - 1, own - 1, -1):
                stages += back(k, k == own, k == further)
            if stages:
                stream(2, *stages)
            else:
                ig[...] = states[5 + own] * BF(2.0)
            if further < own:
                value = None
                for stage in back(further, False, True):
                    value = stage(1, value)
            act[...] = states[own + 1]
            give_x[...] = states[GIVE_X[own], subs[0], :]
            give_y[...] = states[GIVE_Y[own], subs[1], :]
            add_weight_grads(accs, mids[own], slope2[own], states[own], slope1[own], ext_turned)

    store_weight_grads(step, steps, accs, out, plan)


def helped_kernel(
    plan, steps, sc, h_in, g_in, ids, places, cell_shape, weights, got_x, got_y, *refs
):
    act, ig, out, ext, ext_turned, states, mid, slope1, slope2, *accs = refs[2:]
    section = sc[1]
    step = pl.program_id(0)
    rows = h_in.shape[0]
    half = rows // 2
    subs = [pl.ds(0, half), pl.ds(half, half)]
    got = [got_x, got_y]
    do = Block(plan, weights, ext, subs)
    clear(step, accs)
    place_cells(ids, places, cell_shape, plan, ext, ext_turned)

    def active_only(i, z):
        return silu_parts(z)[0]

    def keep_active(i, z):
        active, slope = silu_parts(z)
        mid[subs[i], :] = active
        slope1[subs[i], :] = slope
        return active

    def keep_state(k):
        def stage(i, z):
            states[k + 1, subs[i], :] = silu_parts(z)[0]
        return stage

    def keep_own(top):
        def stage(i, z):
            after, slope = silu_parts(z)
            act[subs[i], :] = after
            grads = g_in[subs[i], :] * BF(0.5) if top else got[i][...]
            grads = slope * grads
            slope2[subs[i], :] = grads
            return grads
        return stage

    def inner_grad(i, grads):
        grads = (grads * slope1[subs[i], :].astype(F32)).astype(BF)
        slope1[subs[i], :] = grads
        return grads

    def enter_grad(i, grads):
        ig[subs[i], :] = (2.0 * grads).astype(BF)

    for own in range(SECTIONS):
        @pl.when(section == own)
        def _(own=own):
            top = own == SECTIONS - 1
            stages = []
            for k in range(own if top else 0, own + 1):
                if top:
                    source = lambda i: got[i][...]
                elif k == 0:
                    source = lambda i: h_in[subs[i], :]
                else:
                    source = lambda i, k=k: states[k, subs[i], :]
                stages.append(do.inner(k, source))
                if k < own:
                    stages += [active_only, do.outer(k), keep_state(k)]
                else:
                    stages += [keep_active, do.outer(k), keep_own(top)]
            stages += [do.back_second(own, lambda i: slope2[subs[i], :]), inner_grad, do.back_first(own), enter_grad]
            stream(2, *stages)
            if top:
                states[0, subs[0], :] = got_x[...]
                states[0, subs[1], :] = got_y[...]
                entering = states[0]
            else:
                entering = h_in[...] if own == 0 else states[own]
            add_weight_grads(accs, mid[...], slope2[...], entering, slope1[...], ext_turned)

    store_weight_grads(step, steps, accs, out, plan)


def run_blocks(plan, helped, steps, scalars, h, g, ids, places, cell_shape, weights, into, got):
    total, width = h.shape
    ahead = lambda i, sc: (sc[0] + i, 0)
    rows = pl.BlockSpec((ROWS, width), ahead)
    halves = pl.BlockSpec((ROWS // 2, width), lambda i, sc: (i, 0))
    hbm = pl.BlockSpec(memory_space=pl.ANY)
    vmem = pl.BlockSpec(memory_space=pltpu.VMEM)
    whole = jax.ShapeDtypeStruct((total, width), BF)
    give = jax.ShapeDtypeStruct((steps * ROWS // 2, width), BF)
    grads = jax.ShapeDtypeStruct((plan.packed, width), BF)
    grads_spec = pl.BlockSpec((plan.packed, width), lambda i, sc: (0, 0))
    block = lambda *lead: pltpu.VMEM((*lead, ROWS, width), BF)
    scratch = [pltpu.VMEM((ROWS, plan.cells), BF), pltpu.VMEM((plan.cells, ROWS), BF)]
    operands = [h, g, ids, places, cell_shape, weights, *got, *into]
    first_into = 1 + 6 + len(got)
    if helped:
        kernel = functools.partial(helped_kernel, plan, steps)
        out_shape, out_specs = [whole, whole, grads], [rows, rows, grads_spec]
        scratch += [block(SECTIONS), block(), block(), block()]
        units = 9
    else:
        kernel = functools.partial(self_kernel, plan, steps, len(into))
        out_shape = [whole, whole, give, give, grads]
        out_specs = [rows, rows, halves, halves, grads_spec]
        scratch += [block(10), block(SECTIONS), block(SECTIONS), block(SECTIONS)]
        units = 20
    scratch += [pltpu.VMEM((width, width), F32), pltpu.VMEM((width, width), F32),
                pltpu.VMEM((plan.cells, width), F32), pltpu.VMEM((8, width), F32)]
    return pl.pallas_call(
        kernel,
        grid_spec=pltpu.PrefetchScalarGridSpec(
            num_scalar_prefetch=1,
            grid=(steps,),
            in_specs=[
                rows, rows,
                pl.BlockSpec((None, 1, ROWS), lambda i, sc: (sc[0] + i, 0, 0)),
                pl.BlockSpec((None, plan.coords, ROWS), lambda i, sc: (sc[0] + i, 0, 0)),
                vmem, vmem, *[halves] * len(got), *[hbm] * len(into),
            ],
            out_specs=out_specs,
            scratch_shapes=scratch,
        ),
        out_shape=out_shape,
        input_output_aliases={first_into + j: j for j in range(len(into))},
        compiler_params=pltpu.CompilerParams(vmem_limit_bytes=VMEM),
        cost_estimate=pl.CostEstimate(
            flops=2 * steps * ROWS * width * width * units, bytes_accessed=steps * ROWS * width * 12,
            transcendentals=steps * ROWS * width * 8,
        ),
    )(scalars, *operands)


def normed(direction, gain_row):
    scale = gain_row / jnp.sqrt(jnp.sum(direction * direction, axis=0, keepdims=True) + 1e-06)
    return (direction * scale).astype(BF)


def pack_kernel(plan, latent, dir_first, gain_first, bias_first, dir_second, gain_second, bias_second, latents,
                cell_shape, packed, skip):
    width = plan.width
    half = BF(0.5)
    first = normed(dir_first[...].astype(F32), gain_first[...].astype(F32))
    second = normed(dir_second[...].astype(F32), gain_second[...].astype(F32))
    packed[:width, :] = first[:width] * half
    packed[width : 2 * width, :] = second * half
    skip[...] = first[width : width + latent]
    shape = lax.broadcasted_iota(jnp.int32, (plan.cells, plan.shapes), 1)
    onehot = jnp.where(cell_shape[...] == shape, 1.0, 0.0).astype(BF)
    by_cell = mm(onehot, latents[...]).astype(BF)
    by_cell = mm(by_cell, skip[...])
    by_cell = 0.5 * jnp.where(cell_shape[...] >= 0, by_cell + bias_first[...].astype(F32), 0.0)
    cell = lax.broadcasted_iota(jnp.int32, by_cell.shape, 0)
    tail = 0.5 * first[width + latent :].astype(F32)
    for j in range(plan.coords):
        by_cell = jnp.where(cell == plan.special(j), tail[j : j + 1], by_cell)
    by_cell = jnp.where(cell == plan.special(plan.coords), 0.5 * bias_second[...].astype(F32), by_cell)
    packed[2 * width :, :] = by_cell.astype(BF)


def pack_weights(plan, latents, cell_shape, *own):
    width = plan.width
    latent = latents.shape[1]
    vmem = pl.BlockSpec(memory_space=pltpu.VMEM)
    return pl.pallas_call(
        functools.partial(pack_kernel, plan, latent),
        in_specs=[vmem] * 8,
        out_specs=[vmem] * 2,
        out_shape=[jax.ShapeDtypeStruct((plan.packed, width), BF), jax.ShapeDtypeStruct((latent, width), BF)],
        compiler_params=pltpu.CompilerParams(vmem_limit_bytes=VMEM),
        cost_estimate=pl.CostEstimate(flops=2 * plan.cells * width * latent, bytes_accessed=4 * plan.packed * width,
                                      transcendentals=0),
    )(*own, latents, cell_shape)


def spread_kernel(plan, sc, own, x_mine, y_mine, far_mine, other, weights, sems):
    section, core, spot = sc[0], sc[1], sc[2]
    half, piece = plan.half, plan.piece
    away = 1 - core
    copies = [(own, weights.at[section])]
    for j, block in enumerate((x_mine, y_mine)):
        there = weights.at[jnp.bitwise_xor(section, j + 1)]
        copies.append((block, there.at[pl.ds(core * half, half)]))
        copies.append((other.at[pl.ds(j * half, half)], there.at[pl.ds(away * half, half)]))
    there = weights.at[jnp.bitwise_xor(section, 3)]
    for j in range(plan.spots):
        z = jnp.bitwise_xor(spot, j)
        copies.append((far_mine.at[pl.ds(j * piece, piece)], there.at[pl.ds(core * half + z * piece, piece)]))
        copies.append((other.at[pl.ds(2 * half + j * piece, piece)], there.at[pl.ds(away * half + z * piece, piece)]))
    copies = [pltpu.make_async_copy(source, target, sems.at[j]) for j, (source, target) in enumerate(copies)]
    for copy in copies:
        copy.start()
    for copy in copies:
        copy.wait()


def spread_weights(plan, scalars, own, x_mine, y_mine, far_mine, other):
    hbm = pl.BlockSpec(memory_space=pl.ANY)
    return pl.pallas_call(
        functools.partial(spread_kernel, plan),
        grid_spec=pltpu.PrefetchScalarGridSpec(
            num_scalar_prefetch=1, grid=(1,), in_specs=[hbm] * 5, out_specs=hbm,
            scratch_shapes=[pltpu.SemaphoreType.DMA((5 + 2 * plan.spots,))],
        ),
        out_shape=jax.ShapeDtypeStruct((SECTIONS, plan.packed, plan.width), BF),
        cost_estimate=pl.CostEstimate(flops=0, bytes_accessed=16 * plan.packed * plan.width, transcendentals=0),
    )(scalars, own, x_mine, y_mine, far_mine, other)


def grads_kernel(plan, latent, sc, mine, other, dir_first, gain_first, dir_second, gain_second, latents, cell_shape,
                 first_out, first_gain, first_bias, second_out, second_gain, second_bias, cells):
    core, spot = sc[1], sc[2]
    width, share, room, piece = plan.width, plan.share, plan.room, plan.piece
    for source, side in ((mine, core), (other, 1 - core)):
        for j in range(plan.spots):
            p = side * plan.spots + jnp.bitwise_xor(spot, j)
            base = j * piece
            rows = pl.ds(pl.multiple_of(p * share, share), share)
            second_out[rows, :] = source[base : base + share, :].astype(F32)
            first_out[rows, :] = source[base + share : base + 2 * share, :].astype(F32)
            rows = pl.ds(pl.multiple_of(p * room, room), room)
            cells[rows, :] = source[base + 2 * share : base + piece, :].astype(F32)
    by_cell = cells[...]
    shaped = jnp.where(cell_shape[...] >= 0, by_cell, 0.0)
    first_bias[...] = jnp.sum(shaped, axis=0, keepdims=True)
    shape = lax.broadcasted_iota(jnp.int32, (plan.cells, plan.shapes), 1)
    onehot = jnp.where(cell_shape[...] == shape, 1.0, 0.0).astype(BF)
    by_shape = mm(onehot, latents[...]).astype(BF)
    first_out[width : width + latent, :] = mm(by_shape, shaped.astype(BF), TN)
    for j in range(plan.coords):
        spot_row = plan.special(j)
        first_out[width + latent + j : width + latent + j + 1, :] = cells[spot_row : spot_row + 1, :]
    spot_row = plan.special(plan.coords)
    second_bias[...] = cells[spot_row : spot_row + 1, :]
    for direction, gain, out, gain_out in ((dir_first, gain_first, first_out, first_gain),
                                           (dir_second, gain_second, second_out, second_gain)):
        values = direction[...].astype(F32)
        summed = out[...]
        norm = jnp.sqrt(jnp.sum(values * values, axis=0, keepdims=True) + 1e-06)
        along = jnp.sum(values * summed, axis=0, keepdims=True)
        gain_out[...] = along / norm
        scale = gain[...].astype(F32) / norm
        out[...] = scale * summed - (scale * along / (norm * norm)) * values


def finish_grads(plan, scalars, mine, other, dir_first, gain_first, dir_second, gain_second, latents, cell_shape):
    width = plan.width
    vmem = pl.BlockSpec(memory_space=pltpu.VMEM)
    row = jax.ShapeDtypeStruct((1, width), F32)
    whole = lambda like: jax.ShapeDtypeStruct(like.shape, F32)
    return pl.pallas_call(
        functools.partial(grads_kernel, plan, latents.shape[1]),
        grid_spec=pltpu.PrefetchScalarGridSpec(
            num_scalar_prefetch=1, grid=(1,), in_specs=[vmem] * 8, out_specs=[vmem] * 6,
            scratch_shapes=[pltpu.VMEM((plan.cells, width), F32)],
        ),
        out_shape=[whole(dir_first), row, row, whole(dir_second), row, row],
        compiler_params=pltpu.CompilerParams(vmem_limit_bytes=VMEM),
        cost_estimate=pl.CostEstimate(flops=2 * plan.cells * width * latents.shape[1],
                                      bytes_accessed=8 * plan.packed * width, transcendentals=0),
    )(scalars, mine, other, dir_first, gain_first, dir_second, gain_second, latents, cell_shape)


def swap_section(block, distance):
    route = [(i, i ^ distance) for i in range(lax.axis_size("section"))]
    return lax.ppermute(block, "section", route)


def swap_dp(block, distance):
    route = [(i, i ^ distance) for i in range(lax.axis_size("dp"))]
    return lax.ppermute(block, "dp", route)


def cut(array, first, count):
    return lax.dynamic_slice_in_dim(array, first, count, 0)


def reduce_pieces(plan, packed, core, spot):
    half, piece = plan.half, plan.piece
    mine = cut(packed, core * half, half)
    theirs = swap_dp(cut(packed, (1 - core) * half, half).astype(BF), 1)
    chip = (mine + theirs.astype(F32)).astype(BF)
    total = cut(chip, spot * piece, piece).astype(F32)
    for distance in range(1, plan.spots):
        away = jnp.bitwise_xor(spot, distance)
        total = total + swap_dp(cut(chip, away * piece, piece), 2 * distance).astype(F32)
    return total.astype(BF)


def gather_chips(plan, piece):
    return jnp.concatenate([piece] + [swap_dp(piece, 2 * distance) for distance in range(1, plan.spots)])


def shards(
    inputs, cotangent, latent_codes, positions, shape_ids,
    direction_first, gain_first, bias_first, direction_second, gain_second, bias_second,
):
    section = lax.axis_index("section")
    dp_rank = lax.axis_index("dp")
    core, spot = dp_rank % 2, dp_rank // 2
    total, width = inputs.shape
    shapes, latent = latent_codes.shape
    coords = positions.shape[0]
    plan = Plan(width, coords, shapes, lax.axis_size("dp"))
    cell_shape = jnp.asarray(plan.cell_shape)
    place = jnp.stack([section, core, spot]).astype(jnp.int32)

    packed, skip = pack_weights(
        plan, latent_codes, cell_shape,
        direction_first[0], gain_first, bias_first, direction_second[0], gain_second, bias_second,
    )
    sending = cut(packed, core * plan.half, plan.half)
    far = swap_section(cut(sending, spot * plan.piece, plan.piece), 3)
    x_mine = swap_section(sending, 1)
    y_mine = swap_section(sending, 2)
    far_mine = gather_chips(plan, far)
    other = swap_dp(jnp.concatenate([x_mine, y_mine, far_mine]), 1)
    weights = spread_weights(plan, place, packed, x_mine, y_mine, far_mine, other)

    blocks = total // ROWS
    ids = shape_ids.reshape(blocks, 1, ROWS)
    places = positions.reshape(coords, blocks, ROWS).transpose(1, 0, 2)
    here = jnp.where((section == 0) | (section == SECTIONS - 1), 0, blocks // 2)
    there = blocks // 2 - here

    given, partials, into = [], [], []
    done = 0
    for steps in CALLS:
        scalars = jnp.stack([here + done, section]).astype(jnp.int32)
        *into, give_x, give_y, grads = run_blocks(
            plan, False, steps, scalars, inputs, cotangent, ids, places, cell_shape, weights, into, []
        )
        given.append((swap_section(give_x, 1), swap_section(give_y, 2)))
        partials.append(grads)
        done += steps
    done = 0
    for steps, got in zip(CALLS, given):
        scalars = jnp.stack([there + done, section]).astype(jnp.int32)
        *into, grads = run_blocks(
            plan, True, steps, scalars, inputs, cotangent, ids, places, cell_shape, weights, into, got
        )
        partials.append(grads)
        done += steps
    act, ig = into

    partial = sum(grads.astype(F32) for grads in partials)
    piece = reduce_pieces(plan, partial, core, spot)
    mine = gather_chips(plan, piece)
    other = swap_dp(mine, 1)
    owned = mm(piece[2 * plan.share : 2 * plan.share + plan.owned], skip, NT)
    code = cut(owned, section * plan.per, plan.per)
    for distance in range(1, SECTIONS):
        away = jnp.bitwise_xor(section, distance)
        code = code + swap_section(cut(owned, away * plan.per, plan.per), distance)
    first, first_gain, first_bias, second, second_gain, second_bias = finish_grads(
        plan, place, mine, other, direction_first[0], gain_first, direction_second[0], gain_second,
        latent_codes, cell_shape,
    )
    return (
        act[None], ig[None], code, first[None], first_gain, first_bias, second[None], second_gain, second_bias,
    )


def solution(mesh):
    in_specs = (
        P("dp", None), P("dp", None), P(), P(None, "dp"), P("dp"),
        P("section", None, None), P("section", None), P("section", None),
        P("section", None, None), P("section", None), P("section", None),
    )
    out_specs = (
        P("section", "dp", None), P("section", "dp", None), P(("section", "dp"), None),
        P("section", None, None), P("section", None), P("section", None),
        P("section", None, None), P("section", None), P("section", None),
    )
    return jax.shard_map(shards, mesh=mesh, in_specs=in_specs, out_specs=out_specs, check_vma=False)
```

```python
import functools

import jax
import jax.numpy as jnp
import numpy as np
from jax import lax
from jax.experimental import pallas as pl
from jax.experimental.pallas import tpu as pltpu
from jax.sharding import PartitionSpec as P

BF = jnp.bfloat16
F32 = jnp.float32
NT = (((1,), (1,)), ((), ()))
TN = (((0,), (0,)), ((), ()))
SECTIONS = 4
ROWS = 768
CALLS = (2, 2, 1)
VMEM = 44 * 2**20
GIVE_X = (7, 6, 3, 8)
GIVE_Y = (8, 3, 6, 7)
FURTHER = (0, 1, 1, 2)


def up(value, step):
    return -(-value // step) * step


def mm(left, right, dims=(((1,), (0,)), ((), ()))):
    return lax.dot_general(left, right, dims, preferred_element_type=F32)


def silu_parts(half):
    lift = 1.0 + jnp.tanh(half)
    out = (half * lift).astype(BF)
    lift = lift.astype(BF)
    return out, lift + out * (BF(2.0) - lift)


def stream(count, *stages):
    values = [None] * count
    for tick in range(count + len(stages) - 1):
        for j, stage in enumerate(stages):
            i = tick - j
            if 0 <= i < count:
                values[i] = stage(i, values[i])


class Plan:
    def __init__(self, width, coords, shapes, devices):
        self.width, self.coords, self.shapes, self.devices = width, coords, shapes, devices
        self.spots = devices // 2
        self.share = width // devices
        self.owned = shapes // devices
        self.per = self.owned // SECTIONS
        self.room = up(self.owned + 1, 16)
        self.cells = self.room * devices
        self.piece = 2 * self.share + self.room
        self.half = self.piece * self.spots
        self.packed = 2 * self.half
        table = np.full((self.cells, 1), -1, np.int32)
        for p in range(devices):
            place = 2 * (p % self.spots) + p // self.spots
            for j in range(self.owned):
                table[p * self.room + j, 0] = ((j // self.per) * devices + place) * self.per + j % self.per
        self.cell_shape = table

    def special(self, j):
        return j * self.room + self.owned


class Block:
    def __init__(self, plan, weights, ext, subs):
        self.width, self.plan, self.weights, self.ext, self.subs = plan.width, plan, weights, ext, subs

    def first(self, k):
        return self.weights[k, : self.width, :]

    def second(self, k):
        return self.weights[k, self.width : 2 * self.width, :]

    def inner(self, k, source):
        beside = self.weights[k, 2 * self.width :, :]
        return lambda i, unused: mm(source(i), self.first(k)) + mm(self.ext[self.subs[i], :], beside)

    def outer(self, k):
        begin = 2 * self.width + self.plan.coords * self.plan.room
        spot = self.plan.owned
        offset = self.weights[k, begin : begin + self.plan.room, :].astype(F32)[spot : spot + 1]
        return lambda i, active: mm(active, self.second(k)) + offset

    def back_second(self, k, grads):
        return lambda i, unused: mm(grads(i), self.second(k), NT)

    def back_first(self, k):
        return lambda i, grads: mm(grads, self.first(k), NT)


def place_cells(point, places, cell_shape, plan, ext, ext_turned):
    rows = ext.shape[0]
    hit = jnp.where(cell_shape[...] == jnp.broadcast_to(point[...], (plan.cells, rows)), 1.0, 0.0)
    cell = lax.broadcasted_iota(jnp.int32, (plan.cells, rows), 0)
    for j in range(plan.coords):
        hit = jnp.where(cell == plan.special(j), places[j : j + 1, :].astype(F32), hit)
    ext_turned[...] = hit.astype(BF)
    ext[...] = hit.T.astype(BF)


def clear(step, accs):
    @pl.when(step == 0)
    def _():
        for acc in accs:
            acc[...] = jnp.zeros_like(acc)


def add_weight_grads(accs, active, outer_grad, entering, inner_grad, ext_turned):
    first, second, cell, bias = accs
    second[...] += mm(active, outer_grad, TN)
    first[...] += mm(entering, inner_grad, TN)
    cell[...] += mm(ext_turned[...], inner_grad)
    bias[...] += jnp.sum(outer_grad.astype(F32).reshape(-1, 8, outer_grad.shape[1]), axis=0)


def store_weight_grads(step, steps, accs, out, plan):
    first, second, cell, bias = accs

    @pl.when(step == steps - 1)
    def _():
        last = jnp.sum(bias[...], axis=0, keepdims=True)
        row = lax.broadcasted_iota(jnp.int32, cell.shape, 0)
        cell[...] = jnp.where(row == plan.special(plan.coords), last, cell[...])
        for p in range(plan.devices):
            base, rows, room = p * plan.piece, plan.share, plan.room
            out[base : base + rows, :] = second[p * rows : (p + 1) * rows, :].astype(BF)
            out[base + rows : base + 2 * rows, :] = first[p * rows : (p + 1) * rows, :].astype(BF)
            out[base + 2 * rows : base + plan.piece, :] = cell[p * room : (p + 1) * room, :].astype(BF)


def self_kernel(
    plan, steps, aliased, sc, h_in, g_in, ids, places, cell_shape, weights, *refs
):
    act, ig, give_x, give_y, out, ext, ext_turned, states, mids, slope1, slope2, *accs = refs[aliased:]
    section = sc[1]
    step = pl.program_id(0)
    rows = h_in.shape[0]
    half = rows // 2
    subs = [pl.ds(0, half), pl.ds(half, half)]
    do = Block(plan, weights, ext, subs)
    clear(step, accs)
    place_cells(ids, places, cell_shape, plan, ext, ext_turned)
    states[0] = h_in[...]

    def keep_active(k):
        def stage(i, z):
            active, slope = silu_parts(z)
            mids[k, subs[i], :] = active
            slope1[k, subs[i], :] = slope
            return active
        return stage

    def keep_state(k):
        def stage(i, z):
            after, slope = silu_parts(z)
            states[k + 1, subs[i], :] = after
            if k == SECTIONS - 1:
                slope = slope * (g_in[subs[i], :] * BF(0.5))
            slope2[k, subs[i], :] = slope
        return stage

    def inner_grad(k):
        def stage(i, grads):
            grads = (grads * slope1[k, subs[i], :].astype(F32)).astype(BF)
            slope1[k, subs[i], :] = grads
            return grads
        return stage

    def enter_grad(k, own, end):
        def stage(i, grads):
            grads = grads.astype(BF)
            states[5 + k, subs[i], :] = grads
            if own:
                ig[subs[i], :] = grads * BF(2.0)
            if not end:
                slope2[k - 1, subs[i], :] = grads * slope2[k - 1, subs[i], :]
        return stage

    def back(k, own, end):
        return [do.back_second(k, lambda i: slope2[k, subs[i], :]), inner_grad(k), do.back_first(k),
                enter_grad(k, own, end)]

    top = SECTIONS - 1
    stages = []
    for k in range(SECTIONS):
        source = (lambda i: h_in[subs[i], :]) if k == 0 else (lambda i, k=k: states[k, subs[i], :])
        stages += [do.inner(k, source), keep_active(k), do.outer(k), keep_state(k)]
    stream(2, *stages, *back(top, False, False))

    for own in range(SECTIONS):
        @pl.when(section == own)
        def _(own=own):
            further = FURTHER[own]
            stages = []
            for k in range(top - 1, own - 1, -1):
                stages += back(k, k == own, k == further)
            if stages:
                stream(2, *stages)
            else:
                ig[...] = states[5 + own] * BF(2.0)
            if further < own:
                value = None
                for stage in back(further, False, True):
                    value = stage(1, value)
            act[...] = states[own + 1]
            give_x[...] = states[GIVE_X[own], subs[0], :]
            give_y[...] = states[GIVE_Y[own], subs[1], :]
            add_weight_grads(accs, mids[own], slope2[own], states[own], slope1[own], ext_turned)

    store_weight_grads(step, steps, accs, out, plan)


def helped_kernel(
    plan, steps, sc, h_in, g_in, ids, places, cell_shape, weights, got_x, got_y, *refs
):
    act, ig, out, ext, ext_turned, states, mid, slope1, slope2, *accs = refs[2:]
    section = sc[1]
    step = pl.program_id(0)
    rows = h_in.shape[0]
    half = rows // 2
    subs = [pl.ds(0, half), pl.ds(half, half)]
    got = [got_x, got_y]
    do = Block(plan, weights, ext, subs)
    clear(step, accs)
    place_cells(ids, places, cell_shape, plan, ext, ext_turned)

    def active_only(i, z):
        return silu_parts(z)[0]

    def keep_active(i, z):
        active, slope = silu_parts(z)
        mid[subs[i], :] = active
        slope1[subs[i], :] = slope
        return active

    def keep_state(k):
        def stage(i, z):
            states[k + 1, subs[i], :] = silu_parts(z)[0]
        return stage

    def keep_own(top):
        def stage(i, z):
            after, slope = silu_parts(z)
            act[subs[i], :] = after
            grads = g_in[subs[i], :] * BF(0.5) if top else got[i][...]
            grads = slope * grads
            slope2[subs[i], :] = grads
            return grads
        return stage

    def inner_grad(i, grads):
        grads = (grads * slope1[subs[i], :].astype(F32)).astype(BF)
        slope1[subs[i], :] = grads
        return grads

    def enter_grad(i, grads):
        ig[subs[i], :] = (2.0 * grads).astype(BF)

    for own in range(SECTIONS):
        @pl.when(section == own)
        def _(own=own):
            top = own == SECTIONS - 1
            stages = []
            for k in range(own if top else 0, own + 1):
                if top:
                    source = lambda i: got[i][...]
                elif k == 0:
                    source = lambda i: h_in[subs[i], :]
                else:
                    source = lambda i, k=k: states[k, subs[i], :]
                stages.append(do.inner(k, source))
                if k < own:
                    stages += [active_only, do.outer(k), keep_state(k)]
                else:
                    stages += [keep_active, do.outer(k), keep_own(top)]
            stages += [do.back_second(own, lambda i: slope2[subs[i], :]), inner_grad, do.back_first(own), enter_grad]
            stream(2, *stages)
            if top:
                states[0, subs[0], :] = got_x[...]
                states[0, subs[1], :] = got_y[...]
                entering = states[0]
            else:
                entering = h_in[...] if own == 0 else states[own]
            add_weight_grads(accs, mid[...], slope2[...], entering, slope1[...], ext_turned)

    store_weight_grads(step, steps, accs, out, plan)


def run_blocks(plan, helped, steps, scalars, h, g, ids, places, cell_shape, weights, into, got):
    total, width = h.shape
    ahead = lambda i, sc: (sc[0] + i, 0)
    rows = pl.BlockSpec((ROWS, width), ahead)
    halves = pl.BlockSpec((ROWS // 2, width), lambda i, sc: (i, 0))
    hbm = pl.BlockSpec(memory_space=pl.ANY)
    vmem = pl.BlockSpec(memory_space=pltpu.VMEM)
    whole = jax.ShapeDtypeStruct((total, width), BF)
    give = jax.ShapeDtypeStruct((steps * ROWS // 2, width), BF)
    grads = jax.ShapeDtypeStruct((plan.packed, width), BF)
    grads_spec = pl.BlockSpec((plan.packed, width), lambda i, sc: (0, 0))
    block = lambda *lead: pltpu.VMEM((*lead, ROWS, width), BF)
    scratch = [pltpu.VMEM((ROWS, plan.cells), BF), pltpu.VMEM((plan.cells, ROWS), BF)]
    operands = [h, g, ids, places, cell_shape, weights, *got, *into]
    first_into = 1 + 6 + len(got)
    if helped:
        kernel = functools.partial(helped_kernel, plan, steps)
        out_shape, out_specs = [whole, whole, grads], [rows, rows, grads_spec]
        scratch += [block(SECTIONS), block(), block(), block()]
        units = 9
    else:
        kernel = functools.partial(self_kernel, plan, steps, len(into))
        out_shape = [whole, whole, give, give, grads]
        out_specs = [rows, rows, halves, halves, grads_spec]
        scratch += [block(10), block(SECTIONS), block(SECTIONS), block(SECTIONS)]
        units = 20
    scratch += [pltpu.VMEM((width, width), F32), pltpu.VMEM((width, width), F32),
                pltpu.VMEM((plan.cells, width), F32), pltpu.VMEM((8, width), F32)]
    return pl.pallas_call(
        kernel,
        grid_spec=pltpu.PrefetchScalarGridSpec(
            num_scalar_prefetch=1,
            grid=(steps,),
            in_specs=[
                rows, rows,
                pl.BlockSpec((None, 1, ROWS), lambda i, sc: (sc[0] + i, 0, 0)),
                pl.BlockSpec((None, plan.coords, ROWS), lambda i, sc: (sc[0] + i, 0, 0)),
                vmem, vmem, *[halves] * len(got), *[hbm] * len(into),
            ],
            out_specs=out_specs,
            scratch_shapes=scratch,
        ),
        out_shape=out_shape,
        input_output_aliases={first_into + j: j for j in range(len(into))},
        compiler_params=pltpu.CompilerParams(vmem_limit_bytes=VMEM),
        cost_estimate=pl.CostEstimate(
            flops=2 * steps * ROWS * width * width * units, bytes_accessed=steps * ROWS * width * 12,
            transcendentals=steps * ROWS * width * 8,
        ),
    )(scalars, *operands)


def normed(direction, gain_row):
    scale = gain_row / jnp.sqrt(jnp.sum(direction * direction, axis=0, keepdims=True) + 1e-06)
    return (direction * scale).astype(BF)


def pack_kernel(plan, latent, *refs):
    sources, (packed, skip), held, sems = refs[:8], refs[8:10], refs[10:18], refs[18]
    copies = [pltpu.make_async_copy(s, h, sems.at[j]) for j, (s, h) in enumerate(zip(sources, held))]
    for copy in copies:
        copy.start()
    for copy in copies:
        copy.wait()
    dir_first, gain_first, bias_first, dir_second, gain_second, bias_second, latents, cell_shape = held
    width = plan.width
    half = BF(0.5)
    first = normed(dir_first[...].astype(F32), gain_first[...].astype(F32))
    second = normed(dir_second[...].astype(F32), gain_second[...].astype(F32))
    packed[:width, :] = first[:width] * half
    packed[width : 2 * width, :] = second * half
    skip[...] = first[width : width + latent]
    shape = lax.broadcasted_iota(jnp.int32, (plan.cells, plan.shapes), 1)
    onehot = jnp.where(cell_shape[...] == shape, 1.0, 0.0).astype(BF)
    by_cell = mm(onehot, latents[...]).astype(BF)
    by_cell = mm(by_cell, skip[...])
    by_cell = 0.5 * jnp.where(cell_shape[...] >= 0, by_cell + bias_first[...].astype(F32), 0.0)
    cell = lax.broadcasted_iota(jnp.int32, by_cell.shape, 0)
    tail = 0.5 * first[width + latent :].astype(F32)
    for j in range(plan.coords):
        by_cell = jnp.where(cell == plan.special(j), tail[j : j + 1], by_cell)
    by_cell = jnp.where(cell == plan.special(plan.coords), 0.5 * bias_second[...].astype(F32), by_cell)
    packed[2 * width :, :] = by_cell.astype(BF)


def pack_weights(plan, latents, cell_shape, *own):
    width = plan.width
    latent = latents.shape[1]
    vmem = pl.BlockSpec(memory_space=pltpu.VMEM)
    return pl.pallas_call(
        functools.partial(pack_kernel, plan, latent),
        in_specs=[pl.BlockSpec(memory_space=pl.ANY)] * 8,
        out_specs=[vmem] * 2,
        scratch_shapes=[pltpu.VMEM(array.shape, array.dtype) for array in (*own, latents, cell_shape)]
        + [pltpu.SemaphoreType.DMA((8,))],
        out_shape=[jax.ShapeDtypeStruct((plan.packed, width), BF), jax.ShapeDtypeStruct((latent, width), BF)],
        compiler_params=pltpu.CompilerParams(vmem_limit_bytes=VMEM),
        cost_estimate=pl.CostEstimate(flops=2 * plan.cells * width * latent, bytes_accessed=4 * plan.packed * width,
                                      transcendentals=0),
    )(*own, latents, cell_shape)


def spread_kernel(plan, sc, own, x_mine, y_mine, far_mine, other, weights, sems):
    section, core, spot = sc[0], sc[1], sc[2]
    half, piece = plan.half, plan.piece
    away = 1 - core
    copies = [(own, weights.at[section])]
    for j, block in enumerate((x_mine, y_mine)):
        there = weights.at[jnp.bitwise_xor(section, j + 1)]
        copies.append((block, there.at[pl.ds(core * half, half)]))
        copies.append((other.at[pl.ds(j * half, half)], there.at[pl.ds(away * half, half)]))
    there = weights.at[jnp.bitwise_xor(section, 3)]
    for j in range(plan.spots):
        z = jnp.bitwise_xor(spot, j)
        copies.append((far_mine.at[pl.ds(j * piece, piece)], there.at[pl.ds(core * half + z * piece, piece)]))
        copies.append((other.at[pl.ds(2 * half + j * piece, piece)], there.at[pl.ds(away * half + z * piece, piece)]))
    copies = [pltpu.make_async_copy(source, target, sems.at[j]) for j, (source, target) in enumerate(copies)]
    for copy in copies:
        copy.start()
    for copy in copies:
        copy.wait()


def spread_weights(plan, scalars, own, x_mine, y_mine, far_mine, other):
    hbm = pl.BlockSpec(memory_space=pl.ANY)
    return pl.pallas_call(
        functools.partial(spread_kernel, plan),
        grid_spec=pltpu.PrefetchScalarGridSpec(
            num_scalar_prefetch=1, grid=(1,), in_specs=[hbm] * 5,
            out_specs=pl.BlockSpec(memory_space=pltpu.VMEM),
            scratch_shapes=[pltpu.SemaphoreType.DMA((5 + 2 * plan.spots,))],
        ),
        out_shape=jax.ShapeDtypeStruct((SECTIONS, plan.packed, plan.width), BF),
        compiler_params=pltpu.CompilerParams(vmem_limit_bytes=VMEM),
        cost_estimate=pl.CostEstimate(flops=0, bytes_accessed=16 * plan.packed * plan.width, transcendentals=0),
    )(scalars, own, x_mine, y_mine, far_mine, other)


def grads_kernel(plan, latent, sc, mine, other, dir_first, gain_first, dir_second, gain_second, latents, cell_shape,
                 first_out, first_gain, first_bias, second_out, second_gain, second_bias, cells):
    core, spot = sc[1], sc[2]
    width, share, room, piece = plan.width, plan.share, plan.room, plan.piece
    for source, side in ((mine, core), (other, 1 - core)):
        for j in range(plan.spots):
            p = side * plan.spots + jnp.bitwise_xor(spot, j)
            base = j * piece
            rows = pl.ds(pl.multiple_of(p * share, share), share)
            second_out[rows, :] = source[base : base + share, :].astype(F32)
            first_out[rows, :] = source[base + share : base + 2 * share, :].astype(F32)
            rows = pl.ds(pl.multiple_of(p * room, room), room)
            cells[rows, :] = source[base + 2 * share : base + piece, :].astype(F32)
    by_cell = cells[...]
    shaped = jnp.where(cell_shape[...] >= 0, by_cell, 0.0)
    first_bias[...] = jnp.sum(shaped, axis=0, keepdims=True)
    shape = lax.broadcasted_iota(jnp.int32, (plan.cells, plan.shapes), 1)
    onehot = jnp.where(cell_shape[...] == shape, 1.0, 0.0).astype(BF)
    by_shape = mm(onehot, latents[...]).astype(BF)
    first_out[width : width + latent, :] = mm(by_shape, shaped.astype(BF), TN)
    for j in range(plan.coords):
        spot_row = plan.special(j)
        first_out[width + latent + j : width + latent + j + 1, :] = cells[spot_row : spot_row + 1, :]
    spot_row = plan.special(plan.coords)
    second_bias[...] = cells[spot_row : spot_row + 1, :]
    for direction, gain, out, gain_out in ((dir_first, gain_first, first_out, first_gain),
                                           (dir_second, gain_second, second_out, second_gain)):
        values = direction[...].astype(F32)
        summed = out[...]
        norm = jnp.sqrt(jnp.sum(values * values, axis=0, keepdims=True) + 1e-06)
        along = jnp.sum(values * summed, axis=0, keepdims=True)
        gain_out[...] = along / norm
        scale = gain[...].astype(F32) / norm
        out[...] = scale * summed - (scale * along / (norm * norm)) * values


def finish_grads(plan, scalars, mine, other, dir_first, gain_first, dir_second, gain_second, latents, cell_shape):
    width = plan.width
    vmem = pl.BlockSpec(memory_space=pltpu.VMEM)
    row = jax.ShapeDtypeStruct((1, width), F32)
    whole = lambda like: jax.ShapeDtypeStruct(like.shape, F32)
    return pl.pallas_call(
        functools.partial(grads_kernel, plan, latents.shape[1]),
        grid_spec=pltpu.PrefetchScalarGridSpec(
            num_scalar_prefetch=1, grid=(1,), in_specs=[vmem] * 8, out_specs=[vmem] * 6,
            scratch_shapes=[pltpu.VMEM((plan.cells, width), F32)],
        ),
        out_shape=[whole(dir_first), row, row, whole(dir_second), row, row],
        compiler_params=pltpu.CompilerParams(vmem_limit_bytes=VMEM),
        cost_estimate=pl.CostEstimate(flops=2 * plan.cells * width * latents.shape[1],
                                      bytes_accessed=8 * plan.packed * width, transcendentals=0),
    )(scalars, mine, other, dir_first, gain_first, dir_second, gain_second, latents, cell_shape)


def swap_section(block, distance):
    route = [(i, i ^ distance) for i in range(lax.axis_size("section"))]
    return lax.ppermute(block, "section", route)


def swap_dp(block, distance):
    route = [(i, i ^ distance) for i in range(lax.axis_size("dp"))]
    return lax.ppermute(block, "dp", route)


def cut(array, first, count):
    return lax.dynamic_slice_in_dim(array, first, count, 0)


def reduce_pieces(plan, packed, core, spot):
    half, piece = plan.half, plan.piece
    mine = cut(packed, core * half, half)
    theirs = swap_dp(cut(packed, (1 - core) * half, half).astype(BF), 1)
    chip = (mine + theirs.astype(F32)).astype(BF)
    total = cut(chip, spot * piece, piece).astype(F32)
    for distance in range(1, plan.spots):
        away = jnp.bitwise_xor(spot, distance)
        total = total + swap_dp(cut(chip, away * piece, piece), 2 * distance).astype(F32)
    return total.astype(BF)


def gather_chips(plan, piece):
    return jnp.concatenate([piece] + [swap_dp(piece, 2 * distance) for distance in range(1, plan.spots)])


def shards(
    inputs, cotangent, latent_codes, positions, shape_ids,
    direction_first, gain_first, bias_first, direction_second, gain_second, bias_second,
):
    section = lax.axis_index("section")
    dp_rank = lax.axis_index("dp")
    core, spot = dp_rank % 2, dp_rank // 2
    total, width = inputs.shape
    shapes, latent = latent_codes.shape
    coords = positions.shape[0]
    plan = Plan(width, coords, shapes, lax.axis_size("dp"))
    cell_shape = jnp.asarray(plan.cell_shape)
    place = jnp.stack([section, core, spot]).astype(jnp.int32)

    packed, skip = pack_weights(
        plan, latent_codes, cell_shape,
        direction_first[0], gain_first, bias_first, direction_second[0], gain_second, bias_second,
    )
    sending = cut(packed, core * plan.half, plan.half)
    far = swap_section(cut(sending, spot * plan.piece, plan.piece), 3)
    sending, far = lax.optimization_barrier((sending, far))
    x_mine = swap_section(sending, 1)
    y_mine = swap_section(sending, 2)
    far_mine = gather_chips(plan, far)
    other = swap_dp(jnp.concatenate([x_mine, y_mine, far_mine]), 1)
    weights = spread_weights(plan, place, packed, x_mine, y_mine, far_mine, other)

    blocks = total // ROWS
    ids = shape_ids.reshape(blocks, 1, ROWS)
    places = positions.reshape(coords, blocks, ROWS).transpose(1, 0, 2)
    here = jnp.where((section == 0) | (section == SECTIONS - 1), 0, blocks // 2)
    there = blocks // 2 - here

    given, partials, into = [], [], []
    done = 0
    for steps in CALLS:
        scalars = jnp.stack([here + done, section]).astype(jnp.int32)
        *into, give_x, give_y, grads = run_blocks(
            plan, False, steps, scalars, inputs, cotangent, ids, places, cell_shape, weights, into, []
        )
        given.append((swap_section(give_x, 1), swap_section(give_y, 2)))
        partials.append(grads)
        done += steps
    done = 0
    for steps, got in zip(CALLS, given):
        scalars = jnp.stack([there + done, section]).astype(jnp.int32)
        *into, grads = run_blocks(
            plan, True, steps, scalars, inputs, cotangent, ids, places, cell_shape, weights, into, got
        )
        partials.append(grads)
        done += steps
    act, ig = into

    partial = sum(grads.astype(F32) for grads in partials)
    piece = reduce_pieces(plan, partial, core, spot)
    mine = gather_chips(plan, piece)
    owned = mm(piece[2 * plan.share : 2 * plan.share + plan.owned], skip, NT)
    code = cut(owned, section * plan.per, plan.per)
    for distance in range(1, SECTIONS):
        away = jnp.bitwise_xor(section, distance)
        code = code + swap_section(cut(owned, away * plan.per, plan.per), distance)
    mine, code = lax.optimization_barrier((mine, code))
    other = swap_dp(mine, 1)
    first, first_gain, first_bias, second, second_gain, second_bias = finish_grads(
        plan, place, mine, other, direction_first[0], gain_first, direction_second[0], gain_second,
        latent_codes, cell_shape,
    )
    return (
        act[None], ig[None], code, first[None], first_gain, first_bias, second[None], second_gain, second_bias,
    )


def solution(mesh):
    in_specs = (
        P("dp", None), P("dp", None), P(), P(None, "dp"), P("dp"),
        P("section", None, None), P("section", None), P("section", None),
        P("section", None, None), P("section", None), P("section", None),
    )
    out_specs = (
        P("section", "dp", None), P("section", "dp", None), P(("section", "dp"), None),
        P("section", None, None), P("section", None), P("section", None),
        P("section", None, None), P("section", None), P("section", None),
    )
    return jax.shard_map(shards, mesh=mesh, in_specs=in_specs, out_specs=out_specs, check_vma=False)
```

```python
import functools

import jax
import jax.numpy as jnp
import numpy as np
from jax import lax
from jax.experimental import pallas as pl
from jax.experimental.pallas import tpu as pltpu
from jax.sharding import PartitionSpec as P

BF = jnp.bfloat16
F32 = jnp.float32
NT = (((1,), (1,)), ((), ()))
TN = (((0,), (0,)), ((), ()))
SECTIONS = 4
ROWS = 768
CALLS = (3, 2)
HELPED_CALLS = ((0,), (1,))
VMEM = 40 * 2**20
SMALL_VMEM = 12 * 2**20
ALL_VMEM = 63 * 2**20
GIVE_X = (7, 6, 3, 8)
GIVE_Y = (8, 3, 6, 7)
FURTHER = (0, 1, 1, 2)


def up(value, step):
    return -(-value // step) * step


def mm(left, right, dims=(((1,), (0,)), ((), ()))):
    return lax.dot_general(left, right, dims, preferred_element_type=F32)


def silu_parts(half):
    lift = 1.0 + jnp.tanh(half)
    out = (half * lift).astype(BF)
    lift = lift.astype(BF)
    return out, lift + out * (BF(2.0) - lift)


def stream(count, *stages):
    values = [None] * count
    for tick in range(count + len(stages) - 1):
        for j, stage in enumerate(stages):
            i = tick - j
            if 0 <= i < count:
                values[i] = stage(i, values[i])


class Plan:
    def __init__(self, width, coords, shapes, devices):
        self.width, self.coords, self.shapes, self.devices = width, coords, shapes, devices
        self.spots = devices // 2
        self.share = width // devices
        self.owned = shapes // devices
        self.per = self.owned // SECTIONS
        self.room = up(self.owned + 1, 16)
        self.cells = self.room * devices
        self.piece = 2 * self.share + self.room
        self.half = self.piece * self.spots
        self.packed = 2 * self.half
        table = np.full((self.cells, 1), -1, np.int32)
        for p in range(devices):
            place = 2 * (p % self.spots) + p // self.spots
            for j in range(self.owned):
                table[p * self.room + j, 0] = ((j // self.per) * devices + place) * self.per + j % self.per
        self.cell_shape = table

    def grant(self, base):
        return base + max(0, self.cells - 128) * 8192

    def special(self, j):
        return j * self.room + self.owned


class Block:
    def __init__(self, plan, weights, ext, subs):
        self.width, self.plan, self.weights, self.ext, self.subs = plan.width, plan, weights, ext, subs

    def first(self, k):
        return self.weights[k, : self.width, :]

    def second(self, k):
        return self.weights[k, self.width : 2 * self.width, :]

    def inner(self, k, source):
        beside = self.weights[k, 2 * self.width :, :]
        return lambda i, unused: mm(source(i), self.first(k)) + mm(self.ext[self.subs[i], :], beside)

    def outer(self, k):
        begin = 2 * self.width + self.plan.coords * self.plan.room
        spot = self.plan.owned
        offset = self.weights[k, begin : begin + self.plan.room, :].astype(F32)[spot : spot + 1]
        return lambda i, active: mm(active, self.second(k)) + offset

    def back_second(self, k, grads):
        return lambda i, unused: mm(grads(i), self.second(k), NT)

    def back_first(self, k):
        return lambda i, grads: mm(grads, self.first(k), NT)


def place_cells(point, places, cell_shape, plan, ext, ext_turned):
    rows = ext.shape[0]
    hit = jnp.where(cell_shape[...] == jnp.broadcast_to(point[...], (plan.cells, rows)), 1.0, 0.0)
    cell = lax.broadcasted_iota(jnp.int32, (plan.cells, rows), 0)
    for j in range(plan.coords):
        hit = jnp.where(cell == plan.special(j), places[j : j + 1, :].astype(F32), hit)
    ext_turned[...] = hit.astype(BF)
    ext[...] = hit.T.astype(BF)


def add_weight_grads(accs, active, outer_grad, entering, inner_grad, ext_turned):
    first, second, cell, bias = accs
    second[...] += mm(active, outer_grad, TN)
    first[...] += mm(entering, inner_grad, TN)
    cell[...] += mm(ext_turned[...], inner_grad)
    bias[...] += jnp.sum(outer_grad.astype(F32).reshape(-1, 8, outer_grad.shape[1]), axis=0)


def store_weight_grads(accs, plan, core, mine, theirs):
    first, second, cell, bias = accs
    share, room = plan.share, plan.room
    last = jnp.sum(bias[...], axis=0, keepdims=True)
    row = lax.broadcasted_iota(jnp.int32, cell.shape, 0)
    cell[...] = jnp.where(row == plan.special(plan.coords), last, cell[...])
    for side in range(2):
        @pl.when(core == side)
        def _(side=side):
            for p in range(plan.devices):
                out = mine if p // plan.spots == side else theirs
                at = (p % plan.spots) * plan.piece
                out[at : at + share, :] = second[p * share : (p + 1) * share, :].astype(BF)
                out[at + share : at + 2 * share, :] = first[p * share : (p + 1) * share, :].astype(BF)
                out[at + 2 * share : at + plan.piece, :] = cell[p * room : (p + 1) * room, :].astype(BF)


def pick(section, choices):
    found = jnp.int32(choices[0])
    for k in range(1, SECTIONS):
        found = jnp.where(section == k, choices[k], found)
    return found


def self_half(section, blocks):
    return jnp.where((section == 0) | (section == SECTIONS - 1), 0, blocks // 2)


def self_kernel(
    plan, steps, aliased, sc, h_in, g_in, ids, places, other_h, other_ids, other_places, cell_shape, weights, *refs
):
    act, ig, give_x, give_y, after_first, mine, theirs, ext, ext_turned, states, mids, slope1, slope2, *accs = refs[aliased:]
    section, core = sc[0], sc[1]
    step = pl.program_id(0)
    rows = h_in.shape[0]
    half = rows // 2
    subs = [pl.ds(0, half), pl.ds(half, half)]
    do = Block(plan, weights, ext, subs)

    @pl.when(step == 0)
    def _():
        for acc in accs:
            acc[...] = jnp.zeros_like(acc)

    @pl.when(section == 2)
    def _():
        place_cells(other_ids, other_places, cell_shape, plan, ext, ext_turned)

        def keep(i, z):
            after_first[subs[i], :] = silu_parts(z)[0]
        stream(2, do.inner(0, lambda i: other_h[subs[i], :]), lambda i, z: silu_parts(z)[0], do.outer(0), keep)

    place_cells(ids, places, cell_shape, plan, ext, ext_turned)
    states[0] = h_in[...]

    def keep_active(k):
        def stage(i, z):
            active, slope = silu_parts(z)
            mids[k, subs[i], :] = active
            slope1[k, subs[i], :] = slope
            return active
        return stage

    def keep_state(k):
        def stage(i, z):
            after, slope = silu_parts(z)
            states[k + 1, subs[i], :] = after
            if k == SECTIONS - 1:
                slope = slope * (g_in[subs[i], :] * BF(0.5))
            slope2[k, subs[i], :] = slope
        return stage

    def inner_grad(k):
        def stage(i, grads):
            grads = (grads * slope1[k, subs[i], :].astype(F32)).astype(BF)
            slope1[k, subs[i], :] = grads
            return grads
        return stage

    def enter_grad(k, below):
        def stage(i, grads):
            grads = grads.astype(BF)
            states[5 + k, subs[i], :] = grads
            if below is not None:
                slope2[below, subs[i], :] = grads * slope2[below, subs[i], :]
        return stage

    def back(k, below):
        return [do.back_second(k, lambda i: slope2[k, subs[i], :]), inner_grad(k), do.back_first(k),
                enter_grad(k, below)]

    top = SECTIONS - 1
    stages = []
    for k in range(SECTIONS):
        source = (lambda i: h_in[subs[i], :]) if k == 0 else (lambda i, k=k: states[k, subs[i], :])
        stages += [do.inner(k, source), keep_active(k), do.outer(k), keep_state(k)]
    stream(2, *stages, *back(top, top - 1))

    for own in range(SECTIONS):
        @pl.when(section == own)
        def _(own=own):
            further = FURTHER[own]
            stages = []
            for k in range(top - 1, own - 1, -1):
                stages += back(k, k - 1 if k > further else None)
            if stages:
                stream(2, *stages)
            if further < own:
                value = None
                for stage in back(further, None):
                    value = stage(1, value)

    act[...] = states[section + 1]
    ig[...] = states[5 + section] * BF(2.0)
    give_x[...] = states[pick(section, GIVE_X), subs[0], :]
    give_y[...] = states[pick(section, GIVE_Y), subs[1], :]
    add_weight_grads(accs, mids[section], slope2[section], states[section], slope1[section], ext_turned)

    @pl.when(step == steps - 1)
    def _():
        store_weight_grads(accs, plan, core, mine, theirs)


def helped_kernel(
    plan, steps, counts, sc, h_in, g_in, ids, places, cell_shape, weights, *refs
):
    sources, refs = refs[: 3 * len(counts)], refs[3 * len(counts) + 2 :]
    act, ig, mine, theirs, ext, ext_turned, entering, got, mid, slope1, slope2, *accs = refs
    section, core = sc[0], sc[1]
    step = pl.program_id(0)
    rows = h_in.shape[0]
    half = rows // 2
    subs = [pl.ds(0, half), pl.ds(half, half)]
    do = Block(plan, weights, ext, subs)

    @pl.when(step == 0)
    def _():
        for acc in accs:
            acc[...] = jnp.zeros_like(acc)

    place_cells(ids, places, cell_shape, plan, ext, ext_turned)
    top = section == SECTIONS - 1
    begin = 0
    for j, count in enumerate(counts):
        got_x, got_y, after_first = sources[3 * j : 3 * j + 3]
        now = (step >= begin) & (step < begin + count)
        begin += count

        @pl.when(now)
        def _():
            got[subs[0], :] = got_x[...]
            got[subs[1], :] = got_y[...]

        @pl.when(now & (section == 2))
        def _():
            entering[...] = after_first[...]

    @pl.when(section <= 1)
    def _():
        entering[...] = h_in[...]

    @pl.when(top)
    def _():
        entering[...] = got[...]
        got[...] = g_in[...] * BF(0.5)

    def active_only(i, z):
        return silu_parts(z)[0]

    def enter(i, z):
        entering[subs[i], :] = silu_parts(z)[0]

    def keep_active(i, z):
        active, slope = silu_parts(z)
        mid[subs[i], :] = active
        slope1[subs[i], :] = slope
        return active

    def keep_own(i, z):
        after, slope = silu_parts(z)
        act[subs[i], :] = after
        grads = slope * got[subs[i], :]
        slope2[subs[i], :] = grads
        return grads

    def inner_grad(i, grads):
        grads = (grads * slope1[subs[i], :].astype(F32)).astype(BF)
        slope1[subs[i], :] = grads
        return grads

    def enter_grad(i, grads):
        ig[subs[i], :] = (2.0 * grads).astype(BF)

    def source(i):
        return entering[subs[i], :]

    @pl.when((section == 1) | (section == 2))
    def _():
        stream(2, do.inner(section - 1, source), active_only, do.outer(section - 1), enter)

    stream(2, do.inner(section, source), keep_active, do.outer(section), keep_own,
           do.back_second(section, lambda i: slope2[subs[i], :]), inner_grad, do.back_first(section), enter_grad)
    add_weight_grads(accs, mid[...], slope2[...], entering[...], slope1[...], ext_turned)

    @pl.when(step == steps - 1)
    def _():
        store_weight_grads(accs, plan, core, mine, theirs)


def run_blocks(plan, done, place, h, g, ids, places, cell_shape, weights, into, counts, sources):
    total, width = h.shape
    blocks = total // ROWS
    helped = len(sources) > 0
    steps = sum(counts)

    def here(i, sc):
        start = self_half(sc[0], blocks)
        return (blocks // 2 - start if helped else start) + done + i

    def there(i, sc):
        return blocks // 2 - self_half(sc[0], blocks) + done + i

    def block_specs(where):
        return [
            pl.BlockSpec((None, 1, ROWS), lambda i, sc: (where(i, sc), 0, 0)),
            pl.BlockSpec((None, plan.coords, ROWS), lambda i, sc: (where(i, sc), 0, 0)),
        ]

    rows = pl.BlockSpec((ROWS, width), lambda i, sc: (here(i, sc), 0))
    other_rows = pl.BlockSpec((ROWS, width), lambda i, sc: (there(i, sc), 0))
    hbm = pl.BlockSpec(memory_space=pl.ANY)
    vmem = pl.BlockSpec(memory_space=pltpu.VMEM)
    fixed = pl.BlockSpec((plan.half, width), lambda i, sc: (0, 0))
    array = lambda count: jax.ShapeDtypeStruct((count, width), BF)
    block = lambda *lead: pltpu.VMEM((*lead, ROWS, width), BF)
    scratch = [pltpu.VMEM((ROWS, plan.cells), BF), pltpu.VMEM((plan.cells, ROWS), BF)]
    if helped:
        kernel = functools.partial(helped_kernel, plan, steps, counts)
        out_shape = [array(total)] * 2 + [array(plan.half)] * 2
        out_specs = [rows, rows, fixed, fixed]
        scratch += [block()] * 5
        source_specs, begin = [], 0
        for count in counts:
            at = lambda i, sc, begin=begin, count=count: (jnp.clip(i - begin, 0, count - 1), 0)
            half_rows = pl.BlockSpec((ROWS // 2, width), at)
            source_specs += [half_rows, half_rows, pl.BlockSpec((ROWS, width), at)]
            begin += count
        operands = [h, g, ids, places, cell_shape, weights, *sources, *into]
        in_specs = [rows, rows, *block_specs(here), vmem, vmem, *source_specs, hbm, hbm]
        units = 8
    else:
        kernel = functools.partial(self_kernel, plan, steps, len(into))
        halves = pl.BlockSpec((ROWS // 2, width), lambda i, sc: (i, 0))
        out_shape = ([array(total)] * 2 + [array(steps * ROWS // 2)] * 2 + [array(steps * ROWS)]
                     + [array(plan.half)] * 2)
        out_specs = [rows, rows, halves, halves, pl.BlockSpec((ROWS, width), lambda i, sc: (i, 0)), fixed, fixed]
        scratch += [block(10), block(SECTIONS), block(SECTIONS), block(SECTIONS)]
        operands = [h, g, ids, places, h, ids, places, cell_shape, weights, *into]
        in_specs = [rows, rows, *block_specs(here), other_rows, *block_specs(there), vmem, vmem, *[hbm] * len(into)]
        units = 21
    scratch += [pltpu.VMEM((width, width), F32), pltpu.VMEM((width, width), F32),
                pltpu.VMEM((plan.cells, width), F32), pltpu.VMEM((8, width), F32)]
    first_into = 1 + len(operands) - len(into)
    return pl.pallas_call(
        kernel,
        grid_spec=pltpu.PrefetchScalarGridSpec(
            num_scalar_prefetch=1, grid=(steps,), in_specs=in_specs, out_specs=out_specs, scratch_shapes=scratch,
        ),
        out_shape=out_shape,
        input_output_aliases={first_into + j: j for j in range(len(into))},
        compiler_params=pltpu.CompilerParams(vmem_limit_bytes=plan.grant(VMEM)),
        cost_estimate=pl.CostEstimate(
            flops=2 * steps * ROWS * width * width * units, bytes_accessed=steps * ROWS * width * 12,
            transcendentals=steps * ROWS * width * 8,
        ),
    )(place, *operands)


def normed(direction, gain_row):
    scale = gain_row / jnp.sqrt(jnp.sum(direction * direction, axis=0, keepdims=True) + 1e-06)
    return (direction * scale).astype(BF)


def pack_kernel(plan, latent, *refs):
    sources, (packed, skip, side, far), held, sems = refs[:8], refs[8:12], refs[12:20], refs[20]
    copies = [pltpu.make_async_copy(s, h, sems.at[j]) for j, (s, h) in enumerate(zip(sources, held))]
    for copy in copies:
        copy.start()
    for copy in copies:
        copy.wait()
    dir_first, gain_first, bias_first, dir_second, gain_second, bias_second, latents, cell_shape = held
    width = plan.width
    half = BF(0.5)
    first = normed(dir_first[...].astype(F32), gain_first[...].astype(F32))
    second = normed(dir_second[...].astype(F32), gain_second[...].astype(F32))
    packed[:width, :] = first[:width] * half
    packed[width : 2 * width, :] = second * half
    skip[...] = first[width : width + latent]
    shape = lax.broadcasted_iota(jnp.int32, (plan.cells, plan.shapes), 1)
    onehot = jnp.where(cell_shape[...] == shape, 1.0, 0.0).astype(BF)
    by_cell = mm(onehot, latents[...]).astype(BF)
    by_cell = mm(by_cell, skip[...])
    by_cell = 0.5 * jnp.where(cell_shape[...] >= 0, by_cell + bias_first[...].astype(F32), 0.0)
    cell = lax.broadcasted_iota(jnp.int32, by_cell.shape, 0)
    tail = 0.5 * first[width + latent :].astype(F32)
    for j in range(plan.coords):
        by_cell = jnp.where(cell == plan.special(j), tail[j : j + 1], by_cell)
    by_cell = jnp.where(cell == plan.special(plan.coords), 0.5 * bias_second[...].astype(F32), by_cell)
    packed[2 * width :, :] = by_cell.astype(BF)
    place = lax.axis_index("dp")
    begin = lax.rem(place, 2) * plan.half
    side[...] = packed[pl.ds(pl.multiple_of(begin, 16), plan.half), :]
    far[...] = packed[pl.ds(pl.multiple_of(begin + lax.div(place, 2) * plan.piece, 16), plan.piece), :]


def pack_weights(plan, latents, cell_shape, *own):
    width = plan.width
    latent = latents.shape[1]
    vmem = pl.BlockSpec(memory_space=pltpu.VMEM)
    return pl.pallas_call(
        functools.partial(pack_kernel, plan, latent),
        in_specs=[pl.BlockSpec(memory_space=pl.ANY)] * 8,
        out_specs=[vmem] * 4,
        scratch_shapes=[pltpu.VMEM(array.shape, array.dtype) for array in (*own, latents, cell_shape)]
        + [pltpu.SemaphoreType.DMA((8,))],
        out_shape=[jax.ShapeDtypeStruct((rows, width), BF) for rows in (plan.packed, latent, plan.half, plan.piece)],
        compiler_params=pltpu.CompilerParams(vmem_limit_bytes=ALL_VMEM),
        cost_estimate=pl.CostEstimate(flops=2 * plan.cells * width * latent, bytes_accessed=4 * plan.packed * width,
                                      transcendentals=0),
    )(*own, latents, cell_shape)


def join_kernel(count, *refs):
    sources, out, sems = refs[:count], refs[count], refs[count + 1]
    copies, row = [], 0
    for j, source in enumerate(sources):
        copies.append(pltpu.make_async_copy(source, out.at[pl.ds(row, source.shape[0])], sems.at[j]))
        row += source.shape[0]
    for copy in copies:
        copy.start()
    for copy in copies:
        copy.wait()


def join(plan, arrays):
    rows = sum(array.shape[0] for array in arrays)
    return pl.pallas_call(
        functools.partial(join_kernel, len(arrays)),
        in_specs=[pl.BlockSpec(memory_space=pl.ANY)] * len(arrays),
        out_specs=pl.BlockSpec(memory_space=pltpu.VMEM),
        scratch_shapes=[pltpu.SemaphoreType.DMA((len(arrays),))],
        out_shape=jax.ShapeDtypeStruct((rows, arrays[0].shape[1]), arrays[0].dtype),
        compiler_params=pltpu.CompilerParams(vmem_limit_bytes=plan.grant(SMALL_VMEM)),
        cost_estimate=pl.CostEstimate(flops=0, bytes_accessed=4 * rows * arrays[0].shape[1], transcendentals=0),
    )(*arrays)


def spread_kernel(plan, sc, own, mine, other, weights, sems):
    section, core, spot = sc[0], sc[1], sc[2]
    half, piece = plan.half, plan.piece
    away = 1 - core
    copies = [(own, weights.at[section])]
    for j in range(2):
        there = weights.at[jnp.bitwise_xor(section, j + 1)]
        for block, side in ((mine, core), (other, away)):
            copies.append((block.at[pl.ds(j * half, half)], there.at[pl.ds(side * half, half)]))
    there = weights.at[jnp.bitwise_xor(section, 3)]
    for j in range(plan.spots):
        z = jnp.bitwise_xor(spot, j)
        for block, side in ((mine, core), (other, away)):
            copies.append((block.at[pl.ds(2 * half + j * piece, piece)], there.at[pl.ds(side * half + z * piece, piece)]))
    copies = [pltpu.make_async_copy(source, target, sems.at[j]) for j, (source, target) in enumerate(copies)]
    for copy in copies:
        copy.start()
    for copy in copies:
        copy.wait()


def spread_weights(plan, scalars, *arrays):
    hbm = pl.BlockSpec(memory_space=pl.ANY)
    return pl.pallas_call(
        functools.partial(spread_kernel, plan),
        grid_spec=pltpu.PrefetchScalarGridSpec(
            num_scalar_prefetch=1, grid=(1,), in_specs=[hbm] * 3,
            out_specs=pl.BlockSpec(memory_space=pltpu.VMEM),
            scratch_shapes=[pltpu.SemaphoreType.DMA((5 + 2 * plan.spots,))],
        ),
        out_shape=jax.ShapeDtypeStruct((SECTIONS, plan.packed, plan.width), BF),
        compiler_params=pltpu.CompilerParams(vmem_limit_bytes=plan.grant(SMALL_VMEM)),
        cost_estimate=pl.CostEstimate(flops=0, bytes_accessed=16 * plan.packed * plan.width, transcendentals=0),
    )(scalars, *arrays)


def grads_kernel(plan, latent, sc, mine, other, dir_first, gain_first, dir_second, gain_second, latents, cell_shape,
                 first_out, first_gain, first_bias, second_out, second_gain, second_bias, cells):
    core, spot = sc[1], sc[2]
    width, share, room, piece = plan.width, plan.share, plan.room, plan.piece
    for source, side in ((mine, core), (other, 1 - core)):
        for j in range(plan.spots):
            p = side * plan.spots + jnp.bitwise_xor(spot, j)
            base = j * piece
            rows = pl.ds(pl.multiple_of(p * share, share), share)
            second_out[rows, :] = source[base : base + share, :].astype(F32)
            first_out[rows, :] = source[base + share : base + 2 * share, :].astype(F32)
            rows = pl.ds(pl.multiple_of(p * room, room), room)
            cells[rows, :] = source[base + 2 * share : base + piece, :].astype(F32)
    by_cell = cells[...]
    shaped = jnp.where(cell_shape[...] >= 0, by_cell, 0.0)
    first_bias[...] = jnp.sum(shaped, axis=0, keepdims=True)
    shape = lax.broadcasted_iota(jnp.int32, (plan.cells, plan.shapes), 1)
    onehot = jnp.where(cell_shape[...] == shape, 1.0, 0.0).astype(BF)
    by_shape = mm(onehot, latents[...]).astype(BF)
    first_out[width : width + latent, :] = mm(by_shape, shaped.astype(BF), TN)
    for j in range(plan.coords):
        spot_row = plan.special(j)
        first_out[width + latent + j : width + latent + j + 1, :] = cells[spot_row : spot_row + 1, :]
    spot_row = plan.special(plan.coords)
    second_bias[...] = cells[spot_row : spot_row + 1, :]
    for direction, gain, out, gain_out in ((dir_first, gain_first, first_out, first_gain),
                                           (dir_second, gain_second, second_out, second_gain)):
        values = direction[...].astype(F32)
        summed = out[...]
        norm = jnp.sqrt(jnp.sum(values * values, axis=0, keepdims=True) + 1e-06)
        along = jnp.sum(values * summed, axis=0, keepdims=True)
        gain_out[...] = along / norm
        scale = gain[...].astype(F32) / norm
        out[...] = scale * summed - (scale * along / (norm * norm)) * values


def finish_grads(plan, scalars, mine, other, dir_first, gain_first, dir_second, gain_second, latents, cell_shape):
    width = plan.width
    vmem = pl.BlockSpec(memory_space=pltpu.VMEM)
    row = jax.ShapeDtypeStruct((1, width), F32)
    whole = lambda like: jax.ShapeDtypeStruct(like.shape, F32)
    return pl.pallas_call(
        functools.partial(grads_kernel, plan, latents.shape[1]),
        grid_spec=pltpu.PrefetchScalarGridSpec(
            num_scalar_prefetch=1, grid=(1,), in_specs=[vmem] * 8, out_specs=[vmem] * 6,
            scratch_shapes=[pltpu.VMEM((plan.cells, width), F32)],
        ),
        out_shape=[whole(dir_first), row, row, whole(dir_second), row, row],
        compiler_params=pltpu.CompilerParams(vmem_limit_bytes=plan.grant(SMALL_VMEM)),
        cost_estimate=pl.CostEstimate(flops=2 * plan.cells * width * latents.shape[1],
                                      bytes_accessed=8 * plan.packed * width, transcendentals=0),
    )(scalars, mine, other, dir_first, gain_first, dir_second, gain_second, latents, cell_shape)


def swap_section(block, distance):
    route = [(i, i ^ distance) for i in range(lax.axis_size("section"))]
    return lax.ppermute(block, "section", route)


def swap_dp(block, distance):
    route = [(i, i ^ distance) for i in range(lax.axis_size("dp"))]
    return lax.ppermute(block, "dp", route)


def cut(array, first, count):
    return lax.dynamic_slice_in_dim(array, first, count, 0)


def reduce_pieces(plan, chip, spot):
    piece = plan.piece
    total = cut(chip, spot * piece, piece).astype(F32)
    for distance in range(1, plan.spots):
        away = jnp.bitwise_xor(spot, distance)
        total = total + swap_dp(cut(chip, away * piece, piece), 2 * distance).astype(F32)
    return total.astype(BF)


def gather_chips(plan, piece):
    return [piece] + [swap_dp(piece, 2 * distance) for distance in range(1, plan.spots)]


def shards(
    inputs, cotangent, latent_codes, positions, shape_ids,
    direction_first, gain_first, bias_first, direction_second, gain_second, bias_second,
):
    section = lax.axis_index("section")
    dp_rank = lax.axis_index("dp")
    core, spot = dp_rank % 2, dp_rank // 2
    total, width = inputs.shape
    shapes, latent = latent_codes.shape
    coords = positions.shape[0]
    plan = Plan(width, coords, shapes, lax.axis_size("dp"))
    cell_shape = jnp.asarray(plan.cell_shape)
    place = jnp.stack([section, core, spot]).astype(jnp.int32)

    packed, skip, sending, far = pack_weights(
        plan, latent_codes, cell_shape,
        direction_first[0], gain_first, bias_first, direction_second[0], gain_second, bias_second,
    )
    far = swap_section(far, 3)
    sending, far = lax.optimization_barrier((sending, far))
    x_mine = swap_section(sending, 1)
    y_mine = swap_section(sending, 2)
    far_mine = gather_chips(plan, far)
    mine = join(plan, [x_mine, y_mine, *far_mine])
    weights = spread_weights(plan, place, packed, mine, swap_dp(mine, 1))

    blocks = total // ROWS
    ids = shape_ids.reshape(blocks, 1, ROWS)
    places = positions.reshape(coords, blocks, ROWS).transpose(1, 0, 2)
    same = (inputs, cotangent, ids, places, cell_shape, weights)
    given, parts, into, starts = [], [], [], []
    done = 0
    for steps in CALLS:
        *into, give_x, give_y, after_first, mine, theirs = run_blocks(
            plan, done, place, *same, into, (steps,), []
        )
        given.append((swap_section(give_x, 1), swap_section(give_y, 2), after_first))
        parts.append((mine, theirs))
        starts.append(done)
        done += steps
    for calls in HELPED_CALLS:
        sources = [source for call in calls for source in given[call]]
        counts = tuple(CALLS[call] for call in calls)
        *into, mine, theirs = run_blocks(plan, starts[calls[0]], place, *same, into, counts, sources)
        parts.append((mine, theirs))
    act, ig = into

    mine, theirs = (sum(part.astype(F32) for part in side) for side in zip(*parts))
    chip = (mine + swap_dp(theirs.astype(BF), 1).astype(F32)).astype(BF)
    piece = reduce_pieces(plan, chip, spot)
    pieces = gather_chips(plan, piece)
    ready, pieces[1] = lax.optimization_barrier((piece, pieces[1]))
    owned = mm(ready[2 * plan.share : 2 * plan.share + plan.owned], skip, NT)
    code = cut(owned, section * plan.per, plan.per)
    for distance in range(1, SECTIONS):
        away = jnp.bitwise_xor(section, distance)
        code = code + swap_section(cut(owned, away * plan.per, plan.per), distance)
    mine = join(plan, pieces)
    mine, code = lax.optimization_barrier((mine, code))
    other = swap_dp(mine, 1)
    first, first_gain, first_bias, second, second_gain, second_bias = finish_grads(
        plan, place, mine, other, direction_first[0], gain_first, direction_second[0], gain_second,
        latent_codes, cell_shape,
    )
    return (
        act[None], ig[None], code, first[None], first_gain, first_bias, second[None], second_gain, second_bias,
    )


def solution(mesh):
    in_specs = (
        P("dp", None), P("dp", None), P(), P(None, "dp"), P("dp"),
        P("section", None, None), P("section", None), P("section", None),
        P("section", None, None), P("section", None), P("section", None),
    )
    out_specs = (
        P("section", "dp", None), P("section", "dp", None), P(("section", "dp"), None),
        P("section", None, None), P("section", None), P("section", None),
        P("section", None, None), P("section", None), P("section", None),
    )
    return jax.shard_map(shards, mesh=mesh, in_specs=in_specs, out_specs=out_specs, check_vma=False)
```

```python
import functools

import jax
import jax.numpy as jnp
import numpy as np
from jax import lax
from jax.experimental import pallas as pl
from jax.experimental.pallas import tpu as pltpu
from jax.sharding import PartitionSpec as P

BF = jnp.bfloat16
F32 = jnp.float32
NT = (((1,), (1,)), ((), ()))
TN = (((0,), (0,)), ((), ()))
SECTIONS = 4
ROWS = 768
CALLS = (3, 2)
HELPED_CALLS = ((0,), (1,))
VMEM = 36 * 2**20
SMALL_VMEM = 12 * 2**20
ALL_VMEM = 63 * 2**20
GIVE_X = (7, 6, 3, 8)
GIVE_Y = (8, 3, 6, 7)


def up(value, step):
    return -(-value // step) * step


def mm(left, right, dims=(((1,), (0,)), ((), ()))):
    return lax.dot_general(left, right, dims, preferred_element_type=F32)


def silu_parts(half):
    lift = 1.0 + jnp.tanh(half)
    out = (half * lift).astype(BF)
    lift = lift.astype(BF)
    return out, lift + out * (BF(2.0) - lift)


def stream(count, *stages):
    values = [None] * count
    for tick in range(count + len(stages) - 1):
        for j, stage in enumerate(stages):
            i = tick - j
            if 0 <= i < count:
                values[i] = stage(i, values[i])


class Plan:
    def __init__(self, width, coords, shapes, devices):
        self.width, self.coords, self.shapes, self.devices = width, coords, shapes, devices
        self.spots = devices // 2
        self.share = width // devices
        self.owned = shapes // devices
        self.per = self.owned // SECTIONS
        self.room = up(self.owned + 1, 16)
        self.cells = self.room * devices
        self.piece = 2 * self.share + self.room
        self.half = self.piece * self.spots
        self.packed = 2 * self.half
        table = np.full((self.cells, 1), -1, np.int32)
        for p in range(devices):
            place = 2 * (p % self.spots) + p // self.spots
            for j in range(self.owned):
                table[p * self.room + j, 0] = ((j // self.per) * devices + place) * self.per + j % self.per
        self.cell_shape = table

    def grant(self, base):
        return base + max(0, self.cells - 128) * 12288

    def special(self, j):
        return j * self.room + self.owned


class Block:
    def __init__(self, plan, weights, ext, subs):
        self.width, self.plan, self.weights, self.ext, self.subs = plan.width, plan, weights, ext, subs

    def first(self, k):
        return self.weights[k, : self.width, :]

    def second(self, k):
        return self.weights[k, self.width : 2 * self.width, :]

    def inner(self, k, source):
        beside = self.weights[k, 2 * self.width :, :]
        return lambda i, unused: mm(source(i), self.first(k)) + mm(self.ext[self.subs[i], :], beside)

    def outer(self, k):
        begin = 2 * self.width + self.plan.coords * self.plan.room
        spot = self.plan.owned
        offset = self.weights[k, begin : begin + self.plan.room, :].astype(F32)[spot : spot + 1]
        return lambda i, active: mm(active, self.second(k)) + offset

    def back_second(self, k, grads):
        return lambda i, unused: mm(grads(i), self.second(k), NT)

    def back_first(self, k):
        return lambda i, grads: mm(grads, self.first(k), NT)


def place_cells(point, places, cell_shape, plan, ext, ext_turned):
    rows = ext.shape[0]
    hit = jnp.where(cell_shape[...] == jnp.broadcast_to(point[...], (plan.cells, rows)), 1.0, 0.0)
    cell = lax.broadcasted_iota(jnp.int32, (plan.cells, rows), 0)
    for j in range(plan.coords):
        hit = jnp.where(cell == plan.special(j), places[j : j + 1, :].astype(F32), hit)
    ext_turned[...] = hit.astype(BF)
    ext[...] = hit.T.astype(BF)


def add_weight_grads(accs, active, outer_grad, entering, inner_grad, ext_turned):
    first, second, cell, bias = accs
    second[...] += mm(active, outer_grad, TN)
    first[...] += mm(entering, inner_grad, TN)
    cell[...] += mm(ext_turned[...], inner_grad)
    bias[...] += jnp.sum(outer_grad.astype(F32).reshape(-1, 8, outer_grad.shape[1]), axis=0)


def store_weight_grads(accs, plan, core, mine, theirs):
    first, second, cell, bias = accs
    share, room = plan.share, plan.room
    last = jnp.sum(bias[...], axis=0, keepdims=True)
    row = lax.broadcasted_iota(jnp.int32, cell.shape, 0)
    cell[...] = jnp.where(row == plan.special(plan.coords), last, cell[...])
    for side in range(2):
        @pl.when(core == side)
        def _(side=side):
            for p in range(plan.devices):
                out = mine if p // plan.spots == side else theirs
                at = (p % plan.spots) * plan.piece
                out[at : at + share, :] = second[p * share : (p + 1) * share, :].astype(BF)
                out[at + share : at + 2 * share, :] = first[p * share : (p + 1) * share, :].astype(BF)
                out[at + 2 * share : at + plan.piece, :] = cell[p * room : (p + 1) * room, :].astype(BF)


def pick(section, choices):
    found = jnp.int32(choices[0])
    for k in range(1, SECTIONS):
        found = jnp.where(section == k, choices[k], found)
    return found


def self_half(section, blocks):
    return jnp.where((section == 0) | (section == SECTIONS - 1), 0, blocks // 2)


def self_kernel(
    plan, steps, aliased, sc, h_in, g_in, ids, places, other_h, other_ids, other_places, cell_shape, weights, *refs
):
    act, ig, give_x, give_y, after_first, mine, theirs, ext, ext_turned, states, mids, slope1, slope2, *accs = refs[aliased:]
    section, core = sc[0], sc[1]
    step = pl.program_id(0)
    rows = h_in.shape[0]
    half = rows // 2
    subs = [pl.ds(0, half), pl.ds(half, half)]
    do = Block(plan, weights, ext, subs)

    @pl.when(step == 0)
    def _():
        for acc in accs:
            acc[...] = jnp.zeros_like(acc)

    @pl.when(section == 2)
    def _():
        place_cells(other_ids, other_places, cell_shape, plan, ext, ext_turned)

        def keep(i, z):
            after_first[pl.ds(pl.multiple_of(step * rows + i * half, 128), half), :] = silu_parts(z)[0]
        stream(2, do.inner(0, lambda i: other_h[subs[i], :]), lambda i, z: silu_parts(z)[0], do.outer(0), keep)

    place_cells(ids, places, cell_shape, plan, ext, ext_turned)
    states[0] = h_in[...]

    def keep_active(k):
        def stage(i, z):
            active, slope = silu_parts(z)
            mids[k, subs[i], :] = active
            slope1[k, subs[i], :] = slope
            return active
        return stage

    def keep_state(k):
        def stage(i, z):
            after, slope = silu_parts(z)
            states[k + 1, subs[i], :] = after
            if k == SECTIONS - 1:
                slope = slope * (g_in[subs[i], :] * BF(0.5))
            slope2[k, subs[i], :] = slope
        return stage

    def inner_grad(k):
        def stage(i, grads):
            grads = (grads * slope1[k, subs[i], :].astype(F32)).astype(BF)
            slope1[k, subs[i], :] = grads
            return grads
        return stage

    def enter_grad(k, below):
        def stage(i, grads):
            grads = grads.astype(BF)
            states[5 + k, subs[i], :] = grads
            if below is not None:
                slope2[below, subs[i], :] = grads * slope2[below, subs[i], :]
        return stage

    def back(k, below):
        return [do.back_second(k, lambda i: slope2[k, subs[i], :]), inner_grad(k), do.back_first(k),
                enter_grad(k, below)]

    top = SECTIONS - 1
    stages = []
    for k in range(SECTIONS):
        source = (lambda i: h_in[subs[i], :]) if k == 0 else (lambda i, k=k: states[k, subs[i], :])
        stages += [do.inner(k, source), keep_active(k), do.outer(k), keep_state(k)]
    stream(2, *stages, *back(top, top - 1))

    def lower(j, unused):
        k = top - 1 - j
        stream(2, *back(k, jnp.where(k > 0, k - 1, SECTIONS)))
        return 0

    lax.fori_loop(0, top - section, lower, 0)

    @pl.when(section >= 2)
    def _():
        value = None
        for stage in back(section - 1, None):
            value = stage(1, value)

    act[...] = states[section + 1]
    ig[...] = states[5 + section] * BF(2.0)
    given = pl.ds(pl.multiple_of(step * half, 128), half)
    give_x[given, :] = states[pick(section, GIVE_X), subs[0], :]
    give_y[given, :] = states[pick(section, GIVE_Y), subs[1], :]
    add_weight_grads(accs, mids[section], slope2[section], states[section], slope1[section], ext_turned)

    @pl.when(step == steps - 1)
    def _():
        store_weight_grads(accs, plan, core, mine, theirs)


def helped_kernel(
    plan, steps, counts, sc, h_in, g_in, ids, places, cell_shape, weights, *refs
):
    sources, refs = refs[: 3 * len(counts)], refs[3 * len(counts) + 2 :]
    act, ig, mine, theirs, ext, ext_turned, entering, got, mid, slope1, slope2, *accs = refs
    section, core = sc[0], sc[1]
    step = pl.program_id(0)
    rows = h_in.shape[0]
    half = rows // 2
    subs = [pl.ds(0, half), pl.ds(half, half)]
    do = Block(plan, weights, ext, subs)

    @pl.when(step == 0)
    def _():
        for acc in accs:
            acc[...] = jnp.zeros_like(acc)

    place_cells(ids, places, cell_shape, plan, ext, ext_turned)
    top = section == SECTIONS - 1
    begin = 0
    for j, count in enumerate(counts):
        got_x, got_y, after_first = sources[3 * j : 3 * j + 3]
        now = (step >= begin) & (step < begin + count)
        begin += count

        @pl.when(now)
        def _():
            got[subs[0], :] = got_x[...]
            got[subs[1], :] = got_y[...]

        @pl.when(now & (section == 2))
        def _():
            entering[...] = after_first[...]

    @pl.when(section <= 1)
    def _():
        entering[...] = h_in[...]

    @pl.when(top)
    def _():
        entering[...] = got[...]
        got[...] = g_in[...] * BF(0.5)

    def active_only(i, z):
        return silu_parts(z)[0]

    def enter(i, z):
        entering[subs[i], :] = silu_parts(z)[0]

    def keep_active(i, z):
        active, slope = silu_parts(z)
        mid[subs[i], :] = active
        slope1[subs[i], :] = slope
        return active

    def keep_own(i, z):
        after, slope = silu_parts(z)
        act[subs[i], :] = after
        grads = slope * got[subs[i], :]
        slope2[subs[i], :] = grads
        return grads

    def inner_grad(i, grads):
        grads = (grads * slope1[subs[i], :].astype(F32)).astype(BF)
        slope1[subs[i], :] = grads
        return grads

    def enter_grad(i, grads):
        ig[subs[i], :] = (2.0 * grads).astype(BF)

    def source(i):
        return entering[subs[i], :]

    @pl.when((section == 1) | (section == 2))
    def _():
        stream(2, do.inner(section - 1, source), active_only, do.outer(section - 1), enter)

    stream(2, do.inner(section, source), keep_active, do.outer(section), keep_own,
           do.back_second(section, lambda i: slope2[subs[i], :]), inner_grad, do.back_first(section), enter_grad)
    add_weight_grads(accs, mid[...], slope2[...], entering[...], slope1[...], ext_turned)

    @pl.when(step == steps - 1)
    def _():
        store_weight_grads(accs, plan, core, mine, theirs)


def run_blocks(plan, done, place, h, g, ids, places, cell_shape, weights, into, counts, sources):
    total, width = h.shape
    blocks = total // ROWS
    helped = len(sources) > 0
    steps = sum(counts)

    def here(i, sc):
        start = self_half(sc[0], blocks)
        return (blocks // 2 - start if helped else start) + done + i

    def there(i, sc):
        return jnp.where(sc[0] == 2, blocks // 2 - self_half(sc[0], blocks) + done + i, 0)

    def block_specs(where):
        return [
            pl.BlockSpec((None, 1, ROWS), lambda i, sc: (where(i, sc), 0, 0)),
            pl.BlockSpec((None, plan.coords, ROWS), lambda i, sc: (where(i, sc), 0, 0)),
        ]

    rows = pl.BlockSpec((ROWS, width), lambda i, sc: (here(i, sc), 0))
    other_rows = pl.BlockSpec((ROWS, width), lambda i, sc: (there(i, sc), 0))
    hbm = pl.BlockSpec(memory_space=pl.ANY)
    vmem = pl.BlockSpec(memory_space=pltpu.VMEM)
    array = lambda count: jax.ShapeDtypeStruct((count, width), BF)
    block = lambda *lead: pltpu.VMEM((*lead, ROWS, width), BF)
    scratch = [pltpu.VMEM((ROWS, plan.cells), BF), pltpu.VMEM((plan.cells, ROWS), BF)]
    if helped:
        kernel = functools.partial(helped_kernel, plan, steps, counts)
        out_shape = [array(total)] * 2 + [array(plan.half)] * 2
        out_specs = [rows, rows, vmem, vmem]
        scratch += [block()] * 5
        source_specs, begin = [], 0
        for count in counts:
            at = lambda i, sc, begin=begin, count=count: (jnp.clip(i - begin, 0, count - 1), 0)
            half_rows = pl.BlockSpec((ROWS // 2, width), at)
            source_specs += [half_rows, half_rows, pl.BlockSpec((ROWS, width), at)]
            begin += count
        operands = [h, g, ids, places, cell_shape, weights, *sources, *into]
        in_specs = [rows, rows, *block_specs(here), vmem, vmem, *source_specs, hbm, hbm]
        units = 8
    else:
        kernel = functools.partial(self_kernel, plan, steps, len(into))
        out_shape = ([array(total)] * 2 + [array(steps * ROWS // 2)] * 2 + [array(steps * ROWS)]
                     + [array(plan.half)] * 2)
        out_specs = [rows, rows, *[vmem] * 5]
        scratch += [block(10), block(SECTIONS), block(SECTIONS), block(SECTIONS + 1)]
        operands = [h, g, ids, places, h, ids, places, cell_shape, weights, *into]
        in_specs = [rows, rows, *block_specs(here), other_rows, *block_specs(there), vmem, vmem, *[hbm] * len(into)]
        units = 21
    scratch += [pltpu.VMEM((width, width), F32), pltpu.VMEM((width, width), F32),
                pltpu.VMEM((plan.cells, width), F32), pltpu.VMEM((8, width), F32)]
    first_into = 1 + len(operands) - len(into)
    return pl.pallas_call(
        kernel,
        grid_spec=pltpu.PrefetchScalarGridSpec(
            num_scalar_prefetch=1, grid=(steps,), in_specs=in_specs, out_specs=out_specs, scratch_shapes=scratch,
        ),
        out_shape=out_shape,
        input_output_aliases={first_into + j: j for j in range(len(into))},
        compiler_params=pltpu.CompilerParams(vmem_limit_bytes=plan.grant(VMEM)),
        cost_estimate=pl.CostEstimate(
            flops=2 * steps * ROWS * width * width * units, bytes_accessed=steps * ROWS * width * 12,
            transcendentals=steps * ROWS * width * 8,
        ),
    )(place, *operands)


def normed(direction, gain_row):
    scale = gain_row / jnp.sqrt(jnp.sum(direction * direction, axis=0, keepdims=True) + 1e-06)
    return (direction * scale).astype(BF)


def pack_kernel(plan, latent, *refs):
    sources, (packed, skip, side, far), held, sems = refs[:8], refs[8:12], refs[12:20], refs[20]
    copies = [pltpu.make_async_copy(s, h, sems.at[j]) for j, (s, h) in enumerate(zip(sources, held))]
    for copy in copies:
        copy.start()
    for copy in copies:
        copy.wait()
    dir_first, gain_first, bias_first, dir_second, gain_second, bias_second, latents, cell_shape = held
    width = plan.width
    half = BF(0.5)
    first = normed(dir_first[...].astype(F32), gain_first[...].astype(F32))
    second = normed(dir_second[...].astype(F32), gain_second[...].astype(F32))
    packed[:width, :] = first[:width] * half
    packed[width : 2 * width, :] = second * half
    skip[...] = first[width : width + latent]
    shape = lax.broadcasted_iota(jnp.int32, (plan.cells, plan.shapes), 1)
    onehot = jnp.where(cell_shape[...] == shape, 1.0, 0.0).astype(BF)
    by_cell = mm(onehot, latents[...]).astype(BF)
    by_cell = mm(by_cell, skip[...])
    by_cell = 0.5 * jnp.where(cell_shape[...] >= 0, by_cell + bias_first[...].astype(F32), 0.0)
    cell = lax.broadcasted_iota(jnp.int32, by_cell.shape, 0)
    tail = 0.5 * first[width + latent :].astype(F32)
    for j in range(plan.coords):
        by_cell = jnp.where(cell == plan.special(j), tail[j : j + 1], by_cell)
    by_cell = jnp.where(cell == plan.special(plan.coords), 0.5 * bias_second[...].astype(F32), by_cell)
    packed[2 * width :, :] = by_cell.astype(BF)
    place = lax.axis_index("dp")
    begin = lax.rem(place, 2) * plan.half
    side[...] = packed[pl.ds(pl.multiple_of(begin, 16), plan.half), :]
    far[...] = packed[pl.ds(pl.multiple_of(begin + lax.div(place, 2) * plan.piece, 16), plan.piece), :]


def pack_weights(plan, latents, cell_shape, *own):
    width = plan.width
    latent = latents.shape[1]
    vmem = pl.BlockSpec(memory_space=pltpu.VMEM)
    return pl.pallas_call(
        functools.partial(pack_kernel, plan, latent),
        in_specs=[pl.BlockSpec(memory_space=pl.ANY)] * 8,
        out_specs=[vmem] * 4,
        scratch_shapes=[pltpu.VMEM(array.shape, array.dtype) for array in (*own, latents, cell_shape)]
        + [pltpu.SemaphoreType.DMA((8,))],
        out_shape=[jax.ShapeDtypeStruct((rows, width), BF) for rows in (plan.packed, latent, plan.half, plan.piece)],
        compiler_params=pltpu.CompilerParams(vmem_limit_bytes=ALL_VMEM),
        cost_estimate=pl.CostEstimate(flops=2 * plan.cells * width * latent, bytes_accessed=4 * plan.packed * width,
                                      transcendentals=0),
    )(*own, latents, cell_shape)


def join_kernel(count, *refs):
    sources, out, sems = refs[:count], refs[count], refs[count + 1]
    copies, row = [], 0
    for j, source in enumerate(sources):
        copies.append(pltpu.make_async_copy(source, out.at[pl.ds(row, source.shape[0])], sems.at[j]))
        row += source.shape[0]
    for copy in copies:
        copy.start()
    for copy in copies:
        copy.wait()


def join(plan, arrays):
    rows = sum(array.shape[0] for array in arrays)
    return pl.pallas_call(
        functools.partial(join_kernel, len(arrays)),
        in_specs=[pl.BlockSpec(memory_space=pl.ANY)] * len(arrays),
        out_specs=pl.BlockSpec(memory_space=pltpu.VMEM),
        scratch_shapes=[pltpu.SemaphoreType.DMA((len(arrays),))],
        out_shape=jax.ShapeDtypeStruct((rows, arrays[0].shape[1]), arrays[0].dtype),
        compiler_params=pltpu.CompilerParams(vmem_limit_bytes=plan.grant(SMALL_VMEM)),
        cost_estimate=pl.CostEstimate(flops=0, bytes_accessed=4 * rows * arrays[0].shape[1], transcendentals=0),
    )(*arrays)


def spread_kernel(plan, sc, own, mine, other, weights, sems):
    section, core, spot = sc[0], sc[1], sc[2]
    half, piece = plan.half, plan.piece
    away = 1 - core
    copies = [(own, weights.at[section])]
    for j in range(2):
        there = weights.at[jnp.bitwise_xor(section, j + 1)]
        for block, side in ((mine, core), (other, away)):
            copies.append((block.at[pl.ds(j * half, half)], there.at[pl.ds(side * half, half)]))
    there = weights.at[jnp.bitwise_xor(section, 3)]
    for j in range(plan.spots):
        z = jnp.bitwise_xor(spot, j)
        for block, side in ((mine, core), (other, away)):
            copies.append((block.at[pl.ds(2 * half + j * piece, piece)], there.at[pl.ds(side * half + z * piece, piece)]))
    copies = [pltpu.make_async_copy(source, target, sems.at[j]) for j, (source, target) in enumerate(copies)]
    for copy in copies:
        copy.start()
    for copy in copies:
        copy.wait()


def spread_weights(plan, scalars, *arrays):
    hbm = pl.BlockSpec(memory_space=pl.ANY)
    return pl.pallas_call(
        functools.partial(spread_kernel, plan),
        grid_spec=pltpu.PrefetchScalarGridSpec(
            num_scalar_prefetch=1, grid=(1,), in_specs=[hbm] * 3,
            out_specs=pl.BlockSpec(memory_space=pltpu.VMEM),
            scratch_shapes=[pltpu.SemaphoreType.DMA((5 + 2 * plan.spots,))],
        ),
        out_shape=jax.ShapeDtypeStruct((SECTIONS, plan.packed, plan.width), BF),
        compiler_params=pltpu.CompilerParams(vmem_limit_bytes=plan.grant(SMALL_VMEM)),
        cost_estimate=pl.CostEstimate(flops=0, bytes_accessed=16 * plan.packed * plan.width, transcendentals=0),
    )(scalars, *arrays)


def grads_kernel(plan, latent, sc, mine, other, dir_first, gain_first, dir_second, gain_second, latents, cell_shape,
                 first_out, first_gain, first_bias, second_out, second_gain, second_bias, cells):
    core, spot = sc[1], sc[2]
    width, share, room, piece = plan.width, plan.share, plan.room, plan.piece
    for source, side in ((mine, core), (other, 1 - core)):
        for j in range(plan.spots):
            p = side * plan.spots + jnp.bitwise_xor(spot, j)
            base = j * piece
            rows = pl.ds(pl.multiple_of(p * share, share), share)
            second_out[rows, :] = source[base : base + share, :].astype(F32)
            first_out[rows, :] = source[base + share : base + 2 * share, :].astype(F32)
            rows = pl.ds(pl.multiple_of(p * room, room), room)
            cells[rows, :] = source[base + 2 * share : base + piece, :].astype(F32)
    by_cell = cells[...]
    shaped = jnp.where(cell_shape[...] >= 0, by_cell, 0.0)
    first_bias[...] = jnp.sum(shaped, axis=0, keepdims=True)
    shape = lax.broadcasted_iota(jnp.int32, (plan.cells, plan.shapes), 1)
    onehot = jnp.where(cell_shape[...] == shape, 1.0, 0.0).astype(BF)
    by_shape = mm(onehot, latents[...]).astype(BF)
    first_out[width : width + latent, :] = mm(by_shape, shaped.astype(BF), TN)
    for j in range(plan.coords):
        spot_row = plan.special(j)
        first_out[width + latent + j : width + latent + j + 1, :] = cells[spot_row : spot_row + 1, :]
    spot_row = plan.special(plan.coords)
    second_bias[...] = cells[spot_row : spot_row + 1, :]
    for direction, gain, out, gain_out in ((dir_first, gain_first, first_out, first_gain),
                                           (dir_second, gain_second, second_out, second_gain)):
        values = direction[...].astype(F32)
        summed = out[...]
        norm = jnp.sqrt(jnp.sum(values * values, axis=0, keepdims=True) + 1e-06)
        along = jnp.sum(values * summed, axis=0, keepdims=True)
        gain_out[...] = along / norm
        scale = gain[...].astype(F32) / norm
        out[...] = scale * summed - (scale * along / (norm * norm)) * values


def finish_grads(plan, scalars, mine, other, dir_first, gain_first, dir_second, gain_second, latents, cell_shape):
    width = plan.width
    vmem = pl.BlockSpec(memory_space=pltpu.VMEM)
    row = jax.ShapeDtypeStruct((1, width), F32)
    whole = lambda like: jax.ShapeDtypeStruct(like.shape, F32)
    return pl.pallas_call(
        functools.partial(grads_kernel, plan, latents.shape[1]),
        grid_spec=pltpu.PrefetchScalarGridSpec(
            num_scalar_prefetch=1, grid=(1,), in_specs=[vmem] * 8, out_specs=[vmem] * 6,
            scratch_shapes=[pltpu.VMEM((plan.cells, width), F32)],
        ),
        out_shape=[whole(dir_first), row, row, whole(dir_second), row, row],
        compiler_params=pltpu.CompilerParams(vmem_limit_bytes=plan.grant(SMALL_VMEM)),
        cost_estimate=pl.CostEstimate(flops=2 * plan.cells * width * latents.shape[1],
                                      bytes_accessed=8 * plan.packed * width, transcendentals=0),
    )(scalars, mine, other, dir_first, gain_first, dir_second, gain_second, latents, cell_shape)


def swap_section(block, distance):
    route = [(i, i ^ distance) for i in range(lax.axis_size("section"))]
    return lax.ppermute(block, "section", route)


def swap_dp(block, distance):
    route = [(i, i ^ distance) for i in range(lax.axis_size("dp"))]
    return lax.ppermute(block, "dp", route)


def cut(array, first, count):
    return lax.dynamic_slice_in_dim(array, first, count, 0)


def reduce_pieces(plan, chip, spot):
    piece = plan.piece
    total = cut(chip, spot * piece, piece).astype(F32)
    for distance in range(plan.spots - 1, 0, -1):
        away = jnp.bitwise_xor(spot, distance)
        total = total + swap_dp(cut(chip, away * piece, piece), 2 * distance).astype(F32)
    return total.astype(BF)


def gather_chips(plan, piece):
    got = [swap_dp(piece, 2 * distance) for distance in range(plan.spots - 1, 0, -1)]
    return [piece] + got[::-1]


def shards(
    inputs, cotangent, latent_codes, positions, shape_ids,
    direction_first, gain_first, bias_first, direction_second, gain_second, bias_second,
):
    section = lax.axis_index("section")
    dp_rank = lax.axis_index("dp")
    core, spot = dp_rank % 2, dp_rank // 2
    total, width = inputs.shape
    shapes, latent = latent_codes.shape
    coords = positions.shape[0]
    plan = Plan(width, coords, shapes, lax.axis_size("dp"))
    cell_shape = jnp.asarray(plan.cell_shape)
    place = jnp.stack([section, core, spot]).astype(jnp.int32)

    packed, skip, sending, far = pack_weights(
        plan, latent_codes, cell_shape,
        direction_first[0], gain_first, bias_first, direction_second[0], gain_second, bias_second,
    )
    far = swap_section(far, 3)
    sending, far = lax.optimization_barrier((sending, far))
    x_mine = swap_section(sending, 1)
    y_mine = swap_section(sending, 2)
    far_mine = gather_chips(plan, far)
    mine = join(plan, [x_mine, y_mine, *far_mine])
    weights = spread_weights(plan, place, packed, mine, swap_dp(mine, 1))

    blocks = total // ROWS
    ids = shape_ids.reshape(blocks, 1, ROWS)
    places = positions.reshape(coords, blocks, ROWS).transpose(1, 0, 2)
    same = (inputs, cotangent, ids, places, cell_shape, weights)
    given, parts, into, starts = [], [], [], []
    done = 0
    for steps in CALLS:
        *into, give_x, give_y, after_first, mine, theirs = run_blocks(
            plan, done, place, *same, into, (steps,), []
        )
        given.append((swap_section(give_x, 1), swap_section(give_y, 2), after_first))
        parts.append((mine, theirs))
        starts.append(done)
        done += steps
    for calls in HELPED_CALLS:
        sources = [source for call in calls for source in given[call]]
        counts = tuple(CALLS[call] for call in calls)
        *into, mine, theirs = run_blocks(plan, starts[calls[0]], place, *same, into, counts, sources)
        parts.append((mine, theirs))
    act, ig = into

    mine, theirs = (sum(part.astype(F32) for part in side) for side in zip(*parts))
    chip = (mine + swap_dp(theirs.astype(BF), 1).astype(F32)).astype(BF)
    piece = reduce_pieces(plan, chip, spot)
    pieces = gather_chips(plan, piece)
    ready, pieces[1] = lax.optimization_barrier((piece, pieces[1]))
    owned = mm(ready[2 * plan.share : 2 * plan.share + plan.owned], skip, NT)
    code = cut(owned, section * plan.per, plan.per)
    for distance in range(1, SECTIONS):
        away = jnp.bitwise_xor(section, distance)
        code = code + swap_section(cut(owned, away * plan.per, plan.per), distance)
    mine = join(plan, pieces)
    mine, code = lax.optimization_barrier((mine, code))
    other = swap_dp(mine, 1)
    first, first_gain, first_bias, second, second_gain, second_bias = finish_grads(
        plan, place, mine, other, direction_first[0], gain_first, direction_second[0], gain_second,
        latent_codes, cell_shape,
    )
    return (
        act[None], ig[None], code, first[None], first_gain, first_bias, second[None], second_gain, second_bias,
    )


def solution(mesh):
    in_specs = (
        P("dp", None), P("dp", None), P(), P(None, "dp"), P("dp"),
        P("section", None, None), P("section", None), P("section", None),
        P("section", None, None), P("section", None), P("section", None),
    )
    out_specs = (
        P("section", "dp", None), P("section", "dp", None), P(("section", "dp"), None),
        P("section", None, None), P("section", None), P("section", None),
        P("section", None, None), P("section", None), P("section", None),
    )
    return jax.shard_map(shards, mesh=mesh, in_specs=in_specs, out_specs=out_specs, check_vma=False)
```

```python
import functools

import jax
import jax.numpy as jnp
import numpy as np
from jax import lax
from jax.experimental import pallas as pl
from jax.experimental.pallas import tpu as pltpu
from jax.sharding import PartitionSpec as P

BF = jnp.bfloat16
F32 = jnp.float32
NT = (((1,), (1,)), ((), ()))
TN = (((0,), (0,)), ((), ()))
SECTIONS = 4
ROWS = 768
CALLS = (3, 2)
HELPED_CALLS = ((0,), (1,))
VMEM = 36 * 2**20
SMALL_VMEM = 12 * 2**20
ALL_VMEM = 63 * 2**20
GIVE_X = (7, 6, 3, 8)
GIVE_Y = (8, 3, 6, 7)


def up(value, step):
    return -(-value // step) * step


def mm(left, right, dims=(((1,), (0,)), ((), ()))):
    return lax.dot_general(left, right, dims, preferred_element_type=F32)


def silu_parts(half):
    lift = 1.0 + jnp.tanh(half)
    out = (half * lift).astype(BF)
    lift = lift.astype(BF)
    return out, lift + out * (BF(2.0) - lift)


def stream(count, *stages):
    values = [None] * count
    for tick in range(count + len(stages) - 1):
        for j, stage in enumerate(stages):
            i = tick - j
            if 0 <= i < count:
                values[i] = stage(i, values[i])


class Plan:
    def __init__(self, width, coords, shapes, devices):
        self.width, self.coords, self.shapes, self.devices = width, coords, shapes, devices
        self.spots = devices // 2
        self.share = width // devices
        self.owned = shapes // devices
        self.per = self.owned // SECTIONS
        self.room = up(self.owned + 1, 16)
        self.cells = self.room * devices
        self.piece = 2 * self.share + self.room
        self.half = self.piece * self.spots
        self.packed = 2 * self.half
        table = np.full((self.cells, 1), -1, np.int32)
        for p in range(devices):
            place = 2 * (p % self.spots) + p // self.spots
            for j in range(self.owned):
                table[p * self.room + j, 0] = ((j // self.per) * devices + place) * self.per + j % self.per
        self.cell_shape = table

    def grant(self, base):
        return base + max(0, self.cells - 128) * 12288

    def special(self, j):
        return j * self.room + self.owned


class Block:
    def __init__(self, plan, weights, ext, subs):
        self.width, self.plan, self.weights, self.ext, self.subs = plan.width, plan, weights, ext, subs

    def first(self, k):
        return self.weights[k, : self.width, :]

    def second(self, k):
        return self.weights[k, self.width : 2 * self.width, :]

    def inner(self, k, source):
        beside = self.weights[k, 2 * self.width :, :]
        return lambda i, unused: mm(source(i), self.first(k)) + mm(self.ext[self.subs[i], :], beside)

    def outer(self, k):
        begin = 2 * self.width + self.plan.coords * self.plan.room
        spot = self.plan.owned
        offset = self.weights[k, begin : begin + self.plan.room, :].astype(F32)[spot : spot + 1]
        return lambda i, active: mm(active, self.second(k)) + offset

    def back_second(self, k, grads):
        return lambda i, unused: mm(grads(i), self.second(k), NT)

    def back_first(self, k):
        return lambda i, grads: mm(grads, self.first(k), NT)


def place_cells(point, places, cell_shape, plan, ext, ext_turned):
    rows = ext.shape[0]
    hit = jnp.where(cell_shape[...] == jnp.broadcast_to(point[...], (plan.cells, rows)), 1.0, 0.0)
    cell = lax.broadcasted_iota(jnp.int32, (plan.cells, rows), 0)
    for j in range(plan.coords):
        hit = jnp.where(cell == plan.special(j), places[j : j + 1, :].astype(F32), hit)
    ext_turned[...] = hit.astype(BF)
    ext[...] = hit.T.astype(BF)


def add_weight_grads(accs, active, outer_grad, entering, inner_grad, ext_turned):
    first, second, cell, bias = accs
    second[...] += mm(active, outer_grad, TN)
    first[...] += mm(entering, inner_grad, TN)
    cell[...] += mm(ext_turned[...], inner_grad)
    bias[...] += jnp.sum(outer_grad.astype(F32).reshape(-1, 8, outer_grad.shape[1]), axis=0)


def store_weight_grads(accs, plan, core, mine, theirs):
    first, second, cell, bias = accs
    share, room = plan.share, plan.room
    last = jnp.sum(bias[...], axis=0, keepdims=True)
    row = lax.broadcasted_iota(jnp.int32, cell.shape, 0)
    cell[...] = jnp.where(row == plan.special(plan.coords), last, cell[...])
    for side in range(2):
        @pl.when(core == side)
        def _(side=side):
            for p in range(plan.devices):
                out = mine if p // plan.spots == side else theirs
                at = (p % plan.spots) * plan.piece
                out[at : at + share, :] = second[p * share : (p + 1) * share, :].astype(BF)
                out[at + share : at + 2 * share, :] = first[p * share : (p + 1) * share, :].astype(BF)
                out[at + 2 * share : at + plan.piece, :] = cell[p * room : (p + 1) * room, :].astype(BF)


def pick(section, choices):
    found = jnp.int32(choices[0])
    for k in range(1, SECTIONS):
        found = jnp.where(section == k, choices[k], found)
    return found


def self_half(section, blocks):
    return jnp.where((section == 0) | (section == SECTIONS - 1), 0, blocks // 2)


def self_kernel(
    plan, steps, aliased, sc, h_in, g_in, ids, places, other_h, other_ids, other_places, cell_shape, weights, *refs
):
    act, ig, give_x, give_y, after_first, mine, theirs, ext, ext_turned, states, mids, slope1, slope2, *accs = refs[aliased:]
    section, core = sc[0], sc[1]
    step = pl.program_id(0)
    rows = h_in.shape[0]
    half = rows // 2
    subs = [pl.ds(0, half), pl.ds(half, half)]
    do = Block(plan, weights, ext, subs)

    @pl.when(step == 0)
    def _():
        for acc in accs:
            acc[...] = jnp.zeros_like(acc)

    @pl.when(section == 2)
    def _():
        place_cells(other_ids, other_places, cell_shape, plan, ext, ext_turned)

        def keep(i, z):
            after_first[pl.ds(pl.multiple_of(step * rows + i * half, 128), half), :] = silu_parts(z)[0]
        stream(2, do.inner(0, lambda i: other_h[subs[i], :]), lambda i, z: silu_parts(z)[0], do.outer(0), keep)

    place_cells(ids, places, cell_shape, plan, ext, ext_turned)
    states[0] = h_in[...]

    def keep_active(k):
        def stage(i, z):
            active, slope = silu_parts(z)
            mids[k, subs[i], :] = active
            slope1[k, subs[i], :] = slope
            return active
        return stage

    def keep_state(k):
        def stage(i, z):
            after, slope = silu_parts(z)
            states[k + 1, subs[i], :] = after
            if k == SECTIONS - 1:
                slope = slope * (g_in[subs[i], :] * BF(0.5))
            slope2[k, subs[i], :] = slope
        return stage

    def inner_grad(k):
        def stage(i, grads):
            grads = (grads * slope1[k, subs[i], :].astype(F32)).astype(BF)
            slope1[k, subs[i], :] = grads
            return grads
        return stage

    def enter_grad(k, below):
        def stage(i, grads):
            grads = grads.astype(BF)
            states[5 + k, subs[i], :] = grads
            if below is not None:
                slope2[below, subs[i], :] = grads * slope2[below, subs[i], :]
        return stage

    def back(k, below):
        return [do.back_second(k, lambda i: slope2[k, subs[i], :]), inner_grad(k), do.back_first(k),
                enter_grad(k, below)]

    top = SECTIONS - 1
    stages = []
    for k in range(SECTIONS):
        source = (lambda i: h_in[subs[i], :]) if k == 0 else (lambda i, k=k: states[k, subs[i], :])
        stages += [do.inner(k, source), keep_active(k), do.outer(k), keep_state(k)]
    stream(2, *stages, *back(top, top - 1))

    def lower(j, unused):
        k = top - 1 - j
        stream(2, *back(k, jnp.where(k > 0, k - 1, SECTIONS)))
        return 0

    lax.fori_loop(0, top - section, lower, 0)

    @pl.when(section >= 2)
    def _():
        value = None
        for stage in back(section - 1, None):
            value = stage(1, value)

    act[...] = states[section + 1]
    ig[...] = states[5 + section] * BF(2.0)
    given = pl.ds(pl.multiple_of(step * half, 128), half)
    give_x[given, :] = states[pick(section, GIVE_X), subs[0], :]
    give_y[given, :] = states[pick(section, GIVE_Y), subs[1], :]
    add_weight_grads(accs, mids[section], slope2[section], states[section], slope1[section], ext_turned)

    @pl.when(step == steps - 1)
    def _():
        store_weight_grads(accs, plan, core, mine, theirs)


def helped_kernel(
    plan, steps, counts, sc, h_in, g_in, ids, places, cell_shape, weights, *refs
):
    sources, refs = refs[: 3 * len(counts)], refs[3 * len(counts) + 2 :]
    act, ig, mine, theirs, ext, ext_turned, entering, got, mid, slope1, slope2, *accs = refs
    section, core = sc[0], sc[1]
    step = pl.program_id(0)
    rows = h_in.shape[0]
    half = rows // 2
    subs = [pl.ds(0, half), pl.ds(half, half)]
    do = Block(plan, weights, ext, subs)

    @pl.when(step == 0)
    def _():
        for acc in accs:
            acc[...] = jnp.zeros_like(acc)

    place_cells(ids, places, cell_shape, plan, ext, ext_turned)
    top = section == SECTIONS - 1
    begin = 0
    for j, count in enumerate(counts):
        got_x, got_y, after_first = sources[3 * j : 3 * j + 3]
        now = (step >= begin) & (step < begin + count)
        begin += count

        @pl.when(now)
        def _():
            got[subs[0], :] = got_x[...]
            got[subs[1], :] = got_y[...]

        @pl.when(now & (section == 2))
        def _():
            entering[...] = after_first[...]

    @pl.when(section <= 1)
    def _():
        entering[...] = h_in[...]

    @pl.when(top)
    def _():
        entering[...] = got[...]
        got[...] = g_in[...] * BF(0.5)

    def active_only(i, z):
        return silu_parts(z)[0]

    def enter(i, z):
        entering[subs[i], :] = silu_parts(z)[0]

    def keep_active(i, z):
        active, slope = silu_parts(z)
        mid[subs[i], :] = active
        slope1[subs[i], :] = slope
        return active

    def keep_own(i, z):
        after, slope = silu_parts(z)
        act[subs[i], :] = after
        grads = slope * got[subs[i], :]
        slope2[subs[i], :] = grads
        return grads

    def inner_grad(i, grads):
        grads = (grads * slope1[subs[i], :].astype(F32)).astype(BF)
        slope1[subs[i], :] = grads
        return grads

    def enter_grad(i, grads):
        ig[subs[i], :] = (2.0 * grads).astype(BF)

    def source(i):
        return entering[subs[i], :]

    @pl.when((section == 1) | (section == 2))
    def _():
        stream(2, do.inner(section - 1, source), active_only, do.outer(section - 1), enter)

    stream(2, do.inner(section, source), keep_active, do.outer(section), keep_own,
           do.back_second(section, lambda i: slope2[subs[i], :]), inner_grad, do.back_first(section), enter_grad)
    add_weight_grads(accs, mid[...], slope2[...], entering[...], slope1[...], ext_turned)

    @pl.when(step == steps - 1)
    def _():
        store_weight_grads(accs, plan, core, mine, theirs)


def run_blocks(plan, done, place, h, g, ids, places, cell_shape, weights, into, counts, sources):
    total, width = h.shape
    blocks = total // ROWS
    helped = len(sources) > 0
    steps = sum(counts)

    def here(i, sc):
        start = self_half(sc[0], blocks)
        return (blocks // 2 - start if helped else start) + done + i

    def there(i, sc):
        return jnp.where(sc[0] == 2, blocks // 2 - self_half(sc[0], blocks) + done + i, 0)

    def block_specs(where):
        return [
            pl.BlockSpec((None, 1, ROWS), lambda i, sc: (where(i, sc), 0, 0)),
            pl.BlockSpec((None, plan.coords, ROWS), lambda i, sc: (where(i, sc), 0, 0)),
        ]

    rows = pl.BlockSpec((ROWS, width), lambda i, sc: (here(i, sc), 0))
    other_rows = pl.BlockSpec((ROWS, width), lambda i, sc: (there(i, sc), 0))
    hbm = pl.BlockSpec(memory_space=pl.ANY)
    vmem = pl.BlockSpec(memory_space=pltpu.VMEM)
    array = lambda count: jax.ShapeDtypeStruct((count, width), BF)
    block = lambda *lead: pltpu.VMEM((*lead, ROWS, width), BF)
    scratch = [pltpu.VMEM((ROWS, plan.cells), BF), pltpu.VMEM((plan.cells, ROWS), BF)]
    if helped:
        kernel = functools.partial(helped_kernel, plan, steps, counts)
        out_shape = [array(total)] * 2 + [array(plan.half)] * 2
        out_specs = [rows, rows, vmem, vmem]
        scratch += [block()] * 5
        source_specs, begin = [], 0
        for count in counts:
            at = lambda i, sc, begin=begin, count=count: (jnp.clip(i - begin, 0, count - 1), 0)
            half_rows = pl.BlockSpec((ROWS // 2, width), at)
            source_specs += [half_rows, half_rows, pl.BlockSpec((ROWS, width), at)]
            begin += count
        operands = [h, g, ids, places, cell_shape, weights, *sources, *into]
        in_specs = [rows, rows, *block_specs(here), vmem, vmem, *source_specs, hbm, hbm]
        units = 8
    else:
        kernel = functools.partial(self_kernel, plan, steps, len(into))
        out_shape = ([array(total)] * 2 + [array(steps * ROWS // 2)] * 2 + [array(steps * ROWS)]
                     + [array(plan.half)] * 2)
        out_specs = [rows, rows, *[vmem] * 5]
        scratch += [block(10), block(SECTIONS), block(SECTIONS), block(SECTIONS + 1)]
        operands = [h, g, ids, places, h, ids, places, cell_shape, weights, *into]
        in_specs = [rows, rows, *block_specs(here), other_rows, *block_specs(there), vmem, vmem, *[hbm] * len(into)]
        units = 21
    scratch += [pltpu.VMEM((width, width), F32), pltpu.VMEM((width, width), F32),
                pltpu.VMEM((plan.cells, width), F32), pltpu.VMEM((8, width), F32)]
    first_into = 1 + len(operands) - len(into)
    return pl.pallas_call(
        kernel,
        grid_spec=pltpu.PrefetchScalarGridSpec(
            num_scalar_prefetch=1, grid=(steps,), in_specs=in_specs, out_specs=out_specs, scratch_shapes=scratch,
        ),
        out_shape=out_shape,
        input_output_aliases={first_into + j: j for j in range(len(into))},
        compiler_params=pltpu.CompilerParams(vmem_limit_bytes=plan.grant(VMEM)),
        cost_estimate=pl.CostEstimate(
            flops=2 * steps * ROWS * width * width * units, bytes_accessed=steps * ROWS * width * 12,
            transcendentals=steps * ROWS * width * 8,
        ),
    )(place, *operands)


def normed(direction, gain_row):
    scale = gain_row / jnp.sqrt(jnp.sum(direction * direction, axis=0, keepdims=True) + 1e-06)
    return (direction * scale).astype(BF)


def pack_kernel(plan, latent, *refs):
    sources, (packed, skip, side, far), held, sems = refs[:8], refs[8:12], refs[12:20], refs[20]
    copies = [pltpu.make_async_copy(s, h, sems.at[j]) for j, (s, h) in enumerate(zip(sources, held))]
    for copy in copies:
        copy.start()
    for copy in copies:
        copy.wait()
    dir_first, gain_first, bias_first, dir_second, gain_second, bias_second, latents, cell_shape = held
    width = plan.width
    half = BF(0.5)
    first = normed(dir_first[...].astype(F32), gain_first[...].astype(F32))
    second = normed(dir_second[...].astype(F32), gain_second[...].astype(F32))
    packed[:width, :] = first[:width] * half
    packed[width : 2 * width, :] = second * half
    skip[...] = first[width : width + latent]
    shape = lax.broadcasted_iota(jnp.int32, (plan.cells, plan.shapes), 1)
    onehot = jnp.where(cell_shape[...] == shape, 1.0, 0.0).astype(BF)
    by_cell = mm(onehot, latents[...]).astype(BF)
    by_cell = mm(by_cell, skip[...])
    by_cell = 0.5 * jnp.where(cell_shape[...] >= 0, by_cell + bias_first[...].astype(F32), 0.0)
    cell = lax.broadcasted_iota(jnp.int32, by_cell.shape, 0)
    tail = 0.5 * first[width + latent :].astype(F32)
    for j in range(plan.coords):
        by_cell = jnp.where(cell == plan.special(j), tail[j : j + 1], by_cell)
    by_cell = jnp.where(cell == plan.special(plan.coords), 0.5 * bias_second[...].astype(F32), by_cell)
    packed[2 * width :, :] = by_cell.astype(BF)
    place = lax.axis_index("dp")
    begin = lax.rem(place, 2) * plan.half
    side[...] = packed[pl.ds(pl.multiple_of(begin, 16), plan.half), :]
    far[...] = packed[pl.ds(pl.multiple_of(begin + lax.div(place, 2) * plan.piece, 16), plan.piece), :]


def pack_weights(plan, latents, cell_shape, *own):
    width = plan.width
    latent = latents.shape[1]
    vmem = pl.BlockSpec(memory_space=pltpu.VMEM)
    return pl.pallas_call(
        functools.partial(pack_kernel, plan, latent),
        in_specs=[pl.BlockSpec(memory_space=pl.ANY)] * 8,
        out_specs=[vmem] * 4,
        scratch_shapes=[pltpu.VMEM(array.shape, array.dtype) for array in (*own, latents, cell_shape)]
        + [pltpu.SemaphoreType.DMA((8,))],
        out_shape=[jax.ShapeDtypeStruct((rows, width), BF) for rows in (plan.packed, latent, plan.half, plan.piece)],
        compiler_params=pltpu.CompilerParams(vmem_limit_bytes=ALL_VMEM),
        cost_estimate=pl.CostEstimate(flops=2 * plan.cells * width * latent, bytes_accessed=4 * plan.packed * width,
                                      transcendentals=0),
    )(*own, latents, cell_shape)


def join_kernel(count, *refs):
    sources, out, sems = refs[:count], refs[count], refs[count + 1]
    copies, row = [], 0
    for j, source in enumerate(sources):
        copies.append(pltpu.make_async_copy(source, out.at[pl.ds(row, source.shape[0])], sems.at[j]))
        row += source.shape[0]
    for copy in copies:
        copy.start()
    for copy in copies:
        copy.wait()


def join(plan, arrays):
    rows = sum(array.shape[0] for array in arrays)
    return pl.pallas_call(
        functools.partial(join_kernel, len(arrays)),
        in_specs=[pl.BlockSpec(memory_space=pl.ANY)] * len(arrays),
        out_specs=pl.BlockSpec(memory_space=pltpu.VMEM),
        scratch_shapes=[pltpu.SemaphoreType.DMA((len(arrays),))],
        out_shape=jax.ShapeDtypeStruct((rows, arrays[0].shape[1]), arrays[0].dtype),
        compiler_params=pltpu.CompilerParams(vmem_limit_bytes=plan.grant(SMALL_VMEM)),
        cost_estimate=pl.CostEstimate(flops=0, bytes_accessed=4 * rows * arrays[0].shape[1], transcendentals=0),
    )(*arrays)


def spread_kernel(plan, near, sc, *refs):
    section, core, spot = sc[0], sc[1], sc[2]
    half, piece = plan.half, plan.piece
    first, block, weights, sems = refs
    side = core if near else 1 - core
    copies = [(first, weights.at[section])] if near else []
    for j in range(2):
        there = weights.at[jnp.bitwise_xor(section, j + 1)]
        copies.append((block.at[pl.ds(j * half, half)], there.at[pl.ds(side * half, half)]))
    there = weights.at[jnp.bitwise_xor(section, 3)]
    for j in range(plan.spots):
        z = jnp.bitwise_xor(spot, j)
        copies.append((block.at[pl.ds(2 * half + j * piece, piece)], there.at[pl.ds(side * half + z * piece, piece)]))
    copies = [pltpu.make_async_copy(source, target, sems.at[j]) for j, (source, target) in enumerate(copies)]
    for copy in copies:
        copy.start()
    for copy in copies:
        copy.wait()


def spread_weights(plan, near, scalars, first, block):
    hbm = pl.BlockSpec(memory_space=pl.ANY)
    vmem = pl.BlockSpec(memory_space=pltpu.VMEM)
    return pl.pallas_call(
        functools.partial(spread_kernel, plan, near),
        grid_spec=pltpu.PrefetchScalarGridSpec(
            num_scalar_prefetch=1, grid=(1,), in_specs=[hbm if near else vmem, hbm], out_specs=vmem,
            scratch_shapes=[pltpu.SemaphoreType.DMA((3 + plan.spots,))],
        ),
        out_shape=jax.ShapeDtypeStruct((SECTIONS, plan.packed, plan.width), BF),
        input_output_aliases={} if near else {1: 0},
        compiler_params=pltpu.CompilerParams(vmem_limit_bytes=plan.grant(SMALL_VMEM)),
        cost_estimate=pl.CostEstimate(flops=0, bytes_accessed=8 * plan.packed * plan.width, transcendentals=0),
    )(scalars, first, block)


def grads_kernel(plan, latent, sc, mine, other, dir_first, gain_first, dir_second, gain_second, latents, cell_shape,
                 first_rows, first_gain, first_bias, second_out, second_gain, second_bias, cells, first_out):
    core, spot = sc[1], sc[2]
    width, share, room, piece = plan.width, plan.share, plan.room, plan.piece
    for source, side in ((mine, core), (other, 1 - core)):
        for j in range(plan.spots):
            p = side * plan.spots + jnp.bitwise_xor(spot, j)
            base = j * piece
            rows = pl.ds(pl.multiple_of(p * share, share), share)
            second_out[rows, :] = source[base : base + share, :].astype(F32)
            first_out[rows, :] = source[base + share : base + 2 * share, :].astype(F32)
            rows = pl.ds(pl.multiple_of(p * room, room), room)
            cells[rows, :] = source[base + 2 * share : base + piece, :].astype(F32)
    by_cell = cells[...]
    shaped = jnp.where(cell_shape[...] >= 0, by_cell, 0.0)
    first_bias[...] = jnp.sum(shaped, axis=0, keepdims=True)
    shape = lax.broadcasted_iota(jnp.int32, (plan.cells, plan.shapes), 1)
    onehot = jnp.where(cell_shape[...] == shape, 1.0, 0.0).astype(BF)
    by_shape = mm(onehot, latents[...]).astype(BF)
    first_out[width : width + latent, :] = mm(by_shape, shaped.astype(BF), TN)
    for j in range(plan.coords):
        spot_row = plan.special(j)
        first_out[width + latent + j : width + latent + j + 1, :] = cells[spot_row : spot_row + 1, :]
    spot_row = plan.special(plan.coords)
    second_bias[...] = cells[spot_row : spot_row + 1, :]
    for direction, gain, out, gain_out in ((dir_first, gain_first, first_out, first_gain),
                                           (dir_second, gain_second, second_out, second_gain)):
        values = direction[...].astype(F32)
        summed = out[...]
        norm = jnp.sqrt(jnp.sum(values * values, axis=0, keepdims=True) + 1e-06)
        along = jnp.sum(values * summed, axis=0, keepdims=True)
        gain_out[...] = along / norm
        scale = gain[...].astype(F32) / norm
        result = scale * summed - (scale * along / (norm * norm)) * values
        if out is first_out:
            for j in range(first_rows.shape[1]):
                first_rows[:, j, :] = result[:, j * 128 : (j + 1) * 128]
        else:
            out[...] = result


def finish_grads(plan, scalars, mine, other, dir_first, gain_first, dir_second, gain_second, latents, cell_shape):
    width = plan.width
    vmem = pl.BlockSpec(memory_space=pltpu.VMEM)
    row = jax.ShapeDtypeStruct((1, width), F32)
    whole = lambda like: jax.ShapeDtypeStruct(like.shape, F32)
    return pl.pallas_call(
        functools.partial(grads_kernel, plan, latents.shape[1]),
        grid_spec=pltpu.PrefetchScalarGridSpec(
            num_scalar_prefetch=1, grid=(1,), in_specs=[vmem] * 8, out_specs=[vmem] * 6,
            scratch_shapes=[pltpu.VMEM((plan.cells, width), F32), pltpu.VMEM(dir_first.shape, F32)],
        ),
        out_shape=[jax.ShapeDtypeStruct((dir_first.shape[0], width // 128, 128), F32), row, row, whole(dir_second), row, row],
        compiler_params=pltpu.CompilerParams(vmem_limit_bytes=plan.grant(SMALL_VMEM)),
        cost_estimate=pl.CostEstimate(flops=2 * plan.cells * width * latents.shape[1],
                                      bytes_accessed=8 * plan.packed * width, transcendentals=0),
    )(scalars, mine, other, dir_first, gain_first, dir_second, gain_second, latents, cell_shape)


def swap_section(block, distance):
    route = [(i, i ^ distance) for i in range(lax.axis_size("section"))]
    return lax.ppermute(block, "section", route)


def swap_dp(block, distance):
    route = [(i, i ^ distance) for i in range(lax.axis_size("dp"))]
    return lax.ppermute(block, "dp", route)


def cut(array, first, count):
    return lax.dynamic_slice_in_dim(array, first, count, 0)


def reduce_pieces(plan, chip, spot):
    piece = plan.piece
    total = cut(chip, spot * piece, piece).astype(F32)
    for distance in range(plan.spots - 1, 0, -1):
        away = jnp.bitwise_xor(spot, distance)
        total = total + swap_dp(cut(chip, away * piece, piece), 2 * distance).astype(F32)
    return total.astype(BF)


def gather_chips(plan, piece):
    got = [swap_dp(piece, 2 * distance) for distance in range(plan.spots - 1, 0, -1)]
    return [piece] + got[::-1]


def shards(
    inputs, cotangent, latent_codes, positions, shape_ids,
    direction_first, gain_first, bias_first, direction_second, gain_second, bias_second,
):
    section = lax.axis_index("section")
    dp_rank = lax.axis_index("dp")
    core, spot = dp_rank % 2, dp_rank // 2
    total, width = inputs.shape
    shapes, latent = latent_codes.shape
    coords = positions.shape[0]
    plan = Plan(width, coords, shapes, lax.axis_size("dp"))
    cell_shape = jnp.asarray(plan.cell_shape)
    place = jnp.stack([section, core, spot]).astype(jnp.int32)

    packed, skip, sending, far = pack_weights(
        plan, latent_codes, cell_shape,
        direction_first[0], gain_first, bias_first, direction_second[0], gain_second, bias_second,
    )
    blocks = total // ROWS
    ids = shape_ids.reshape(blocks, 1, ROWS)
    places = positions.reshape(coords, blocks, ROWS).transpose(1, 0, 2)
    far = swap_section(far, 3)
    sending, far, ids, places, place = lax.optimization_barrier((sending, far, ids, places, place))
    x_mine = swap_section(sending, 1)
    y_mine = swap_section(sending, 2)
    far_mine = gather_chips(plan, far)
    mine = join(plan, [x_mine, y_mine, *far_mine])
    other = swap_dp(mine, 1)
    weights = spread_weights(plan, True, place, packed, mine)
    weights = spread_weights(plan, False, place, weights, other)

    same = (inputs, cotangent, ids, places, cell_shape, weights)
    given, parts, into, starts = [], [], [], []
    done = 0
    for steps in CALLS:
        *into, give_x, give_y, after_first, mine, theirs = run_blocks(
            plan, done, place, *same, into, (steps,), []
        )
        given.append((swap_section(give_x, 1), swap_section(give_y, 2), after_first))
        parts.append((mine, theirs))
        starts.append(done)
        done += steps
    for calls in HELPED_CALLS:
        sources = [source for call in calls for source in given[call]]
        counts = tuple(CALLS[call] for call in calls)
        *into, mine, theirs = run_blocks(plan, starts[calls[0]], place, *same, into, counts, sources)
        parts.append((mine, theirs))
    act, ig = into

    mine, theirs = (sum(part.astype(F32) for part in side) for side in zip(*parts))
    chip = (mine + swap_dp(theirs.astype(BF), 1).astype(F32)).astype(BF)
    piece = reduce_pieces(plan, chip, spot)
    pieces = gather_chips(plan, piece)
    ready, pieces[1] = lax.optimization_barrier((piece, pieces[1]))
    owned = mm(ready[2 * plan.share : 2 * plan.share + plan.owned], skip, NT)
    code = cut(owned, section * plan.per, plan.per)
    for distance in range(1, SECTIONS):
        away = jnp.bitwise_xor(section, distance)
        code = code + swap_section(cut(owned, away * plan.per, plan.per), distance)
    mine = join(plan, pieces)
    mine, code = lax.optimization_barrier((mine, code))
    other = swap_dp(mine, 1)
    first, first_gain, first_bias, second, second_gain, second_bias = finish_grads(
        plan, place, mine, other, direction_first[0], gain_first, direction_second[0], gain_second,
        latent_codes, cell_shape,
    )
    return (
        act[None], ig[None], code, first.reshape(direction_first.shape), first_gain, first_bias, second[None], second_gain, second_bias,
    )


def solution(mesh):
    in_specs = (
        P("dp", None), P("dp", None), P(), P(None, "dp"), P("dp"),
        P("section", None, None), P("section", None), P("section", None),
        P("section", None, None), P("section", None), P("section", None),
    )
    out_specs = (
        P("section", "dp", None), P("section", "dp", None), P(("section", "dp"), None),
        P("section", None, None), P("section", None), P("section", None),
        P("section", None, None), P("section", None), P("section", None),
    )
    return jax.shard_map(shards, mesh=mesh, in_specs=in_specs, out_specs=out_specs, check_vma=False)
```

```python
import functools

import jax
import jax.numpy as jnp
import numpy as np
from jax import lax
from jax.experimental import pallas as pl
from jax.experimental.pallas import tpu as pltpu
from jax.sharding import PartitionSpec as P

BF = jnp.bfloat16
F32 = jnp.float32
NT = (((1,), (1,)), ((), ()))
TN = (((0,), (0,)), ((), ()))
SECTIONS = 4
ROWS = 768
CALLS = (3, 2)
HELPED_CALLS = ((0,), (1,))
VMEM = 36 * 2**20
SMALL_VMEM = 12 * 2**20
ALL_VMEM = 63 * 2**20
GIVE_X = (7, 6, 3, 8)
GIVE_Y = (8, 3, 6, 7)


def up(value, step):
    return -(-value // step) * step


def mm(left, right, dims=(((1,), (0,)), ((), ()))):
    return lax.dot_general(left, right, dims, preferred_element_type=F32)


def silu_parts(half):
    lift = 1.0 + jnp.tanh(half)
    out = (half * lift).astype(BF)
    lift = lift.astype(BF)
    return out, lift + out * (BF(2.0) - lift)


def stream(count, *stages):
    values = [None] * count
    for tick in range(count + len(stages) - 1):
        for j, stage in enumerate(stages):
            i = tick - j
            if 0 <= i < count:
                values[i] = stage(i, values[i])


class Plan:
    def __init__(self, width, coords, shapes, devices):
        self.width, self.coords, self.shapes, self.devices = width, coords, shapes, devices
        self.spots = devices // 2
        self.share = width // devices
        self.owned = shapes // devices
        self.per = self.owned // SECTIONS
        self.room = up(self.owned + 1, 16)
        self.cells = self.room * devices
        self.piece = 2 * self.share + self.room
        self.half = self.piece * self.spots
        self.packed = 2 * self.half
        table = np.full((self.cells, 1), -1, np.int32)
        for p in range(devices):
            place = 2 * (p % self.spots) + p // self.spots
            for j in range(self.owned):
                table[p * self.room + j, 0] = ((j // self.per) * devices + place) * self.per + j % self.per
        self.cell_shape = table

    def grant(self, base):
        return base + max(0, self.cells - 128) * 12288

    def special(self, j):
        return j * self.room + self.owned


class Block:
    def __init__(self, plan, weights, ext, subs):
        self.width, self.plan, self.weights, self.ext, self.subs = plan.width, plan, weights, ext, subs

    def first(self, k):
        return self.weights[k, : self.width, :]

    def second(self, k):
        return self.weights[k, self.width : 2 * self.width, :]

    def inner(self, k, source):
        beside = self.weights[k, 2 * self.width :, :]
        return lambda i, unused: mm(source(i), self.first(k)) + mm(self.ext[self.subs[i], :], beside)

    def outer(self, k):
        begin = 2 * self.width + self.plan.coords * self.plan.room
        spot = self.plan.owned
        offset = self.weights[k, begin : begin + self.plan.room, :].astype(F32)[spot : spot + 1]
        return lambda i, active: mm(active, self.second(k)) + offset

    def back_second(self, k, grads):
        return lambda i, unused: mm(grads(i), self.second(k), NT)

    def back_first(self, k):
        return lambda i, grads: mm(grads, self.first(k), NT)


def place_cells(point, places, cell_shape, plan, ext, ext_turned):
    rows = ext.shape[0]
    hit = jnp.where(cell_shape[...] == jnp.broadcast_to(point[...], (plan.cells, rows)), 1.0, 0.0)
    cell = lax.broadcasted_iota(jnp.int32, (plan.cells, rows), 0)
    for j in range(plan.coords):
        hit = jnp.where(cell == plan.special(j), places[j : j + 1, :].astype(F32), hit)
    ext_turned[...] = hit.astype(BF)
    ext[...] = hit.T.astype(BF)


def add_weight_grads(accs, active, outer_grad, entering, inner_grad, ext_turned):
    first, second, cell, bias = accs
    second[...] += mm(active, outer_grad, TN)
    first[...] += mm(entering, inner_grad, TN)
    cell[...] += mm(ext_turned[...], inner_grad)
    bias[...] += jnp.sum(outer_grad.astype(F32).reshape(-1, 8, outer_grad.shape[1]), axis=0)


def store_weight_grads(accs, plan, core, mine, theirs):
    first, second, cell, bias = accs
    share, room = plan.share, plan.room
    last = jnp.sum(bias[...], axis=0, keepdims=True)
    row = lax.broadcasted_iota(jnp.int32, cell.shape, 0)
    cell[...] = jnp.where(row == plan.special(plan.coords), last, cell[...])
    for side in range(2):
        @pl.when(core == side)
        def _(side=side):
            for p in range(plan.devices):
                out = mine if p // plan.spots == side else theirs
                at = (p % plan.spots) * plan.piece
                out[at : at + share, :] = second[p * share : (p + 1) * share, :].astype(BF)
                out[at + share : at + 2 * share, :] = first[p * share : (p + 1) * share, :].astype(BF)
                out[at + 2 * share : at + plan.piece, :] = cell[p * room : (p + 1) * room, :].astype(BF)


def pick(section, choices):
    found = jnp.int32(choices[0])
    for k in range(1, SECTIONS):
        found = jnp.where(section == k, choices[k], found)
    return found


def self_half(section, blocks):
    return jnp.where((section == 0) | (section == SECTIONS - 1), 0, blocks // 2)


def self_kernel(
    plan, steps, deep, aliased, sc, h_in, g_in, ids, places, other_h, other_ids, other_places, cell_shape, weights, *refs
):
    act, ig, give_x, give_y, after_first, mine, theirs, ext, ext_turned, states, mids, slope1, slope2, *accs = refs[aliased:]
    section, core = sc[0], sc[1]
    step = pl.program_id(0)
    rows = h_in.shape[0]
    half = rows // 2
    subs = [pl.ds(0, half), pl.ds(half, half)]
    do = Block(plan, weights, ext, subs)

    @pl.when(step == 0)
    def _():
        for acc in accs:
            acc[...] = jnp.zeros_like(acc)

    other = lambda i: pl.ds(pl.multiple_of(step * rows + i * half, 128), half)

    def ahead(k, source):
        def keep(i, z):
            after_first[other(i), :] = silu_parts(z)[0]
        stream(2, do.inner(k, source), lambda i, z: silu_parts(z)[0], do.outer(k), keep)

    @pl.when((section == 2) | (section == 1) if deep else section == 2)
    def _():
        place_cells(other_ids, other_places, cell_shape, plan, ext, ext_turned)
        ahead(0, lambda i: other_h[subs[i], :])

    if deep:
        @pl.when(section == 2)
        def _():
            ahead(1, lambda i: after_first[other(i), :])

    place_cells(ids, places, cell_shape, plan, ext, ext_turned)
    states[0] = h_in[...]

    def keep_active(k):
        def stage(i, z):
            active, slope = silu_parts(z)
            mids[k, subs[i], :] = active
            slope1[k, subs[i], :] = slope
            return active
        return stage

    def keep_state(k):
        def stage(i, z):
            after, slope = silu_parts(z)
            states[k + 1, subs[i], :] = after
            if k == SECTIONS - 1:
                slope = slope * (g_in[subs[i], :] * BF(0.5))
            slope2[k, subs[i], :] = slope
        return stage

    def inner_grad(k):
        def stage(i, grads):
            grads = (grads * slope1[k, subs[i], :].astype(F32)).astype(BF)
            slope1[k, subs[i], :] = grads
            return grads
        return stage

    def enter_grad(k, below):
        def stage(i, grads):
            grads = grads.astype(BF)
            states[5 + k, subs[i], :] = grads
            if below is not None:
                slope2[below, subs[i], :] = grads * slope2[below, subs[i], :]
        return stage

    def back(k, below):
        return [do.back_second(k, lambda i: slope2[k, subs[i], :]), inner_grad(k), do.back_first(k),
                enter_grad(k, below)]

    top = SECTIONS - 1
    stages = []
    for k in range(SECTIONS):
        source = (lambda i: h_in[subs[i], :]) if k == 0 else (lambda i, k=k: states[k, subs[i], :])
        stages += [do.inner(k, source), keep_active(k), do.outer(k), keep_state(k)]
    stream(2, *stages, *back(top, top - 1))

    def lower(j, unused):
        k = top - 1 - j
        stream(2, *back(k, jnp.where(k > 0, k - 1, SECTIONS)))
        return 0

    lax.fori_loop(0, top - section, lower, 0)

    @pl.when(section >= 2)
    def _():
        value = None
        for stage in back(section - 1, None):
            value = stage(1, value)

    act[...] = states[section + 1]
    ig[...] = states[5 + section] * BF(2.0)
    given = pl.ds(pl.multiple_of(step * half, 128), half)
    give_x[given, :] = states[pick(section, GIVE_X), subs[0], :]
    give_y[given, :] = states[pick(section, GIVE_Y), subs[1], :]
    add_weight_grads(accs, mids[section], slope2[section], states[section], slope1[section], ext_turned)

    @pl.when(step == steps - 1)
    def _():
        store_weight_grads(accs, plan, core, mine, theirs)


def helped_kernel(
    plan, steps, deep, counts, sc, h_in, g_in, ids, places, cell_shape, weights, *refs
):
    sources, refs = refs[: 3 * len(counts)], refs[3 * len(counts) + 2 :]
    act, ig, mine, theirs, ext, ext_turned, entering, got, mid, slope1, slope2, *accs = refs
    section, core = sc[0], sc[1]
    step = pl.program_id(0)
    rows = h_in.shape[0]
    half = rows // 2
    subs = [pl.ds(0, half), pl.ds(half, half)]
    do = Block(plan, weights, ext, subs)

    @pl.when(step == 0)
    def _():
        for acc in accs:
            acc[...] = jnp.zeros_like(acc)

    place_cells(ids, places, cell_shape, plan, ext, ext_turned)
    top = section == SECTIONS - 1
    begin = 0
    for j, count in enumerate(counts):
        got_x, got_y, after_first = sources[3 * j : 3 * j + 3]
        now = (step >= begin) & (step < begin + count)
        begin += count

        @pl.when(now)
        def _():
            got[subs[0], :] = got_x[...]
            got[subs[1], :] = got_y[...]

        @pl.when(now & ((section == 2) | (section == 1) if deep else section == 2))
        def _():
            entering[...] = after_first[...]

    @pl.when((section == 0) if deep else (section <= 1))
    def _():
        entering[...] = h_in[...]

    @pl.when(top)
    def _():
        entering[...] = got[...]
        got[...] = g_in[...] * BF(0.5)

    def active_only(i, z):
        return silu_parts(z)[0]

    def enter(i, z):
        entering[subs[i], :] = silu_parts(z)[0]

    def keep_active(i, z):
        active, slope = silu_parts(z)
        mid[subs[i], :] = active
        slope1[subs[i], :] = slope
        return active

    def keep_own(i, z):
        after, slope = silu_parts(z)
        act[subs[i], :] = after
        grads = slope * got[subs[i], :]
        slope2[subs[i], :] = grads
        return grads

    def inner_grad(i, grads):
        grads = (grads * slope1[subs[i], :].astype(F32)).astype(BF)
        slope1[subs[i], :] = grads
        return grads

    def enter_grad(i, grads):
        ig[subs[i], :] = (2.0 * grads).astype(BF)

    def source(i):
        return entering[subs[i], :]

    if not deep:
        @pl.when((section == 1) | (section == 2))
        def _():
            stream(2, do.inner(section - 1, source), active_only, do.outer(section - 1), enter)

    stream(2, do.inner(section, source), keep_active, do.outer(section), keep_own,
           do.back_second(section, lambda i: slope2[subs[i], :]), inner_grad, do.back_first(section), enter_grad)
    add_weight_grads(accs, mid[...], slope2[...], entering[...], slope1[...], ext_turned)

    @pl.when(step == steps - 1)
    def _():
        store_weight_grads(accs, plan, core, mine, theirs)


def run_blocks(plan, deep, done, place, h, g, ids, places, cell_shape, weights, into, counts, sources):
    total, width = h.shape
    blocks = total // ROWS
    helped = len(sources) > 0
    steps = sum(counts)

    def here(i, sc):
        start = self_half(sc[0], blocks)
        return (blocks // 2 - start if helped else start) + done + i

    def there(i, sc):
        used = (sc[0] == 2) | (sc[0] == 1) if deep else sc[0] == 2
        return jnp.where(used, blocks // 2 - self_half(sc[0], blocks) + done + i, 0)

    def block_specs(where):
        return [
            pl.BlockSpec((None, 1, ROWS), lambda i, sc: (where(i, sc), 0, 0)),
            pl.BlockSpec((None, plan.coords, ROWS), lambda i, sc: (where(i, sc), 0, 0)),
        ]

    rows = pl.BlockSpec((ROWS, width), lambda i, sc: (here(i, sc), 0))
    other_rows = pl.BlockSpec((ROWS, width), lambda i, sc: (there(i, sc), 0))
    hbm = pl.BlockSpec(memory_space=pl.ANY)
    vmem = pl.BlockSpec(memory_space=pltpu.VMEM)
    array = lambda count: jax.ShapeDtypeStruct((count, width), BF)
    block = lambda *lead: pltpu.VMEM((*lead, ROWS, width), BF)
    scratch = [pltpu.VMEM((ROWS, plan.cells), BF), pltpu.VMEM((plan.cells, ROWS), BF)]
    if helped:
        kernel = functools.partial(helped_kernel, plan, steps, deep, counts)
        out_shape = [array(total)] * 2 + [array(plan.half)] * 2
        out_specs = [rows, rows, vmem, vmem]
        scratch += [block()] * 5
        source_specs, begin = [], 0
        for count in counts:
            at = lambda i, sc, begin=begin, count=count: (jnp.clip(i - begin, 0, count - 1), 0)
            half_rows = pl.BlockSpec((ROWS // 2, width), at)
            source_specs += [half_rows, half_rows, pl.BlockSpec((ROWS, width), at)]
            begin += count
        operands = [h, g, ids, places, cell_shape, weights, *sources, *into]
        in_specs = [rows, rows, *block_specs(here), vmem, vmem, *source_specs, hbm, hbm]
        units = 8
    else:
        kernel = functools.partial(self_kernel, plan, steps, deep, len(into))
        out_shape = ([array(total)] * 2 + [array(steps * ROWS // 2)] * 2 + [array(steps * ROWS)]
                     + [array(plan.half)] * 2)
        out_specs = [rows, rows, *[vmem] * 5]
        scratch += [block(10), block(SECTIONS), block(SECTIONS), block(SECTIONS + 1)]
        operands = [h, g, ids, places, h, ids, places, cell_shape, weights, *into]
        in_specs = [rows, rows, *block_specs(here), other_rows, *block_specs(there), vmem, vmem, *[hbm] * len(into)]
        units = 21
    scratch += [pltpu.VMEM((width, width), F32), pltpu.VMEM((width, width), F32),
                pltpu.VMEM((plan.cells, width), F32), pltpu.VMEM((8, width), F32)]
    first_into = 1 + len(operands) - len(into)
    return pl.pallas_call(
        kernel,
        grid_spec=pltpu.PrefetchScalarGridSpec(
            num_scalar_prefetch=1, grid=(steps,), in_specs=in_specs, out_specs=out_specs, scratch_shapes=scratch,
        ),
        out_shape=out_shape,
        input_output_aliases={first_into + j: j for j in range(len(into))},
        compiler_params=pltpu.CompilerParams(vmem_limit_bytes=plan.grant(VMEM)),
        cost_estimate=pl.CostEstimate(
            flops=2 * steps * ROWS * width * width * units, bytes_accessed=steps * ROWS * width * 12,
            transcendentals=steps * ROWS * width * 8,
        ),
    )(place, *operands)


def normed(direction, gain_row):
    scale = gain_row / jnp.sqrt(jnp.sum(direction * direction, axis=0, keepdims=True) + 1e-06)
    return (direction * scale).astype(BF)


def pack_kernel(plan, latent, *refs):
    sources, (packed, skip, side, far), held, sems = refs[:8], refs[8:12], refs[12:20], refs[20]
    copies = [pltpu.make_async_copy(s, h, sems.at[j]) for j, (s, h) in enumerate(zip(sources, held))]
    for copy in copies:
        copy.start()
    for copy in copies:
        copy.wait()
    dir_first, gain_first, bias_first, dir_second, gain_second, bias_second, latents, cell_shape = held
    width = plan.width
    half = BF(0.5)
    first = normed(dir_first[...].astype(F32), gain_first[...].astype(F32))
    second = normed(dir_second[...].astype(F32), gain_second[...].astype(F32))
    packed[:width, :] = first[:width] * half
    packed[width : 2 * width, :] = second * half
    skip[...] = first[width : width + latent]
    shape = lax.broadcasted_iota(jnp.int32, (plan.cells, plan.shapes), 1)
    onehot = jnp.where(cell_shape[...] == shape, 1.0, 0.0).astype(BF)
    by_cell = mm(onehot, latents[...]).astype(BF)
    by_cell = mm(by_cell, skip[...])
    by_cell = 0.5 * jnp.where(cell_shape[...] >= 0, by_cell + bias_first[...].astype(F32), 0.0)
    cell = lax.broadcasted_iota(jnp.int32, by_cell.shape, 0)
    tail = 0.5 * first[width + latent :].astype(F32)
    for j in range(plan.coords):
        by_cell = jnp.where(cell == plan.special(j), tail[j : j + 1], by_cell)
    by_cell = jnp.where(cell == plan.special(plan.coords), 0.5 * bias_second[...].astype(F32), by_cell)
    packed[2 * width :, :] = by_cell.astype(BF)
    place = lax.axis_index("dp")
    begin = lax.rem(place, 2) * plan.half
    side[...] = packed[pl.ds(pl.multiple_of(begin, 16), plan.half), :]
    far[...] = packed[pl.ds(pl.multiple_of(begin + lax.div(place, 2) * plan.piece, 16), plan.piece), :]


def pack_weights(plan, latents, cell_shape, *own):
    width = plan.width
    latent = latents.shape[1]
    vmem = pl.BlockSpec(memory_space=pltpu.VMEM)
    return pl.pallas_call(
        functools.partial(pack_kernel, plan, latent),
        in_specs=[pl.BlockSpec(memory_space=pl.ANY)] * 8,
        out_specs=[vmem] * 4,
        scratch_shapes=[pltpu.VMEM(array.shape, array.dtype) for array in (*own, latents, cell_shape)]
        + [pltpu.SemaphoreType.DMA((8,))],
        out_shape=[jax.ShapeDtypeStruct((rows, width), BF) for rows in (plan.packed, latent, plan.half, plan.piece)],
        compiler_params=pltpu.CompilerParams(vmem_limit_bytes=ALL_VMEM),
        cost_estimate=pl.CostEstimate(flops=2 * plan.cells * width * latent, bytes_accessed=4 * plan.packed * width,
                                      transcendentals=0),
    )(*own, latents, cell_shape)


def join_kernel(count, *refs):
    sources, out, sems = refs[:count], refs[count], refs[count + 1]
    copies, row = [], 0
    for j, source in enumerate(sources):
        copies.append(pltpu.make_async_copy(source, out.at[pl.ds(row, source.shape[0])], sems.at[j]))
        row += source.shape[0]
    for copy in copies:
        copy.start()
    for copy in copies:
        copy.wait()


def join(plan, arrays):
    rows = sum(array.shape[0] for array in arrays)
    return pl.pallas_call(
        functools.partial(join_kernel, len(arrays)),
        in_specs=[pl.BlockSpec(memory_space=pl.ANY)] * len(arrays),
        out_specs=pl.BlockSpec(memory_space=pltpu.VMEM),
        scratch_shapes=[pltpu.SemaphoreType.DMA((len(arrays),))],
        out_shape=jax.ShapeDtypeStruct((rows, arrays[0].shape[1]), arrays[0].dtype),
        compiler_params=pltpu.CompilerParams(vmem_limit_bytes=plan.grant(SMALL_VMEM)),
        cost_estimate=pl.CostEstimate(flops=0, bytes_accessed=4 * rows * arrays[0].shape[1], transcendentals=0),
    )(*arrays)


def spread_kernel(plan, near, sc, *refs):
    section, core, spot = sc[0], sc[1], sc[2]
    half, piece = plan.half, plan.piece
    first, block, weights, sems = refs
    side = core if near else 1 - core
    copies = [(first, weights.at[section])] if near else []
    for j in range(2):
        there = weights.at[jnp.bitwise_xor(section, j + 1)]
        copies.append((block.at[pl.ds(j * half, half)], there.at[pl.ds(side * half, half)]))
    there = weights.at[jnp.bitwise_xor(section, 3)]
    for j in range(plan.spots):
        z = jnp.bitwise_xor(spot, j)
        copies.append((block.at[pl.ds(2 * half + j * piece, piece)], there.at[pl.ds(side * half + z * piece, piece)]))
    copies = [pltpu.make_async_copy(source, target, sems.at[j]) for j, (source, target) in enumerate(copies)]
    for copy in copies:
        copy.start()
    for copy in copies:
        copy.wait()


def spread_weights(plan, near, scalars, first, block):
    hbm = pl.BlockSpec(memory_space=pl.ANY)
    vmem = pl.BlockSpec(memory_space=pltpu.VMEM)
    return pl.pallas_call(
        functools.partial(spread_kernel, plan, near),
        grid_spec=pltpu.PrefetchScalarGridSpec(
            num_scalar_prefetch=1, grid=(1,), in_specs=[hbm if near else vmem, hbm], out_specs=vmem,
            scratch_shapes=[pltpu.SemaphoreType.DMA((3 + plan.spots,))],
        ),
        out_shape=jax.ShapeDtypeStruct((SECTIONS, plan.packed, plan.width), BF),
        input_output_aliases={} if near else {1: 0},
        compiler_params=pltpu.CompilerParams(vmem_limit_bytes=plan.grant(SMALL_VMEM)),
        cost_estimate=pl.CostEstimate(flops=0, bytes_accessed=8 * plan.packed * plan.width, transcendentals=0),
    )(scalars, first, block)


def grads_kernel(plan, latent, sc, mine, other, dir_first, gain_first, dir_second, gain_second, latents, cell_shape,
                 first_rows, first_gain, first_bias, second_out, second_gain, second_bias, cells, first_out):
    core, spot = sc[1], sc[2]
    width, share, room, piece = plan.width, plan.share, plan.room, plan.piece
    for source, side in ((mine, core), (other, 1 - core)):
        for j in range(plan.spots):
            p = side * plan.spots + jnp.bitwise_xor(spot, j)
            base = j * piece
            rows = pl.ds(pl.multiple_of(p * share, share), share)
            second_out[rows, :] = source[base : base + share, :].astype(F32)
            first_out[rows, :] = source[base + share : base + 2 * share, :].astype(F32)
            rows = pl.ds(pl.multiple_of(p * room, room), room)
            cells[rows, :] = source[base + 2 * share : base + piece, :].astype(F32)
    by_cell = cells[...]
    shaped = jnp.where(cell_shape[...] >= 0, by_cell, 0.0)
    first_bias[...] = jnp.sum(shaped, axis=0, keepdims=True)
    shape = lax.broadcasted_iota(jnp.int32, (plan.cells, plan.shapes), 1)
    onehot = jnp.where(cell_shape[...] == shape, 1.0, 0.0).astype(BF)
    by_shape = mm(onehot, latents[...]).astype(BF)
    first_out[width : width + latent, :] = mm(by_shape, shaped.astype(BF), TN)
    for j in range(plan.coords):
        spot_row = plan.special(j)
        first_out[width + latent + j : width + latent + j + 1, :] = cells[spot_row : spot_row + 1, :]
    spot_row = plan.special(plan.coords)
    second_bias[...] = cells[spot_row : spot_row + 1, :]
    for direction, gain, out, gain_out in ((dir_first, gain_first, first_out, first_gain),
                                           (dir_second, gain_second, second_out, second_gain)):
        values = direction[...].astype(F32)
        summed = out[...]
        norm = jnp.sqrt(jnp.sum(values * values, axis=0, keepdims=True) + 1e-06)
        along = jnp.sum(values * summed, axis=0, keepdims=True)
        gain_out[...] = along / norm
        scale = gain[...].astype(F32) / norm
        result = scale * summed - (scale * along / (norm * norm)) * values
        if out is first_out:
            for j in range(first_rows.shape[1]):
                first_rows[:, j, :] = result[:, j * 128 : (j + 1) * 128]
        else:
            out[...] = result


def finish_grads(plan, scalars, mine, other, dir_first, gain_first, dir_second, gain_second, latents, cell_shape):
    width = plan.width
    vmem = pl.BlockSpec(memory_space=pltpu.VMEM)
    row = jax.ShapeDtypeStruct((1, width), F32)
    whole = lambda like: jax.ShapeDtypeStruct(like.shape, F32)
    return pl.pallas_call(
        functools.partial(grads_kernel, plan, latents.shape[1]),
        grid_spec=pltpu.PrefetchScalarGridSpec(
            num_scalar_prefetch=1, grid=(1,), in_specs=[vmem] * 8, out_specs=[vmem] * 6,
            scratch_shapes=[pltpu.VMEM((plan.cells, width), F32), pltpu.VMEM(dir_first.shape, F32)],
        ),
        out_shape=[jax.ShapeDtypeStruct((dir_first.shape[0], width // 128, 128), F32), row, row, whole(dir_second), row, row],
        compiler_params=pltpu.CompilerParams(vmem_limit_bytes=plan.grant(SMALL_VMEM)),
        cost_estimate=pl.CostEstimate(flops=2 * plan.cells * width * latents.shape[1],
                                      bytes_accessed=8 * plan.packed * width, transcendentals=0),
    )(scalars, mine, other, dir_first, gain_first, dir_second, gain_second, latents, cell_shape)


def swap_section(block, distance):
    route = [(i, i ^ distance) for i in range(lax.axis_size("section"))]
    return lax.ppermute(block, "section", route)


def swap_dp(block, distance):
    route = [(i, i ^ distance) for i in range(lax.axis_size("dp"))]
    return lax.ppermute(block, "dp", route)


def cut(array, first, count):
    return lax.dynamic_slice_in_dim(array, first, count, 0)


def reduce_pieces(plan, chip, spot):
    piece = plan.piece
    total = cut(chip, spot * piece, piece).astype(F32)
    for distance in range(plan.spots - 1, 0, -1):
        away = jnp.bitwise_xor(spot, distance)
        total = total + swap_dp(cut(chip, away * piece, piece), 2 * distance).astype(F32)
    return total.astype(BF)


def gather_chips(plan, piece):
    got = [swap_dp(piece, 2 * distance) for distance in range(plan.spots - 1, 0, -1)]
    return [piece] + got[::-1]


def shards(
    inputs, cotangent, latent_codes, positions, shape_ids,
    direction_first, gain_first, bias_first, direction_second, gain_second, bias_second,
):
    section = lax.axis_index("section")
    dp_rank = lax.axis_index("dp")
    core, spot = dp_rank % 2, dp_rank // 2
    total, width = inputs.shape
    shapes, latent = latent_codes.shape
    coords = positions.shape[0]
    plan = Plan(width, coords, shapes, lax.axis_size("dp"))
    cell_shape = jnp.asarray(plan.cell_shape)
    place = jnp.stack([section, core, spot]).astype(jnp.int32)

    packed, skip, sending, far = pack_weights(
        plan, latent_codes, cell_shape,
        direction_first[0], gain_first, bias_first, direction_second[0], gain_second, bias_second,
    )
    blocks = total // ROWS
    ids = shape_ids.reshape(blocks, 1, ROWS)
    places = positions.reshape(coords, blocks, ROWS).transpose(1, 0, 2)
    far = swap_section(far, 3)
    sending, far, ids, places, place = lax.optimization_barrier((sending, far, ids, places, place))
    x_mine = swap_section(sending, 1)
    y_mine = swap_section(sending, 2)
    far_mine = gather_chips(plan, far)
    mine = join(plan, [x_mine, y_mine, *far_mine])
    other = swap_dp(mine, 1)
    weights = spread_weights(plan, True, place, packed, mine)
    weights = spread_weights(plan, False, place, weights, other)

    same = (inputs, cotangent, ids, places, cell_shape, weights)
    given, parts, into, starts = [], [], [], []
    done = 0
    for turn, steps in enumerate(CALLS):
        *into, give_x, give_y, after_first, mine, theirs = run_blocks(
            plan, turn > 0, done, place, *same, into, (steps,), []
        )
        given.append((swap_section(give_x, 1), swap_section(give_y, 2), after_first))
        parts.append((mine, theirs))
        starts.append(done)
        done += steps
    for calls in HELPED_CALLS:
        sources = [source for call in calls for source in given[call]]
        counts = tuple(CALLS[call] for call in calls)
        *into, mine, theirs = run_blocks(plan, calls[0] > 0, starts[calls[0]], place, *same, into, counts, sources)
        parts.append((mine, theirs))
    act, ig = into

    mine, theirs = (sum(part.astype(F32) for part in side) for side in zip(*parts))
    chip = (mine + swap_dp(theirs.astype(BF), 1).astype(F32)).astype(BF)
    piece = reduce_pieces(plan, chip, spot)
    pieces = gather_chips(plan, piece)
    ready, pieces[1] = lax.optimization_barrier((piece, pieces[1]))
    owned = mm(ready[2 * plan.share : 2 * plan.share + plan.owned], skip, NT)
    code = cut(owned, section * plan.per, plan.per)
    for distance in range(1, SECTIONS):
        away = jnp.bitwise_xor(section, distance)
        code = code + swap_section(cut(owned, away * plan.per, plan.per), distance)
    mine = join(plan, pieces)
    mine, code = lax.optimization_barrier((mine, code))
    other = swap_dp(mine, 1)
    first, first_gain, first_bias, second, second_gain, second_bias = finish_grads(
        plan, place, mine, other, direction_first[0], gain_first, direction_second[0], gain_second,
        latent_codes, cell_shape,
    )
    return (
        act[None], ig[None], code, first.reshape(direction_first.shape), first_gain, first_bias, second[None], second_gain, second_bias,
    )


def solution(mesh):
    in_specs = (
        P("dp", None), P("dp", None), P(), P(None, "dp"), P("dp"),
        P("section", None, None), P("section", None), P("section", None),
        P("section", None, None), P("section", None), P("section", None),
    )
    out_specs = (
        P("section", "dp", None), P("section", "dp", None), P(("section", "dp"), None),
        P("section", None, None), P("section", None), P("section", None),
        P("section", None, None), P("section", None), P("section", None),
    )
    return jax.shard_map(shards, mesh=mesh, in_specs=in_specs, out_specs=out_specs, check_vma=False)
```

```python
import functools

import jax
import jax.numpy as jnp
import numpy as np
from jax import lax
from jax.experimental import pallas as pl
from jax.experimental.pallas import tpu as pltpu
from jax.sharding import PartitionSpec as P

BF = jnp.bfloat16
F32 = jnp.float32
NT = (((1,), (1,)), ((), ()))
TN = (((0,), (0,)), ((), ()))
SECTIONS = 4
ROWS = 768
CALLS = (3, 2)
HELPED_CALLS = ((0,), (1,))
VMEM = 36 * 2**20
SMALL_VMEM = 12 * 2**20
ALL_VMEM = 63 * 2**20
GIVE_X = (7, 6, 3, 8)
GIVE_Y = (8, 3, 6, 7)


def up(value, step):
    return -(-value // step) * step


def mm(left, right, dims=(((1,), (0,)), ((), ()))):
    return lax.dot_general(left, right, dims, preferred_element_type=F32)


def silu_parts(half):
    lift = 1.0 + jnp.tanh(half)
    out = (half * lift).astype(BF)
    lift = lift.astype(BF)
    return out, lift + out * (BF(2.0) - lift)


def stream(count, *stages):
    values = [None] * count
    for tick in range(count + len(stages) - 1):
        for j, stage in enumerate(stages):
            i = tick - j
            if 0 <= i < count:
                values[i] = stage(i, values[i])


class Plan:
    def __init__(self, width, coords, shapes, devices):
        self.width, self.coords, self.shapes, self.devices = width, coords, shapes, devices
        self.spots = devices // 2
        self.share = width // devices
        self.owned = shapes // devices
        self.per = self.owned // SECTIONS
        self.room = up(self.owned + 1, 16)
        self.cells = self.room * devices
        self.piece = 2 * self.share + self.room
        self.half = self.piece * self.spots
        self.packed = 2 * self.half
        table = np.full((self.cells, 1), -1, np.int32)
        for p in range(devices):
            place = 2 * (p % self.spots) + p // self.spots
            for j in range(self.owned):
                table[p * self.room + j, 0] = ((j // self.per) * devices + place) * self.per + j % self.per
        self.cell_shape = table

    def grant(self, base):
        return base + max(0, self.cells - 128) * 12288

    def special(self, j):
        return j * self.room + self.owned


class Block:
    def __init__(self, plan, weights, ext, subs):
        self.width, self.plan, self.weights, self.ext, self.subs = plan.width, plan, weights, ext, subs

    def first(self, k):
        return self.weights[k, : self.width, :]

    def second(self, k):
        return self.weights[k, self.width : 2 * self.width, :]

    def inner(self, k, source):
        beside = self.weights[k, 2 * self.width :, :]
        return lambda i, unused: mm(source(i), self.first(k)) + mm(self.ext[self.subs[i], :], beside)

    def outer(self, k):
        begin = 2 * self.width + self.plan.coords * self.plan.room
        spot = self.plan.owned
        offset = self.weights[k, begin : begin + self.plan.room, :].astype(F32)[spot : spot + 1]
        return lambda i, active: mm(active, self.second(k)) + offset

    def back_second(self, k, grads):
        return lambda i, unused: mm(grads(i), self.second(k), NT)

    def back_first(self, k):
        return lambda i, grads: mm(grads, self.first(k), NT)


def place_cells(point, places, cell_shape, plan, ext, ext_turned):
    rows = ext.shape[0]
    hit = jnp.where(cell_shape[...] == jnp.broadcast_to(point[...], (plan.cells, rows)), 1.0, 0.0)
    cell = lax.broadcasted_iota(jnp.int32, (plan.cells, rows), 0)
    for j in range(plan.coords):
        hit = jnp.where(cell == plan.special(j), places[j : j + 1, :].astype(F32), hit)
    ext_turned[...] = hit.astype(BF)
    ext[...] = hit.T.astype(BF)


def add_weight_grads(accs, active, outer_grad, entering, inner_grad, ext_turned):
    first, second, cell, bias = accs
    second[...] += mm(active, outer_grad, TN)
    first[...] += mm(entering, inner_grad, TN)
    cell[...] += mm(ext_turned[...], inner_grad)
    bias[...] += jnp.sum(outer_grad.astype(F32).reshape(-1, 8, outer_grad.shape[1]), axis=0)


def store_weight_grads(accs, plan, core, mine, theirs):
    first, second, cell, bias = accs
    share, room = plan.share, plan.room
    last = jnp.sum(bias[...], axis=0, keepdims=True)
    row = lax.broadcasted_iota(jnp.int32, cell.shape, 0)
    cell[...] = jnp.where(row == plan.special(plan.coords), last, cell[...])
    for side in range(2):
        @pl.when(core == side)
        def _(side=side):
            for p in range(plan.devices):
                out = mine if p // plan.spots == side else theirs
                at = (p % plan.spots) * plan.piece
                out[at : at + share, :] = second[p * share : (p + 1) * share, :].astype(BF)
                out[at + share : at + 2 * share, :] = first[p * share : (p + 1) * share, :].astype(BF)
                out[at + 2 * share : at + plan.piece, :] = cell[p * room : (p + 1) * room, :].astype(BF)


def pick(section, choices):
    found = jnp.int32(choices[0])
    for k in range(1, SECTIONS):
        found = jnp.where(section == k, choices[k], found)
    return found


def self_half(section, blocks):
    return jnp.where((section == 0) | (section == SECTIONS - 1), 0, blocks // 2)


def self_kernel(
    plan, steps, deep, aliased, sc, h_in, g_in, ids, places, other_h, other_ids, other_places, cell_shape, weights, *refs
):
    act, ig, give_x, give_y, after_first, mine, theirs, ext, ext_turned, states, mids, slope1, slope2, *accs = refs[aliased:]
    section, core = sc[0], sc[1]
    step = pl.program_id(0)
    rows = h_in.shape[0]
    half = rows // 2
    subs = [pl.ds(0, half), pl.ds(half, half)]
    do = Block(plan, weights, ext, subs)

    @pl.when(step == 0)
    def _():
        for acc in accs:
            acc[...] = jnp.zeros_like(acc)

    other = lambda i: pl.ds(pl.multiple_of(step * rows + i * half, 128), half)

    def ahead(k, source):
        def keep(i, z):
            after_first[other(i), :] = silu_parts(z)[0]
        stream(2, do.inner(k, source), lambda i, z: silu_parts(z)[0], do.outer(k), keep)

    @pl.when((section == 2) | (section == 1) if deep else section == 2)
    def _():
        place_cells(other_ids, other_places, cell_shape, plan, ext, ext_turned)
        ahead(0, lambda i: other_h[subs[i], :])

    if deep:
        @pl.when(section == 2)
        def _():
            ahead(1, lambda i: after_first[other(i), :])

    place_cells(ids, places, cell_shape, plan, ext, ext_turned)
    states[0] = h_in[...]

    def keep_active(k):
        def stage(i, z):
            active, slope = silu_parts(z)
            mids[k, subs[i], :] = active
            slope1[k, subs[i], :] = slope
            return active
        return stage

    def keep_state(k):
        def stage(i, z):
            after, slope = silu_parts(z)
            states[k + 1, subs[i], :] = after
            if k == SECTIONS - 1:
                slope = slope * (g_in[subs[i], :] * BF(0.5))
            slope2[k, subs[i], :] = slope
        return stage

    def inner_grad(k):
        def stage(i, grads):
            grads = (grads * slope1[k, subs[i], :].astype(F32)).astype(BF)
            slope1[k, subs[i], :] = grads
            return grads
        return stage

    def enter_grad(k, below):
        def stage(i, grads):
            grads = grads.astype(BF)
            states[5 + k, subs[i], :] = grads
            if below is not None:
                slope2[below, subs[i], :] = grads * slope2[below, subs[i], :]
        return stage

    def back(k, below):
        return [do.back_second(k, lambda i: slope2[k, subs[i], :]), inner_grad(k), do.back_first(k),
                enter_grad(k, below)]

    top = SECTIONS - 1
    stages = []
    for k in range(SECTIONS):
        source = (lambda i: h_in[subs[i], :]) if k == 0 else (lambda i, k=k: states[k, subs[i], :])
        stages += [do.inner(k, source), keep_active(k), do.outer(k), keep_state(k)]
    stream(2, *stages, *back(top, top - 1))

    def lower(j, unused):
        k = top - 1 - j
        stream(2, *back(k, jnp.where(k > 0, k - 1, SECTIONS)))
        return 0

    lax.fori_loop(0, top - section, lower, 0)

    @pl.when(section >= 2)
    def _():
        value = None
        for stage in back(section - 1, None):
            value = stage(1, value)

    act[...] = states[section + 1]
    ig[...] = states[5 + section] * BF(2.0)
    given = pl.ds(pl.multiple_of(step * half, 128), half)
    give_x[given, :] = states[pick(section, GIVE_X), subs[0], :]
    give_y[given, :] = states[pick(section, GIVE_Y), subs[1], :]
    add_weight_grads(accs, mids[section], slope2[section], states[section], slope1[section], ext_turned)

    @pl.when(step == steps - 1)
    def _():
        store_weight_grads(accs, plan, core, mine, theirs)


def helped_kernel(
    plan, steps, deep, counts, sc, h_in, g_in, ids, places, cell_shape, weights, *refs
):
    sources, refs = refs[: 3 * len(counts)], refs[3 * len(counts) + 2 :]
    act, ig, mine, theirs, ext, ext_turned, entering, got, mid, slope1, slope2, *accs = refs
    section, core = sc[0], sc[1]
    step = pl.program_id(0)
    rows = h_in.shape[0]
    half = rows // 2
    subs = [pl.ds(0, half), pl.ds(half, half)]
    do = Block(plan, weights, ext, subs)

    @pl.when(step == 0)
    def _():
        for acc in accs:
            acc[...] = jnp.zeros_like(acc)

    place_cells(ids, places, cell_shape, plan, ext, ext_turned)
    top = section == SECTIONS - 1
    begin = 0
    for j, count in enumerate(counts):
        got_x, got_y, after_first = sources[3 * j : 3 * j + 3]
        now = (step >= begin) & (step < begin + count)
        begin += count

        @pl.when(now)
        def _():
            got[subs[0], :] = got_x[...]
            got[subs[1], :] = got_y[...]

        @pl.when(now & ((section == 2) | (section == 1) if deep else section == 2))
        def _():
            entering[...] = after_first[...]

    @pl.when((section == 0) if deep else (section <= 1))
    def _():
        entering[...] = h_in[...]

    @pl.when(top)
    def _():
        entering[...] = got[...]
        got[...] = g_in[...] * BF(0.5)

    def active_only(i, z):
        return silu_parts(z)[0]

    def enter(i, z):
        entering[subs[i], :] = silu_parts(z)[0]

    def keep_active(i, z):
        active, slope = silu_parts(z)
        mid[subs[i], :] = active
        slope1[subs[i], :] = slope
        return active

    def keep_own(i, z):
        after, slope = silu_parts(z)
        act[subs[i], :] = after
        grads = slope * got[subs[i], :]
        slope2[subs[i], :] = grads
        return grads

    def inner_grad(i, grads):
        grads = (grads * slope1[subs[i], :].astype(F32)).astype(BF)
        slope1[subs[i], :] = grads
        return grads

    def enter_grad(i, grads):
        ig[subs[i], :] = (2.0 * grads).astype(BF)

    def source(i):
        return entering[subs[i], :]

    if not deep:
        @pl.when((section == 1) | (section == 2))
        def _():
            stream(2, do.inner(section - 1, source), active_only, do.outer(section - 1), enter)

    stream(2, do.inner(section, source), keep_active, do.outer(section), keep_own,
           do.back_second(section, lambda i: slope2[subs[i], :]), inner_grad, do.back_first(section), enter_grad)
    add_weight_grads(accs, mid[...], slope2[...], entering[...], slope1[...], ext_turned)

    @pl.when(step == steps - 1)
    def _():
        store_weight_grads(accs, plan, core, mine, theirs)


def run_blocks(plan, deep, done, place, h, g, ids, places, cell_shape, weights, into, counts, sources):
    total, width = h.shape
    blocks = total // ROWS
    helped = len(sources) > 0
    steps = sum(counts)

    def here(i, sc):
        start = self_half(sc[0], blocks)
        return (blocks // 2 - start if helped else start) + done + i

    def there(i, sc):
        used = (sc[0] == 2) | (sc[0] == 1) if deep else sc[0] == 2
        return jnp.where(used, blocks // 2 - self_half(sc[0], blocks) + done + i, 0)

    def block_specs(where):
        return [
            pl.BlockSpec((None, 1, ROWS), lambda i, sc: (where(i, sc), 0, 0)),
            pl.BlockSpec((None, plan.coords, ROWS), lambda i, sc: (where(i, sc), 0, 0)),
        ]

    rows = pl.BlockSpec((ROWS, width), lambda i, sc: (here(i, sc), 0))
    other_rows = pl.BlockSpec((ROWS, width), lambda i, sc: (there(i, sc), 0))
    hbm = pl.BlockSpec(memory_space=pl.ANY)
    vmem = pl.BlockSpec(memory_space=pltpu.VMEM)
    array = lambda count: jax.ShapeDtypeStruct((count, width), BF)
    block = lambda *lead: pltpu.VMEM((*lead, ROWS, width), BF)
    scratch = [pltpu.VMEM((ROWS, plan.cells), BF), pltpu.VMEM((plan.cells, ROWS), BF)]
    if helped:
        kernel = functools.partial(helped_kernel, plan, steps, deep, counts)
        out_shape = [array(total)] * 2 + [array(plan.half)] * 2
        out_specs = [rows, rows, vmem, vmem]
        scratch += [block()] * 5
        source_specs, begin = [], 0
        for count in counts:
            at = lambda i, sc, begin=begin, count=count: (jnp.clip(i - begin, 0, count - 1), 0)
            half_rows = pl.BlockSpec((ROWS // 2, width), at)
            source_specs += [half_rows, half_rows, pl.BlockSpec((ROWS, width), at)]
            begin += count
        operands = [h, g, ids, places, cell_shape, weights, *sources, *into]
        in_specs = [rows, rows, *block_specs(here), vmem, vmem, *source_specs, hbm, hbm]
        units = 8
    else:
        kernel = functools.partial(self_kernel, plan, steps, deep, len(into))
        out_shape = ([array(total)] * 2 + [array(steps * ROWS // 2)] * 2 + [array(steps * ROWS)]
                     + [array(plan.half)] * 2)
        out_specs = [rows, rows, *[vmem] * 5]
        scratch += [block(10), block(SECTIONS), block(SECTIONS), block(SECTIONS + 1)]
        operands = [h, g, ids, places, h, ids, places, cell_shape, weights, *into]
        in_specs = [rows, rows, *block_specs(here), other_rows, *block_specs(there), vmem, vmem, *[hbm] * len(into)]
        units = 21
    scratch += [pltpu.VMEM((width, width), F32), pltpu.VMEM((width, width), F32),
                pltpu.VMEM((plan.cells, width), F32), pltpu.VMEM((8, width), F32)]
    first_into = 1 + len(operands) - len(into)
    return pl.pallas_call(
        kernel,
        grid_spec=pltpu.PrefetchScalarGridSpec(
            num_scalar_prefetch=1, grid=(steps,), in_specs=in_specs, out_specs=out_specs, scratch_shapes=scratch,
        ),
        out_shape=out_shape,
        input_output_aliases={first_into + j: j for j in range(len(into))},
        compiler_params=pltpu.CompilerParams(vmem_limit_bytes=plan.grant(VMEM)),
        cost_estimate=pl.CostEstimate(
            flops=2 * steps * ROWS * width * width * units, bytes_accessed=steps * ROWS * width * 12,
            transcendentals=steps * ROWS * width * 8,
        ),
    )(place, *operands)


def normed(direction, gain_row):
    scale = gain_row / jnp.sqrt(jnp.sum(direction * direction, axis=0, keepdims=True) + 1e-06)
    return (direction * scale).astype(BF)


def pack_kernel(plan, latent, *refs):
    sources, (packed, skip, side, far), held, sems = refs[:8], refs[8:12], refs[12:20], refs[20]
    copies = [pltpu.make_async_copy(s, h, sems.at[j]) for j, (s, h) in enumerate(zip(sources, held))]
    for copy in copies:
        copy.start()
    for copy in copies:
        copy.wait()
    dir_first, gain_first, bias_first, dir_second, gain_second, bias_second, latents, cell_shape = held
    width = plan.width
    half = BF(0.5)
    first = normed(dir_first[...].astype(F32), gain_first[...].astype(F32))
    second = normed(dir_second[...].astype(F32), gain_second[...].astype(F32))
    packed[:width, :] = first[:width] * half
    packed[width : 2 * width, :] = second * half
    skip[...] = first[width : width + latent]
    shape = lax.broadcasted_iota(jnp.int32, (plan.cells, plan.shapes), 1)
    onehot = jnp.where(cell_shape[...] == shape, 1.0, 0.0).astype(BF)
    by_cell = mm(onehot, latents[...]).astype(BF)
    by_cell = mm(by_cell, skip[...])
    by_cell = 0.5 * jnp.where(cell_shape[...] >= 0, by_cell + bias_first[...].astype(F32), 0.0)
    cell = lax.broadcasted_iota(jnp.int32, by_cell.shape, 0)
    tail = 0.5 * first[width + latent :].astype(F32)
    for j in range(plan.coords):
        by_cell = jnp.where(cell == plan.special(j), tail[j : j + 1], by_cell)
    by_cell = jnp.where(cell == plan.special(plan.coords), 0.5 * bias_second[...].astype(F32), by_cell)
    packed[2 * width :, :] = by_cell.astype(BF)
    place = lax.axis_index("dp")
    begin = lax.rem(place, 2) * plan.half
    side[...] = packed[pl.ds(pl.multiple_of(begin, 16), plan.half), :]
    far[...] = packed[pl.ds(pl.multiple_of(begin + lax.div(place, 2) * plan.piece, 16), plan.piece), :]


def pack_weights(plan, latents, cell_shape, *own):
    width = plan.width
    latent = latents.shape[1]
    vmem = pl.BlockSpec(memory_space=pltpu.VMEM)
    return pl.pallas_call(
        functools.partial(pack_kernel, plan, latent),
        in_specs=[pl.BlockSpec(memory_space=pl.ANY)] * 8,
        out_specs=[vmem] * 4,
        scratch_shapes=[pltpu.VMEM(array.shape, array.dtype) for array in (*own, latents, cell_shape)]
        + [pltpu.SemaphoreType.DMA((8,))],
        out_shape=[jax.ShapeDtypeStruct((rows, width), BF) for rows in (plan.packed, latent, plan.half, plan.piece)],
        compiler_params=pltpu.CompilerParams(vmem_limit_bytes=ALL_VMEM),
        cost_estimate=pl.CostEstimate(flops=2 * plan.cells * width * latent, bytes_accessed=4 * plan.packed * width,
                                      transcendentals=0),
    )(*own, latents, cell_shape)


def join_kernel(count, *refs):
    sources, out, sems = refs[:count], refs[count], refs[count + 1]
    copies, row = [], 0
    for j, source in enumerate(sources):
        copies.append(pltpu.make_async_copy(source, out.at[pl.ds(row, source.shape[0])], sems.at[j]))
        row += source.shape[0]
    for copy in copies:
        copy.start()
    for copy in copies:
        copy.wait()


def join(plan, arrays):
    rows = sum(array.shape[0] for array in arrays)
    return pl.pallas_call(
        functools.partial(join_kernel, len(arrays)),
        in_specs=[pl.BlockSpec(memory_space=pl.ANY)] * len(arrays),
        out_specs=pl.BlockSpec(memory_space=pltpu.VMEM),
        scratch_shapes=[pltpu.SemaphoreType.DMA((len(arrays),))],
        out_shape=jax.ShapeDtypeStruct((rows, arrays[0].shape[1]), arrays[0].dtype),
        compiler_params=pltpu.CompilerParams(vmem_limit_bytes=plan.grant(SMALL_VMEM)),
        cost_estimate=pl.CostEstimate(flops=0, bytes_accessed=4 * rows * arrays[0].shape[1], transcendentals=0),
    )(*arrays)


def spread_kernel(plan, near, sc, *refs):
    section, core, spot = sc[0], sc[1], sc[2]
    half, piece = plan.half, plan.piece
    first, block, weights, sems = refs
    side = core if near else 1 - core
    copies = [(first, weights.at[section])] if near else []
    for j in range(2):
        there = weights.at[jnp.bitwise_xor(section, j + 1)]
        copies.append((block.at[pl.ds(j * half, half)], there.at[pl.ds(side * half, half)]))
    there = weights.at[jnp.bitwise_xor(section, 3)]
    for j in range(plan.spots):
        z = jnp.bitwise_xor(spot, j)
        copies.append((block.at[pl.ds(2 * half + j * piece, piece)], there.at[pl.ds(side * half + z * piece, piece)]))
    copies = [pltpu.make_async_copy(source, target, sems.at[j]) for j, (source, target) in enumerate(copies)]
    for copy in copies:
        copy.start()
    for copy in copies:
        copy.wait()


def spread_weights(plan, near, scalars, first, block):
    hbm = pl.BlockSpec(memory_space=pl.ANY)
    vmem = pl.BlockSpec(memory_space=pltpu.VMEM)
    return pl.pallas_call(
        functools.partial(spread_kernel, plan, near),
        grid_spec=pltpu.PrefetchScalarGridSpec(
            num_scalar_prefetch=1, grid=(1,), in_specs=[hbm if near else vmem, hbm], out_specs=vmem,
            scratch_shapes=[pltpu.SemaphoreType.DMA((3 + plan.spots,))],
        ),
        out_shape=jax.ShapeDtypeStruct((SECTIONS, plan.packed, plan.width), BF),
        input_output_aliases={} if near else {1: 0},
        compiler_params=pltpu.CompilerParams(vmem_limit_bytes=plan.grant(SMALL_VMEM)),
        cost_estimate=pl.CostEstimate(flops=0, bytes_accessed=8 * plan.packed * plan.width, transcendentals=0),
    )(scalars, first, block)


def grads_kernel(plan, latent, sc, mine, other, dir_first, gain_first, dir_second, gain_second, latents, cell_shape,
                 first_rows, first_gain, first_bias, second_out, second_gain, second_bias, cells, first_out):
    core, spot = sc[1], sc[2]
    width, share, room, piece = plan.width, plan.share, plan.room, plan.piece
    for source, side in ((mine, core), (other, 1 - core)):
        for j in range(plan.spots):
            p = side * plan.spots + jnp.bitwise_xor(spot, j)
            base = j * piece
            rows = pl.ds(pl.multiple_of(p * share, share), share)
            second_out[rows, :] = source[base : base + share, :].astype(F32)
            first_out[rows, :] = source[base + share : base + 2 * share, :].astype(F32)
            rows = pl.ds(pl.multiple_of(p * room, room), room)
            cells[rows, :] = source[base + 2 * share : base + piece, :].astype(F32)
    by_cell = cells[...]
    shaped = jnp.where(cell_shape[...] >= 0, by_cell, 0.0)
    first_bias[...] = jnp.sum(shaped, axis=0, keepdims=True)
    shape = lax.broadcasted_iota(jnp.int32, (plan.cells, plan.shapes), 1)
    onehot = jnp.where(cell_shape[...] == shape, 1.0, 0.0).astype(BF)
    by_shape = mm(onehot, latents[...]).astype(BF)
    first_out[width : width + latent, :] = mm(by_shape, shaped.astype(BF), TN)
    for j in range(plan.coords):
        spot_row = plan.special(j)
        first_out[width + latent + j : width + latent + j + 1, :] = cells[spot_row : spot_row + 1, :]
    spot_row = plan.special(plan.coords)
    second_bias[...] = cells[spot_row : spot_row + 1, :]
    for direction, gain, out, gain_out in ((dir_first, gain_first, first_out, first_gain),
                                           (dir_second, gain_second, second_out, second_gain)):
        values = direction[...].astype(F32)
        summed = out[...]
        norm = jnp.sqrt(jnp.sum(values * values, axis=0, keepdims=True) + 1e-06)
        along = jnp.sum(values * summed, axis=0, keepdims=True)
        gain_out[...] = along / norm
        scale = gain[...].astype(F32) / norm
        result = scale * summed - (scale * along / (norm * norm)) * values
        if out is first_out:
            for j in range(first_rows.shape[1]):
                first_rows[:, j, :] = result[:, j * 128 : (j + 1) * 128]
        else:
            out[...] = result


def finish_grads(plan, scalars, mine, other, dir_first, gain_first, dir_second, gain_second, latents, cell_shape):
    width = plan.width
    vmem = pl.BlockSpec(memory_space=pltpu.VMEM)
    row = jax.ShapeDtypeStruct((1, width), F32)
    whole = lambda like: jax.ShapeDtypeStruct(like.shape, F32)
    return pl.pallas_call(
        functools.partial(grads_kernel, plan, latents.shape[1]),
        grid_spec=pltpu.PrefetchScalarGridSpec(
            num_scalar_prefetch=1, grid=(1,), in_specs=[vmem] * 8, out_specs=[vmem] * 6,
            scratch_shapes=[pltpu.VMEM((plan.cells, width), F32), pltpu.VMEM(dir_first.shape, F32)],
        ),
        out_shape=[jax.ShapeDtypeStruct((dir_first.shape[0], width // 128, 128), F32), row, row, whole(dir_second), row, row],
        compiler_params=pltpu.CompilerParams(vmem_limit_bytes=plan.grant(SMALL_VMEM)),
        cost_estimate=pl.CostEstimate(flops=2 * plan.cells * width * latents.shape[1],
                                      bytes_accessed=8 * plan.packed * width, transcendentals=0),
    )(scalars, mine, other, dir_first, gain_first, dir_second, gain_second, latents, cell_shape)


def swap_section(block, distance):
    route = [(i, i ^ distance) for i in range(lax.axis_size("section"))]
    return lax.ppermute(block, "section", route)


def swap_dp(block, distance):
    route = [(i, i ^ distance) for i in range(lax.axis_size("dp"))]
    return lax.ppermute(block, "dp", route)


def cut(array, first, count):
    return lax.dynamic_slice_in_dim(array, first, count, 0)


def reduce_pieces(plan, chip, spot):
    piece = plan.piece
    total = cut(chip, spot * piece, piece).astype(F32)
    for distance in range(plan.spots - 1, 0, -1):
        away = jnp.bitwise_xor(spot, distance)
        total = total + swap_dp(cut(chip, away * piece, piece), 2 * distance).astype(F32)
    return total.astype(BF)


def gather_chips(plan, piece):
    got = [swap_dp(piece, 2 * distance) for distance in range(plan.spots - 1, 0, -1)]
    return [piece] + got[::-1]


def shards(
    inputs, cotangent, latent_codes, positions, shape_ids,
    direction_first, gain_first, bias_first, direction_second, gain_second, bias_second,
):
    section = lax.axis_index("section")
    dp_rank = lax.axis_index("dp")
    core, spot = dp_rank % 2, dp_rank // 2
    total, width = inputs.shape
    shapes, latent = latent_codes.shape
    coords = positions.shape[0]
    plan = Plan(width, coords, shapes, lax.axis_size("dp"))
    cell_shape = jnp.asarray(plan.cell_shape)
    place = jnp.stack([section, core, spot]).astype(jnp.int32)

    packed, skip, sending, far = pack_weights(
        plan, latent_codes, cell_shape,
        direction_first[0], gain_first, bias_first, direction_second[0], gain_second, bias_second,
    )
    blocks = total // ROWS
    ids = shape_ids.reshape(blocks, 1, ROWS)
    places = positions.reshape(coords, blocks, ROWS).transpose(1, 0, 2)
    far = swap_section(far, 3)
    x_mine = swap_section(sending, 1)
    sending, far, ids, places, place = lax.optimization_barrier((sending, far, ids, places, place))
    y_mine = swap_section(sending, 2)
    far_mine = gather_chips(plan, far)
    mine = join(plan, [x_mine, y_mine, *far_mine])
    other = swap_dp(mine, 1)
    weights = spread_weights(plan, True, place, packed, mine)
    weights = spread_weights(plan, False, place, weights, other)

    same = (inputs, cotangent, ids, places, cell_shape, weights)
    given, parts, into, starts = [], [], [], []
    done = 0
    for turn, steps in enumerate(CALLS):
        *into, give_x, give_y, after_first, mine, theirs = run_blocks(
            plan, turn > 0, done, place, *same, into, (steps,), []
        )
        given.append((swap_section(give_x, 1), swap_section(give_y, 2), after_first))
        parts.append((mine, theirs))
        starts.append(done)
        done += steps
    for calls in HELPED_CALLS:
        sources = [source for call in calls for source in given[call]]
        counts = tuple(CALLS[call] for call in calls)
        *into, mine, theirs = run_blocks(plan, calls[0] > 0, starts[calls[0]], place, *same, into, counts, sources)
        parts.append((mine, theirs))
    act, ig = into

    mine, theirs = (sum(part.astype(F32) for part in side) for side in zip(*parts))
    chip = (mine + swap_dp(theirs.astype(BF), 1).astype(F32)).astype(BF)
    piece = reduce_pieces(plan, chip, spot)
    pieces = gather_chips(plan, piece)
    ready, pieces[1] = lax.optimization_barrier((piece, pieces[1]))
    owned = mm(ready[2 * plan.share : 2 * plan.share + plan.owned], skip, NT)
    code = cut(owned, section * plan.per, plan.per)
    for distance in range(1, SECTIONS):
        away = jnp.bitwise_xor(section, distance)
        code = code + swap_section(cut(owned, away * plan.per, plan.per), distance)
    mine = join(plan, pieces)
    mine, code = lax.optimization_barrier((mine, code))
    other = swap_dp(mine, 1)
    first, first_gain, first_bias, second, second_gain, second_bias = finish_grads(
        plan, place, mine, other, direction_first[0], gain_first, direction_second[0], gain_second,
        latent_codes, cell_shape,
    )
    return (
        act[None], ig[None], code, first.reshape(direction_first.shape), first_gain, first_bias, second[None], second_gain, second_bias,
    )


def solution(mesh):
    in_specs = (
        P("dp", None), P("dp", None), P(), P(None, "dp"), P("dp"),
        P("section", None, None), P("section", None), P("section", None),
        P("section", None, None), P("section", None), P("section", None),
    )
    out_specs = (
        P("section", "dp", None), P("section", "dp", None), P(("section", "dp"), None),
        P("section", None, None), P("section", None), P("section", None),
        P("section", None, None), P("section", None), P("section", None),
    )
    return jax.shard_map(shards, mesh=mesh, in_specs=in_specs, out_specs=out_specs, check_vma=False)
```
